32 devices in a mesh: replica: 16 (over z, x, core), shard: 2 (over y).
Axes of the slice: x: 2, y: 2, z: 4, core: 2. Of those that a mesh axis runs over, the one named last changes fastest.
Arguments:
- tokens: bfloat16 [256, 14, 14, 512], P(('replica', 'shard')), may hold values from -6 to 6
- cotangent: bfloat16 [256, 14, 14, 512], P(('replica', 'shard')), may hold values from -6 to 6
- counts: int32 [32], P(('replica', 'shard')), may hold values from 1 to 8, 153 in all
- w_qkv: float32 [512, 1536], P('shard'), may hold values from -0.25 to 0.25
- w_proj: float32 [512, 512], P('shard'), may hold values from -0.75 to 0.75
- w_fc1: float32 [512, 2048], P('shard'), may hold values from -0.25 to 0.25
- w_fc2: float32 [2048, 512], P('shard'), may hold values from -0.125 to 0.125
- vectors: float32 [8848], P('shard'), may hold values from -0.3 to 0.3
- first_qkv: float32 [512, 1536], P('shard'), may hold values from -103.90226 to 103.90226
- first_proj: float32 [512, 512], P('shard'), may hold values from -103.90226 to 103.90226
- first_fc1: float32 [512, 2048], P('shard'), may hold values from -103.90226 to 103.90226
- first_fc2: float32 [2048, 512], P('shard'), may hold values from -103.90226 to 103.90226
- first_vec: float32 [8848], P('shard'), may hold values from -103.90226 to 103.90226
- second_qkv: float32 [512, 1536], P('shard'), may hold values from 2.9988 to 29.988
- second_proj: float32 [512, 512], P('shard'), may hold values from 2.9988 to 29.988
- second_fc1: float32 [512, 2048], P('shard'), may hold values from 2.9988 to 29.988
- second_fc2: float32 [2048, 512], P('shard'), may hold values from 2.9988 to 29.988
- second_vec: float32 [8848], P('shard'), may hold values from 2.9988 to 29.988
Outputs:
- out: bfloat16 [256, 14, 14, 512], P(('replica', 'shard'))
- grad_input: bfloat16 [256, 14, 14, 512], P(('replica', 'shard'))
- grad_qkv: float32 [512, 1536], P('shard')
- grad_proj: float32 [512, 512], P('shard')
- grad_fc1: float32 [512, 2048], P('shard')
- grad_fc2: float32 [2048, 512], P('shard')
- grad_vec: float32 [8848], P('shard')
- new_qkv: float32 [512, 1536], P('shard')
- new_proj: float32 [512, 512], P('shard')
- new_fc1: float32 [512, 2048], P('shard')
- new_fc2: float32 [2048, 512], P('shard')
- new_vec: float32 [8848], P('shard')
- new_first_qkv: float32 [512, 1536], P('shard')
- new_first_proj: float32 [512, 512], P('shard')
- new_first_fc1: float32 [512, 2048], P('shard')
- new_first_fc2: float32 [2048, 512], P('shard')
- new_first_vec: float32 [8848], P('shard')
- new_second_qkv: float32 [512, 1536], P('shard')
- new_second_proj: float32 [512, 512], P('shard')
- new_second_fc1: float32 [512, 2048], P('shard')
- new_second_fc2: float32 [2048, 512], P('shard')
- new_second_vec: float32 [8848], P('shard')
The draws below stay inside these ranges and needn't reach their ends.
Inputs may be any that keep to these rules, and one draw needn't show every extreme that they name: Device g holds images in its first counts[g] slots, g * 8 .. g * 8 + counts[g] - 1; its other slots are empty. The counts sum to 153, and some device has exactly 8.
All inputs are finite; a program needn't handle non-finite values.
Results may differ from the reference program's by a relative error of at most 0.012.
The reference program's roundings to bfloat16 on the way count: a program that leaves them out, or rounds other values in their place, can miss the bound.
Values may be sent and summed in bfloat16 or wider, within the bound.
No kernel may reach another device: no remote copies, remote signals or barrier semaphores. Data moves between devices by JAX's collectives and lax.ppermute only.
A program may use at most 256 MiB of HBM per device.

```python
import math
import jax
import jax.numpy as jnp
import numpy as np
from jax import lax

D = 512
HEADS = 16
HEAD_DIM = 32
FF = 2048
WIN = 7
SIDE = 14
SHIFT = 3
STEP = 3
IMG_CAP = 8
IMAGES = 256
LIVE = 153
RELS = 169
SMALL = 8848
DEVICES = 32


def steps_of(own_key, extent, split, least, largest):
    factor_of = 1.0
    for axis_at, parts in split:
        draws = jax.random.uniform(jax.random.fold_in(jax.random.fold_in(own_key, 6), axis_at), (parts,), jnp.float32, least / len(split), largest / len(split))
        factor_of = factor_of * jnp.repeat(jnp.exp(draws), extent[axis_at] // parts).reshape((-1,) + (1,) * (len(extent) - 1 - axis_at))
    return factor_of


def split_up(amount, total, limit, lean):
    loads = [(1 << 20) // math.isqrt(rank ** lean) + 1 for rank in range(2, amount + 1)]
    rest, given = total - limit - (amount - 1), [1] * (amount - 1)
    while rest > 0:
        candidates = [i for i in range(amount - 1) if given[i] < limit]
        whole, remaining = sum([loads[i] for i in candidates]), rest
        for i in candidates:
            more = min(limit - given[i], max(1, remaining * loads[i] // whole), rest)
            given[i] = given[i] + more
            rest = rest - more
    return np.array([limit] + given)


def ragged_sizes(stream_key, count, total, bound, skew):
    if count == 2:
        one = jax.random.randint(stream_key, (), max(1, total - bound), min(bound, total - 1) + 1)
        return jnp.stack([one, total - one])
    lengths = jnp.asarray(split_up(count, total, bound, skew), jnp.int32)
    couples = (count - 1) // 2
    donor, sink = lengths[1:1 + 2 * couples:2], lengths[2:2 + 2 * couples:2]
    slack = jnp.minimum(donor - 1, bound - sink)
    shifted = jax.random.randint(jax.random.fold_in(stream_key, 1), (couples,), 0, 1 << 20) % (slack + 1)
    lengths = lengths.at[1:1 + 2 * couples:2].set(donor - shifted).at[2:2 + 2 * couples:2].set(sink + shifted)
    return lengths[jax.random.permutation(jax.random.fold_in(stream_key, 2), count)]


def gaussian(own_key, dims, spread, most, cuts=(), kind=jnp.bfloat16):
    level = steps_of(own_key, dims, cuts, -0.22, 0.18) if cuts else 1.0
    array = jax.random.normal(own_key, dims, jnp.float32) * spread * level
    return jnp.minimum(jnp.maximum(array, -most), most).astype(kind)


def setup_inputs(seed: int = 0) -> dict:
    seeds = jax.random.split(jax.random.key(seed), 19)
    tokens = gaussian(seeds[0], (IMAGES, SIDE, SIDE, D), 1.0, 6.0, ((0, 32),))
    cotangent = gaussian(seeds[1], (IMAGES, SIDE, SIDE, D), 1.0, 6.0, ((0, 32),))
    counts = ragged_sizes(seeds[2], DEVICES, LIVE, IMG_CAP, 2).astype(jnp.int32)
    w_qkv = gaussian(seeds[3], (D, 3 * D), D ** -0.5, 0.25, ((0, 2),), jnp.float32)
    w_proj = gaussian(seeds[4], (D, D), (D // 8) ** -0.5, 0.75, ((0, 2),), jnp.float32)
    w_fc1 = gaussian(seeds[5], (D, FF), D ** -0.5, 0.25, ((0, 2),), jnp.float32)
    w_fc2 = gaussian(seeds[6], (FF, D), FF ** -0.5, 0.125, ((0, 2),), jnp.float32)
    vectors = gaussian(seeds[7], (SMALL,), 0.05, 0.3, ((0, 2),), jnp.float32)
    first_qkv = gaussian(seeds[8], (D, 3 * D), (0.1 * (LIVE * SIDE * SIDE) ** 0.5), 103.90226, ((0, 2),), jnp.float32)
    first_proj = gaussian(seeds[9], (D, D), (0.1 * (LIVE * SIDE * SIDE) ** 0.5), 103.90226, ((0, 2),), jnp.float32)
    first_fc1 = gaussian(seeds[10], (D, FF), (0.1 * (LIVE * SIDE * SIDE) ** 0.5), 103.90226, ((0, 2),), jnp.float32)
    first_fc2 = gaussian(seeds[11], (FF, D), (0.1 * (LIVE * SIDE * SIDE) ** 0.5), 103.90226, ((0, 2),), jnp.float32)
    first_vec = gaussian(seeds[12], (SMALL,), (0.1 * (LIVE * SIDE * SIDE) ** 0.5), 103.90226, ((0, 2),), jnp.float32)
    second_qkv = jnp.clip(jnp.exp(math.log(29.988) - 2.3025851 * jax.random.uniform(seeds[13], (D, 3 * D), jnp.float32) ** steps_of(seeds[13], (D, 3 * D), ((0, 2),), -0.2, 0.2)), 2.9988, 29.988)
    second_proj = jnp.clip(jnp.exp(math.log(29.988) - 2.3025851 * jax.random.uniform(seeds[14], (D, D), jnp.float32) ** steps_of(seeds[14], (D, D), ((0, 2),), -0.2, 0.2)), 2.9988, 29.988)
    second_fc1 = jnp.clip(jnp.exp(math.log(29.988) - 2.3025851 * jax.random.uniform(seeds[15], (D, FF), jnp.float32) ** steps_of(seeds[15], (D, FF), ((0, 2),), -0.2, 0.2)), 2.9988, 29.988)
    second_fc2 = jnp.clip(jnp.exp(math.log(29.988) - 2.3025851 * jax.random.uniform(seeds[16], (FF, D), jnp.float32) ** steps_of(seeds[16], (FF, D), ((0, 2),), -0.2, 0.2)), 2.9988, 29.988)
    second_vec = jnp.clip(jnp.exp(math.log(29.988) - 2.3025851 * jax.random.uniform(seeds[17], (SMALL,), jnp.float32) ** steps_of(seeds[17], (SMALL,), ((0, 2),), -0.2, 0.2)), 2.9988, 29.988)
    return dict(tokens=tokens, cotangent=cotangent, counts=counts, w_qkv=w_qkv, w_proj=w_proj, w_fc1=w_fc1, w_fc2=w_fc2, vectors=vectors, first_qkv=first_qkv, first_proj=first_proj, first_fc1=first_fc1, first_fc2=first_fc2, first_vec=first_vec, second_qkv=second_qkv, second_proj=second_proj, second_fc1=second_fc1, second_fc2=second_fc2, second_vec=second_vec)


@jax.custom_vjp
def low(v):
    return lax.optimization_barrier(v.astype(jnp.bfloat16)).astype(jnp.float32)

@jax.custom_vjp
def low_back(v):
    return v

def low_keep(v):
    return (low(v), None)

def low_pass(kept, grad):
    return (grad,)

def back_keep(v):
    return (v, None)

def back_low(kept, grad):
    return (low(grad),)
low.defvjp(low_keep, low_pass)
low_back.defvjp(back_keep, back_low)
norm_eps = 1e-05
mask_fill = -100.0
learn_rate = 0.01
beta_first = 0.9
beta_second = 0.999
adam_eps = 1e-08
decay_rate = 0.05
highest = lax.Precision.HIGHEST

def layer_norm(values, gain_vec, shift_vec):
    average = lax.optimization_barrier(jnp.mean(values, axis=-1, keepdims=True))
    centred = values - average
    variance = lax.optimization_barrier(jnp.mean(centred * centred, axis=-1, keepdims=True))
    return centred * lax.rsqrt(variance + norm_eps) * (1.0 + gain_vec) + shift_vec

def window_split(grid_in):
    images = grid_in.shape[0]
    blocks = SIDE // WIN
    shaped = grid_in.reshape(images, blocks, WIN, blocks, WIN, grid_in.shape[-1])
    return shaped.transpose(0, 1, 3, 2, 4, 5).reshape(images * blocks * blocks, WIN * WIN, grid_in.shape[-1])

def window_join(windows, images):
    blocks = SIDE // WIN
    shaped = windows.reshape(images, blocks, blocks, WIN, WIN, windows.shape[-1])
    return shaped.transpose(0, 1, 3, 2, 4, 5).reshape(images, SIDE, SIDE, windows.shape[-1])

def relative_index():
    places = jnp.arange(WIN * WIN, dtype=jnp.int32)
    row_pos = places // WIN
    col_pos = places % WIN
    row_diff = row_pos[:, None] - row_pos[None, :] + WIN - 1
    col_diff = col_pos[:, None] - col_pos[None, :] + WIN - 1
    return row_diff * (2 * WIN - 1) + col_diff

def shift_mask():
    places = jnp.arange(SIDE, dtype=jnp.int32)
    band_ids = (places >= SIDE - WIN).astype(jnp.int32) + (places >= SIDE - SHIFT).astype(jnp.int32)
    region = band_ids[:, None] * 3 + band_ids[None, :]
    region_win = window_split(region[None, :, :, None])[:, :, 0]
    matching = region_win[:, :, None] == region_win[:, None, :]
    return jnp.where(matching, 0.0, mask_fill).astype(jnp.float32)

def unpack(vectors):
    pieces = [vectors[slot_num * D:(slot_num + 1) * D] for slot_num in range(8)]
    fc1_bias = vectors[8 * D:8 * D + FF]
    rel_table = vectors[8 * D + FF:].reshape(HEADS, RELS)
    return (pieces, fc1_bias, rel_table)

def block_forward(params, tokens_blk, alive_blk):
    w_qkv, w_proj, w_fc1, w_fc2, vectors = params
    pieces, fc1_bias, rel_table = unpack(vectors)
    gain_a, shift_a, q_bias, v_bias, proj_bias, gain_b, shift_b, fc2_bias = pieces
    images = tokens_blk.shape[0]
    normed_one = low(layer_norm(tokens_blk, gain_a, shift_a))
    rolled = jnp.roll(normed_one, (-SHIFT, -SHIFT), axis=(1, 2))
    windows = window_split(rolled)
    count_win = windows.shape[0]
    win_rows = windows.reshape(-1, D)
    qkv_bias = jnp.concatenate([q_bias, jnp.zeros((D,), jnp.float32), v_bias])
    packed = jnp.dot(win_rows, w_qkv, precision=highest, preferred_element_type=jnp.float32) + qkv_bias
    packed = low_back(low(packed)).reshape(count_win, WIN * WIN, 3, HEADS, HEAD_DIM)
    q_part = packed[:, :, 0]
    k_part = packed[:, :, 1]
    v_part = packed[:, :, 2]
    rel_bias = rel_table[:, relative_index()]
    mask_all = jnp.tile(shift_mask(), (images, 1, 1))
    scores = jnp.einsum('wqhd,wkhd->whqk', q_part, k_part, precision=highest) * HEAD_DIM ** (-0.5)
    scores = low_back(scores + rel_bias[None] + mask_all[:, None])
    expo_scores = jnp.exp(scores)
    attn_probs = low(expo_scores / lax.optimization_barrier(jnp.sum(expo_scores, axis=-1, keepdims=True)))
    attended = jnp.einsum('whqk,wkhd->wqhd', attn_probs, v_part, precision=highest)
    attended = low_back(low(attended.reshape(-1, D)))
    branch = jnp.dot(attended, w_proj, precision=highest, preferred_element_type=jnp.float32) + proj_bias
    branch = low_back(low(branch))
    branch_grid = window_join(branch.reshape(count_win, WIN * WIN, D), images)
    branch_grid = jnp.roll(branch_grid, (SHIFT, SHIFT), axis=(1, 2))
    middle = tokens_blk + branch_grid
    normed_two = low(layer_norm(middle, gain_b, shift_b)).reshape(-1, D)
    hidden = low_back(jnp.dot(normed_two, w_fc1, precision=highest, preferred_element_type=jnp.float32) + fc1_bias)
    activated = low(jax.nn.gelu(hidden, approximate=False))
    mlp_out = low_back(jnp.dot(activated, w_fc2, precision=highest, preferred_element_type=jnp.float32) + fc2_bias)
    result = middle + mlp_out.reshape(middle.shape)
    return result * alive_blk[:, None, None, None]

def forward(params, tokens_all, alive_mask):
    block_len = 2 * IMG_CAP
    blocks = IMAGES // block_len
    tok_blocks = tokens_all.reshape(blocks, block_len, SIDE, SIDE, D)
    alive_blocks = alive_mask.reshape(blocks, block_len)
    rounded = jax.tree.map(low, params)
    step_fn = jax.checkpoint(lambda block_pair: block_forward(rounded, block_pair[0], block_pair[1]))
    outputs = lax.map(step_fn, (tok_blocks, alive_blocks))
    return outputs.reshape(IMAGES, SIDE, SIDE, D)

def adam_step(weight, gradient, moment_one, moment_two, decay_here):
    moment_one_new = beta_first * moment_one + (1.0 - beta_first) * gradient
    moment_two_new = beta_second * moment_two + (1.0 - beta_second) * gradient * gradient
    first_hat = moment_one_new / (1.0 - beta_first ** STEP)
    second_hat = moment_two_new / (1.0 - beta_second ** STEP)
    weight_new = weight - learn_rate * (first_hat / (jnp.sqrt(second_hat) + adam_eps) + decay_here * weight)
    return (weight_new, moment_one_new, moment_two_new)

def reference(tokens, cotangent, counts, w_qkv, w_proj, w_fc1, w_fc2, vectors, first_qkv, first_proj, first_fc1, first_fc2, first_vec, second_qkv, second_proj, second_fc1, second_fc2, second_vec):
    slot_ids = jnp.arange(IMAGES, dtype=jnp.int32)
    alive_mask = (slot_ids % IMG_CAP < counts[slot_ids // IMG_CAP]).astype(jnp.float32)
    params = (w_qkv, w_proj, w_fc1, w_fc2, vectors)
    outputs, pullback = jax.vjp(lambda tok_in, par_in: forward(par_in, tok_in, alive_mask), tokens.astype(jnp.float32), params)
    grad_input, weight_grads = pullback(cotangent.astype(jnp.float32))
    grad_qkv, grad_proj, grad_fc1, grad_fc2, grad_vec = weight_grads
    new_qkv, new_first_qkv, new_second_qkv = adam_step(w_qkv, grad_qkv, first_qkv, second_qkv, decay_rate)
    new_proj, new_first_proj, new_second_proj = adam_step(w_proj, grad_proj, first_proj, second_proj, decay_rate)
    new_fc1, new_first_fc1, new_second_fc1 = adam_step(w_fc1, grad_fc1, first_fc1, second_fc1, decay_rate)
    new_fc2, new_first_fc2, new_second_fc2 = adam_step(w_fc2, grad_fc2, first_fc2, second_fc2, decay_rate)
    new_vec, new_first_vec, new_second_vec = adam_step(vectors, grad_vec, first_vec, second_vec, 0.0)
    return (outputs.astype(jnp.bfloat16), grad_input.astype(jnp.bfloat16), grad_qkv, grad_proj, grad_fc1, grad_fc2, grad_vec, new_qkv, new_proj, new_fc1, new_fc2, new_vec, new_first_qkv, new_first_proj, new_first_fc1, new_first_fc2, new_first_vec, new_second_qkv, new_second_proj, new_second_fc1, new_second_fc2, new_second_vec)
```

```python
import functools

import jax
import jax.numpy as jnp
import numpy as np
from jax import lax
from jax.experimental import pallas as pl
from jax.experimental.pallas import tpu as pltpu
from jax.sharding import PartitionSpec as P

HEADS = 16
HEAD_DIM = 32
WIN = 7
SIDE = 14
SHIFT = 3
STEP = 3
RELS = 169
TOK = SIDE * SIDE
TOK_PAD = 208
WIN_ROWS = 4 * 64
LANES = 128
GROUPS = HEADS * HEAD_DIM // LANES
PER_STEP = 2


norm_eps = 1e-05
mask_fill = -100.0
learn_rate = 0.01
beta_first = 0.9
beta_second = 0.999
adam_eps = 1e-08
decay_rate = 0.05
log2_e = 1.4426950408889634
score_scale = HEAD_DIM ** (-0.5)

CALLS = ((0, 1), (2,), (3,))

COSTS_US = dict(
    pack_a=3, pack_f=4, enter=7, attend=18, mlp=32, leave=5, heads_2=11, heads_1=6, project_back=5, finish=6, close=6, unpack_a=3,
    unpack_f=4,
)

VMEM_MIB = dict(
    pack_a=60, pack_f=60, enter=60, attend=60, mlp=60, leave=24, heads_2=32, heads_1=32, project_back=24,
    finish=32, close=32, unpack_a=16, unpack_f=20,
)

f32 = jnp.float32
bf16 = jnp.bfloat16


def nn(a, b):
    return lax.dot_general(a, b, (((1,), (0,)), ((), ())), preferred_element_type=f32)


def nt(a, b):
    return lax.dot_general(a, b, (((1,), (1,)), ((), ())), preferred_element_type=f32)


def tn(a, b):
    return lax.dot_general(a, b, (((0,), (0,)), ((), ())), preferred_element_type=f32)


def window_places():
    win, row, col = np.meshgrid(np.arange(4), np.arange(WIN), np.arange(WIN), indexing="ij")
    rolled_r = (win // 2) * WIN + row
    rolled_c = (win % 2) * WIN + col
    src = ((rolled_r + SHIFT) % SIDE) * SIDE + (rolled_c + SHIFT) % SIDE
    dst = win * 64 + row * 8 + col
    return src.reshape(-1), dst.reshape(-1), rolled_r, rolled_c


def shuffle_matrix():
    src, dst, _, _ = window_places()
    out = np.zeros((WIN_ROWS, TOK_PAD), np.float32)
    out[dst, src] = 1.0
    return out


def mask_table():
    _, _, rolled_r, rolled_c = window_places()
    band = lambda r: (r >= SIDE - WIN).astype(np.int32) + (r >= SIDE - SHIFT).astype(np.int32)
    region = (3 * band(rolled_r) + band(rolled_c)).reshape(4, WIN * WIN)
    places = (np.arange(WIN)[:, None] * 8 + np.arange(WIN)[None, :]).reshape(-1)
    out = np.full((4, 64, 64), 0.0, np.float32)
    out[:, :, :] = -1e30
    out[:, :, places] = 0.0
    block = np.where(region[:, :, None] == region[:, None, :], 0.0, mask_fill * log2_e)
    out[np.arange(4)[:, None, None], places[None, :, None], places[None, None, :]] = block
    keys_first = out.transpose(0, 2, 1).reshape(2, LANES, 64)
    return np.tile(keys_first, (1, 1, 4)).astype(np.float32)


def relative_onehot():
    row, col = np.meshgrid(np.arange(WIN), np.arange(WIN), indexing="ij")
    row, col = row.reshape(-1), col.reshape(-1)
    places = row * 8 + col
    index = (row[:, None] - row[None, :] + WIN - 1) * (2 * WIN - 1) + (
        col[:, None] - col[None, :] + WIN - 1
    )
    out = np.zeros((RELS, 64, 64), np.float32)
    out[index, places[None, :], places[:, None]] = 1.0
    return out


def table_matrix():
    row, col = np.meshgrid(np.arange(WIN), np.arange(WIN), indexing="ij")
    out = np.zeros((2, 64, 256), np.float32)
    reach = 2 * WIN - 1
    out[:, row * 8 + col, (WIN - 1) * (reach + 1) - reach * row - col] = 1.0
    return out.reshape(LANES, 256)


def stats(values):
    average = jnp.mean(values, axis=-1, keepdims=True)
    centred = values - average
    variance = jnp.mean(centred * centred, axis=-1, keepdims=True)
    inv_std = lax.rsqrt(variance + norm_eps)
    return centred * inv_std, inv_std


def norm_back(grad_out, normed, inv_std, gain_row):
    scaled = grad_out * gain_row
    first_mean = jnp.mean(scaled, axis=-1, keepdims=True)
    second_mean = jnp.mean(scaled * normed, axis=-1, keepdims=True)
    return inv_std * (scaled - first_mean - normed * second_mean)


def get_slot(sheet, slot, slots):
    rows = pl.ds(slot, TOK_PAD, stride=slots)
    return jnp.concatenate([sheet[g, rows, :] for g in range(GROUPS)], axis=1)


def put_slot(sheet, slot, slots, values):
    rows = pl.ds(slot, TOK_PAD, stride=slots)
    for g in range(GROUPS):
        sheet[g, rows, :] = values[:, g * LANES : (g + 1) * LANES]


def get_sheet(sheet, rows):
    return jnp.concatenate([sheet[g, 0:rows, :] for g in range(GROUPS)], axis=1)


def put_sheet(sheet, here, values):
    for g in range(GROUPS):
        sheet[g, here, :] = values[:, g * LANES : (g + 1) * LANES]


def pair_up(rows, diag):
    return jnp.concatenate([rows, rows], axis=1) * diag


def stack_heads(rows, head_masks):
    wide = jnp.concatenate([rows[0:64], rows[64:128]], axis=1)
    return jnp.concatenate([wide * m for m in head_masks], axis=0)


def merge_heads(stacked, lane_head):
    out = stacked[192:256]
    for h in (2, 1, 0):
        out = jnp.where(lane_head == h, stacked[64 * h : 64 * h + 64], out)
    return out


def over_keys(values):
    sums = [
        jnp.broadcast_to(jnp.sum(values[w : w + 64], axis=0, keepdims=True), (64, values.shape[1]))
        for w in (0, 64)
    ]
    return jnp.concatenate(sums, axis=0)


def block_masks():
    lane = lax.broadcasted_iota(jnp.int32, (1, 2 * LANES), 1)
    lane_head = (lane % LANES) // HEAD_DIM
    head_masks = [(lane_head == h).astype(f32).astype(bf16) for h in range(4)]
    row = lax.broadcasted_iota(jnp.int32, (LANES, 2 * LANES), 0)
    col = lax.broadcasted_iota(jnp.int32, (LANES, 2 * LANES), 1)
    diag = ((row // 64) == (col // LANES)).astype(f32).astype(bf16)
    lane_head64 = jnp.broadcast_to(lane_head, (64, 2 * LANES))
    return lane_head64, head_masks, diag


def join_rows(pos_ref, full, own_ref, near_ref, far_ref):
    half = own_ref.shape[0]
    shard, core = pos_ref[1], pos_ref[2]
    other = (1 - shard) * half
    part = half // 2
    full[pl.ds(pl.multiple_of(shard * half, 16), half), :] = own_ref[...]
    full[pl.ds(pl.multiple_of(other + core * part, 16), part), :] = near_ref[...]
    full[pl.ds(pl.multiple_of(other + (1 - core) * part, 16), part), :] = far_ref[...]


def enter_kernel(
    pos_ref, tok_ref, shuf_ref, vec_ref, rel_ref, mask_ref, low_ref, normed_ref, bias_ref, sheet
):
    step = pl.program_id(0)
    rows, width = tok_ref.shape
    slots = rows // TOK

    @pl.when(step == 0)
    def _():
        normed, _ = stats(tok_ref[...].astype(f32))
        put_sheet(sheet, slice(0, rows), normed)
        sheet[:, rows:, :] = jnp.zeros((GROUPS, sheet.shape[1] - rows, LANES), f32)
        for kind in range(2):
            for g in range(GROUPS):
                for w in (0, 64):
                    bias_ref[kind * GROUPS + g, w : w + 64, :] = (
                        rel_ref[g] + mask_ref[kind, w : w + 64, :]
                    )

    for i in range(PER_STEP):
        at = slice(i * WIN_ROWS, (i + 1) * WIN_ROWS)
        normed = get_slot(sheet, step * PER_STEP + i, slots)
        low = (normed * (1.0 + vec_ref[0:1, :]) + vec_ref[1:2, :]).astype(bf16)
        low_ref[at, :] = nn(shuf_ref[...], low).astype(bf16)
        normed_ref[at, :] = nn(shuf_ref[...], normed.astype(bf16)).astype(bf16)


def attend_kernel(
    pos_ref, win_ref, back_ref, own_ref, near_ref, far_ref, vec_ref, qkvb_ref, bias_ref, *refs
):
    packed_refs, prob_refs = refs[: len(CALLS)], refs[len(CALLS) : 2 * len(CALLS)]
    o_ref, att_ref, w_ref, sheet = refs[2 * len(CALLS) :]
    step = pl.program_id(0)
    rows, width = att_ref.shape
    slots = rows // TOK

    @pl.when(step == 0)
    def _():
        join_rows(pos_ref, w_ref, own_ref, near_ref, far_ref)

    at = 0
    for packed_ref in packed_refs:
        cols = slice(at, at + packed_ref.shape[1])
        packed_ref[...] = (nn(win_ref[...], w_ref[:, cols]) + qkvb_ref[0:1, cols]).astype(bf16)
        at = cols.stop

    lane_head, head_masks, diag = block_masks()
    units = [(i, n, len(groups)) for i, groups in enumerate(CALLS) for n in range(len(groups))]
    for pair in range(2 * PER_STEP):
        pick = slice(pair * LANES, (pair + 1) * LANES)
        take = lambda u, j: packed_refs[u[0]][
            pick, (j * u[2] + u[1]) * LANES : (j * u[2] + u[1] + 1) * LANES
        ]
        q = [stack_heads(take(u, 0), head_masks) for u in units]
        k = [pair_up(take(u, 1), diag) for u in units]
        s = [nt(a, b) for a, b in zip(k, q)]
        e = [
            jnp.exp2(s[g] * (score_scale * log2_e) + bias_ref[(pair % 2) * GROUPS + g])
            for g in range(GROUPS)
        ]
        p = [(a * (1.0 / over_keys(a))).astype(bf16) for a in e]
        for g, (i, n, count) in enumerate(units):
            prob_refs[i][pair * count + n] = p[g]
        v = [pair_up(take(u, 2), diag) for u in units]
        for g in range(GROUPS):
            o = merge_heads(tn(p[g], v[g]), lane_head).astype(bf16)
            cols = slice(g * LANES, (g + 1) * LANES)
            o_ref[pair * LANES : pair * LANES + 64, cols] = o[:, 0:LANES]
            o_ref[pair * LANES + 64 : (pair + 1) * LANES, cols] = o[:, LANES:]

    branch = (nn(o_ref[...], w_ref[:, 3 * width :]) + vec_ref[4:5, :]).astype(bf16)
    for i in range(PER_STEP):
        att = nn(back_ref[...], branch[i * WIN_ROWS : (i + 1) * WIN_ROWS])
        put_slot(sheet, step * PER_STEP + i, slots, att)

    @pl.when(step == pl.num_programs(0) - 1)
    def _():
        att_ref[...] = get_sheet(sheet, rows).astype(bf16)


def join_fc2(pos_ref, full, own_ref, near_ref, far_ref):
    half = own_ref.shape[0]
    shard, core = pos_ref[1], pos_ref[2]
    part = near_ref.shape[0] // 2
    width = full.shape[1]
    full[pl.ds(pl.multiple_of(shard * half, 16), half), :] = own_ref[...]
    for which, src in ((core, near_ref), (1 - core, far_ref)):
        for k in range(half // (2 * part)):
            at = (1 - shard) * half + k * 2 * part + which * part
            full[pl.ds(pl.multiple_of(at, 16), part), :] = src[
                part:, k * width : (k + 1) * width
            ]


def block_place(core, shard, block):
    return jnp.where(core == 0, 2 * shard + block, 2 * block + shard)


def mlp_kernel(
    pos_ref, tok_ref, att_ref, cot_ref, own1_ref, own2_ref, near_ref, far_ref, vec_ref, b1_ref,
    act, dx1_ref, keep_ref, send_ref, sum_ref, sumb_ref,
    w1_ref, w2_ref, acc1, acc2, dhid,
):
    step = pl.program_id(0)
    rows, width = tok_ref.shape
    hidden_width = w1_ref.shape[-1]
    slots = rows * pl.num_programs(0) // TOK
    shard, core = pos_ref[1], pos_ref[2]
    part = width // 4
    blocks = hidden_width // width

    @pl.when(step == 0)
    def _():
        join_rows(pos_ref, w1_ref, own1_ref, near_ref.at[0:part], far_ref.at[0:part])
        join_fc2(pos_ref, w2_ref, own2_ref, near_ref, far_ref)
        acc1[...] = jnp.zeros_like(acc1)
        acc2[...] = jnp.zeros_like(acc2)
        sum_ref[...] = jnp.zeros_like(sum_ref)
        sumb_ref[...] = jnp.zeros_like(sumb_ref)

    slot = lax.broadcasted_iota(jnp.int32, (rows, 1), 0) % slots
    alive = (slot < pos_ref[0]).astype(f32)
    x1 = tok_ref[...].astype(f32) + att_ref[...].astype(f32)
    normed, inv_std = stats(x1)
    gain = 1.0 + vec_ref[5:6, :]
    low = (normed * gain + vec_ref[6:7, :]).astype(bf16)
    dm = (cot_ref[...].astype(f32) * alive).astype(bf16)
    chunk = 512
    for c in range(hidden_width // chunk):
        cols = slice(c * chunk, (c + 1) * chunk)
        u = nn(low, w1_ref[:, cols]) + b1_ref[0:1, cols]
        bell = jnp.exp2(u * u * (-0.5 * log2_e))
        cdf = 0.5 + 0.5 * lax.erf(u * 0.7071067811865476)
        g = (u * cdf).astype(bf16)
        act[:, cols] = g
        dg = nt(dm, w2_ref[cols, :])
        du = (dg * (cdf + u * (bell * 0.3989422804014327))).astype(bf16)
        dhid[:, cols] = du
        sumb_ref[0:1, cols] += jnp.sum(du.astype(f32), axis=0, keepdims=True)
        acc1[:, cols] += tn(low, du)
        acc2[cols, :] += tn(g, dm)
    dh2 = nt(dhid[...], w1_ref[...])
    dm_f = dm.astype(f32)
    dx1_ref[...] = (dm_f + norm_back(dh2, normed, inv_std, gain)).astype(bf16)
    sum_ref[0:1, :] += jnp.sum(dh2 * normed, axis=0, keepdims=True)
    sum_ref[1:2, :] += jnp.sum(dh2, axis=0, keepdims=True)
    sum_ref[2:3, :] += jnp.sum(dm_f, axis=0, keepdims=True)

    @pl.when(step == pl.num_programs(0) - 1)
    def _():
        for which, dst in ((core, keep_ref), (1 - core, send_ref)):
            for sh in range(2):
                to = pl.ds(pl.multiple_of(block_place(which, sh, 0) * part, 16), part)
                at = sh * 2 * part + which * part
                dst[to, :] = acc1[pl.ds(pl.multiple_of(at, 16), part), :].astype(bf16)
                to = pl.ds(pl.multiple_of(block_place(which, sh, 1) * part, 16), part)
                for k in range(blocks):
                    at = sh * (hidden_width // 2) + k * 2 * part + which * part
                    dst[to, k * width : (k + 1) * width] = acc2[
                        pl.ds(pl.multiple_of(at, 16), part), :
                    ].astype(bf16)


def close_kernel(
    pos_ref, tok_ref, att_ref, act_ref, own_ref, near_ref, far_ref, vec_ref, out_ref, w_ref
):
    step = pl.program_id(0)
    rows = tok_ref.shape[0]
    slots = rows * pl.num_programs(0) // TOK

    @pl.when(step == 0)
    def _():
        join_fc2(pos_ref, w_ref, own_ref, near_ref, far_ref)

    slot = lax.broadcasted_iota(jnp.int32, (rows, 1), 0) % slots
    alive = (slot < pos_ref[0]).astype(f32)
    x1 = tok_ref[...].astype(f32) + att_ref[...].astype(f32)
    out = alive * (x1 + nn(act_ref[...], w_ref[...]) + vec_ref[7:8, :])
    out_ref[...] = out.astype(bf16)


def fold_table(ds_ref, lanes_ref, flat, first_head):
    flat[...] = jnp.zeros_like(flat)
    for g in range(ds_ref.shape[0]):
        whole_g = ds_ref[g].T
        high = whole_g.astype(bf16)
        low = (whole_g - high.astype(f32)).astype(bf16)
        spread = nn(high, lanes_ref[...]) + nn(low, lanes_ref[...])
        for h in range(4):
            total = jnp.zeros((8, 256), f32)
            for r in range(WIN):
                at = 64 * h + 8 * r
                total += pltpu.roll(spread[at : at + 8], (2 * WIN - 1) * r, 1)
            total = pltpu.roll(total, 0, 1, stride=1, stride_axis=0)
            entries = jnp.sum(total, axis=0, keepdims=True)
            entries = jnp.concatenate([entries, jnp.zeros((1, LANES), f32)], axis=1)
            first, shift = divmod((first_head + 4 * g + h) * RELS, LANES)
            if shift:
                entries = pltpu.roll(entries, shift, 1)
            for k in range(3):
                flat[first + k : first + k + 1, :] += entries[:, k * LANES : (k + 1) * LANES]


def leave_kernel(
    pos_ref, dx1_ref, shuf_ref, own_ref, near_ref, far_ref, o_ref,
    *refs,
):
    do_refs = refs[: len(CALLS)]
    gp_ref, sum_ref, w_ref, sheet = refs[len(CALLS) :]
    step = pl.program_id(0)
    rows, width = dx1_ref.shape
    slots = rows // TOK

    @pl.when(step == 0)
    def _():
        join_rows(pos_ref, w_ref, own_ref, near_ref, far_ref)
        put_sheet(sheet, slice(0, rows), dx1_ref[...].astype(f32))
        sheet[:, rows:, :] = jnp.zeros((GROUPS, sheet.shape[1] - rows, LANES), f32)
        gp_ref[...] = jnp.zeros_like(gp_ref)
        sum_ref[...] = jnp.zeros_like(sum_ref)

    da = []
    for i in range(PER_STEP):
        low = get_slot(sheet, step * PER_STEP + i, slots).astype(bf16)
        da.append(nn(shuf_ref[...], low))
    da = jnp.concatenate(da, axis=0)
    sum_ref[0:1, :] += jnp.sum(da, axis=0, keepdims=True)
    da = da.astype(bf16)
    do = nt(da, w_ref[...]).astype(bf16)
    for groups, do_ref in zip(CALLS, do_refs):
        do_ref[...] = do[:, groups[0] * LANES : (groups[-1] + 1) * LANES]
    gp_ref[...] += tn(o_ref[...], da)


def heads_kernel(*refs, groups, earlier_calls):
    (pos_ref, packed_ref, prob_ref, do_ref, normed_ref, vec_ref, lanes_ref,
     own_ref, near_ref, far_ref) = refs[:10]
    refs = refs[10:]
    last = earlier_calls > 0
    if last:
        g_refs, sum_refs, flat_refs = (
            refs[n * earlier_calls : (n + 1) * earlier_calls] for n in range(3)
        )
        (gp_ref, suma_ref, sumb_ref, sumh_ref, dp_ref, keep_ref, send_ref,
         w_ref, acc, ds_ref, flat, sum_ref) = refs[3 * earlier_calls :]
    else:
        dp_ref, g_ref, sum_ref, flat, w_ref, acc, ds_ref = refs
    step = pl.program_id(0)
    width, span = acc.shape
    third = span // 3

    @pl.when(step == 0)
    def _():
        join_rows(pos_ref, w_ref, own_ref, near_ref, far_ref)
        acc[...] = jnp.zeros_like(acc)
        ds_ref[...] = jnp.zeros_like(ds_ref)
        sum_ref[...] = jnp.zeros_like(sum_ref)

    lane_head, head_masks, diag = block_masks()
    for pair in range(2 * PER_STEP):
        pick = slice(pair * LANES, (pair + 1) * LANES)
        low_rows = slice(pair * LANES, pair * LANES + 64)
        high_rows = slice(pair * LANES + 64, (pair + 1) * LANES)
        every = range(len(groups))
        count = len(groups)
        at = [slice(g * LANES, (g + 1) * LANES) for g in range(3 * count)]
        do = [stack_heads(do_ref[pick, at[g]], head_masks) for g in every]
        v = [pair_up(packed_ref[pick, at[2 * count + g]], diag) for g in every]
        p = [prob_ref[pair * count + g] for g in every]
        dp = [nt(v[g], do[g]) for g in every]
        pf = [p[g].astype(f32) for g in every]
        delta = [over_keys(pf[g] * dp[g]) for g in every]
        dv = [nn(p[g], do[g]).astype(bf16) for g in every]
        ds = [pf[g] * (dp[g] - delta[g]) for g in every]
        for g in every:
            ds_ref[g] += ds[g]
        ds = [ds[g].astype(bf16) for g in every]
        k = [pair_up(packed_ref[pick, at[count + g]], diag) for g in every]
        q = [stack_heads(packed_ref[pick, at[g]], head_masks) for g in every]
        dk = [(nn(ds[g], q[g]) * score_scale).astype(bf16) for g in every]
        dq = [(merge_heads(tn(ds[g], k[g]), lane_head) * score_scale).astype(bf16) for g in every]
        for g in every:
            dp_ref[low_rows, at[g]] = dq[g][:, 0:LANES]
            dp_ref[high_rows, at[g]] = dq[g][:, LANES:]
            dp_ref[low_rows, at[count + g]] = dk[g][0:64, 0:LANES]
            dp_ref[high_rows, at[count + g]] = dk[g][64:, LANES:]
            dp_ref[low_rows, at[2 * count + g]] = dv[g][0:64, 0:LANES]
            dp_ref[high_rows, at[2 * count + g]] = dv[g][64:, LANES:]
    acc[...] += tn(normed_ref[...], dp_ref[...])
    sum_ref[0:1, 0:span] += jnp.sum(dp_ref[...].astype(f32), axis=0, keepdims=True)

    @pl.when(step == pl.num_programs(0) - 1)
    def _():
        weights = w_ref[...]
        sums = sum_ref[0:1, 0:span]
        ones = jnp.ones((8, span), bf16)
        high = sums.astype(bf16)
        low = (sums - high.astype(f32)).astype(bf16)
        both = jnp.concatenate([high, low, jnp.zeros((6, span), bf16)], axis=0)
        shift_grad = jnp.sum(nt(both, weights), axis=0, keepdims=True)
        product = weights.astype(f32) * acc[...]
        high = product.astype(bf16)
        low = (product - high.astype(f32)).astype(bf16)
        gain_grad = (nt(ones, high) + nt(ones, low))[0:1]
        gain = (1.0 + vec_ref[0:1, :]).reshape(width, 1)
        shift = vec_ref[1:2, :].reshape(width, 1)
        grads = gain * acc[...] + shift * sums
        fold_table(ds_ref, lanes_ref, flat, 4 * groups[0])
        if not last:
            g_ref[...] = grads.astype(bf16)
            sum_ref[1:2, 0:width] = gain_grad
            sum_ref[2:3, 0:width] = shift_grad
            return
        acc[...] = grads
        core = pos_ref[2]
        part = width // 8
        per = width // LANES
        all_sums = [r[0:1, 0 : 3 * len(c) * LANES] for r, c in zip(sum_refs, CALLS)] + [sums]
        thirds = lambda n: jnp.concatenate(
            [a[:, n * a.shape[1] // 3 : (n + 1) * a.shape[1] // 3] for a in all_sums], axis=1
        )
        rows_of = [
            sum([r[1:2, 0:width] for r in sum_refs], gain_grad),
            sum([r[2:3, 0:width] for r in sum_refs], shift_grad),
            thirds(0),
            thirds(2),
            suma_ref[0:1, :],
        ]
        rows_of += [sumb_ref[n : n + 1, :] for n in range(3)]
        pieces = [v[:, k * LANES : (k + 1) * LANES] for v in rows_of for k in range(per)]
        pieces += [
            sumh_ref[0:1, k * LANES : (k + 1) * LANES] for k in range(sumh_ref.shape[1] // LANES)
        ]
        block = jnp.concatenate(pieces + [sum([r[...] for r in flat_refs], flat[...])], axis=0)
        block = jnp.concatenate(
            [block, jnp.zeros((2 * part - block.shape[0], LANES), f32)], axis=0
        ).astype(bf16)
        for which, dst in ((core, keep_ref), (1 - core, send_ref)):
            for sh in range(2):
                for half in range(2):
                    src = sh * 4 * part + which * 2 * part + half * part
                    src = pl.ds(pl.multiple_of(src, 16), part)
                    to = pl.ds(pl.multiple_of(block_place(which, sh, half) * part, 16), part)
                    at = 0
                    for part_ref in (*g_refs, acc, gp_ref):
                        cols = slice(at, at + part_ref.shape[1])
                        dst[to, cols] = part_ref[src, :].astype(bf16)
                        at = cols.stop
                    dst[to, at:] = block[half * part : (half + 1) * part]


def project_back_kernel(pos_ref, *refs):
    dp_refs = refs[: len(CALLS)]
    own_ref, near_ref, far_ref, dh_ref, w_ref = refs[len(CALLS) :]

    @pl.when(pl.program_id(0) == 0)
    def _():
        join_rows(pos_ref, w_ref, own_ref, near_ref, far_ref)

    dp = jnp.concatenate([r[...] for r in dp_refs], axis=1)
    dh_ref[...] = nt(dp, w_ref[...]).astype(bf16)


def finish_kernel(pos_ref, dh_ref, back_ref, tok_ref, dx1_ref, vec_ref, gi_ref, sheet):
    step = pl.program_id(0)
    rows, width = tok_ref.shape
    slots = rows // TOK
    for i in range(PER_STEP):
        dh = nn(back_ref[...], dh_ref[i * WIN_ROWS : (i + 1) * WIN_ROWS, :])
        put_slot(sheet, step * PER_STEP + i, slots, dh)

    @pl.when(step == pl.num_programs(0) - 1)
    def _():
        normed, inv_std = stats(tok_ref[...].astype(f32))
        grad = norm_back(get_sheet(sheet, rows), normed, inv_std, 1.0 + vec_ref[0:1, :])
        gi_ref[...] = (dx1_ref[...].astype(f32) + grad).astype(bf16)


def whole(shape):
    return pl.BlockSpec(shape, lambda i, *_: (0,) * len(shape))


def by_rows(rows, cols):
    return pl.BlockSpec((rows, cols), lambda i, *_: (i, 0))


def struct(shape, dtype):
    return jax.ShapeDtypeStruct(shape, dtype)


def params(name):
    return pltpu.CompilerParams(
        dimension_semantics=("arbitrary",), vmem_limit_bytes=VMEM_MIB[name] << 20
    )


def call(kernel, name, steps, pos, ops, in_specs, outs, out_specs, scratch):
    return pl.pallas_call(
        kernel,
        grid_spec=pltpu.PrefetchScalarGridSpec(
            num_scalar_prefetch=1,
            grid=(steps,),
            in_specs=in_specs,
            out_specs=out_specs,
            scratch_shapes=scratch,
        ),
        out_shape=outs,
        compiler_params=params(name),
        cost_estimate=pl.CostEstimate(
            flops=COSTS_US[name] * 1_000_000_000, bytes_accessed=0, transcendentals=0
        ),
        name=name,
    )(pos, *ops)


def by_units(units):
    return pl.BlockSpec((units, LANES, 256), lambda i, *_: (i, 0, 0))


def columns(rows, cols, block):
    return pl.BlockSpec((rows, cols), lambda i, *_: (0, block))


def sheet_of(slots):
    return pltpu.VMEM((GROUPS, slots * TOK_PAD, LANES), f32)


def enter(pos, tokens, shuf, vec, rel, mask):
    rows, width = tokens.shape
    slots = rows // TOK
    wr = PER_STEP * WIN_ROWS
    ops = (tokens, shuf, vec, rel, mask)
    win = struct((slots * WIN_ROWS, width), bf16)
    bias = (2 * GROUPS, LANES, 256)
    return call(
        enter_kernel, "enter", slots // PER_STEP, pos, ops,
        [whole(a.shape) for a in ops],
        [win, win, struct(bias, f32)],
        [by_rows(wr, width), by_rows(wr, width), whole(bias)],
        [sheet_of(slots)],
    )


def attend(pos, win, *rest):
    rows, width = win.shape
    slots = rows // WIN_ROWS
    steps = slots // PER_STEP
    wr = PER_STEP * WIN_ROWS
    spans = [3 * len(groups) * LANES for groups in CALLS]
    units = [2 * PER_STEP * len(groups) for groups in CALLS]
    return call(
        attend_kernel, "attend", steps, pos, (win, *rest),
        [by_rows(wr, width)] + [whole(a.shape) for a in rest],
        [struct((rows, span), bf16) for span in spans]
        + [struct((steps * n, LANES, 256), bf16) for n in units]
        + [struct((rows, width), bf16), struct((slots * TOK, width), bf16)],
        [by_rows(wr, span) for span in spans]
        + [by_units(n) for n in units]
        + [by_rows(wr, width), whole((slots * TOK, width))],
        [pltpu.VMEM((width, 4 * width), bf16), sheet_of(slots)],
    )


def mlp(pos, tokens, att, cot, *rest):
    rows, width = cot.shape
    hidden = rest[0].shape[1]
    steps = 2
    part = rows // steps
    return call(
        mlp_kernel, "mlp", steps, pos, (tokens, att, cot, *rest),
        [by_rows(part, width)] * 3 + [whole(a.shape) for a in rest],
        [
            struct((rows, hidden), bf16),
            struct(cot.shape, bf16),
            struct((width, hidden), bf16),
            struct((width, hidden), bf16),
            struct((8, width), f32),
            struct((8, hidden), f32),
        ],
        [
            by_rows(part, hidden),
            by_rows(part, width),
            whole((width, hidden)),
            whole((width, hidden)),
            whole((8, width)),
            whole((8, hidden)),
        ],
        [
            pltpu.VMEM((width, hidden), bf16),
            pltpu.VMEM((hidden, width), bf16),
            pltpu.VMEM((width, hidden), f32),
            pltpu.VMEM((hidden, width), f32),
            pltpu.VMEM((part, hidden), bf16),
        ],
    )


def close(pos, tokens, att, act, own, near, far, vec):
    rows, width = tokens.shape
    hidden = act.shape[1]
    steps = 2
    part = rows // steps
    fixed = (own, near, far, vec)
    return call(
        close_kernel, "close", steps, pos, (tokens, att, act, *fixed),
        [by_rows(part, width)] * 2 + [by_rows(part, hidden)] + [whole(a.shape) for a in fixed],
        struct(tokens.shape, bf16), by_rows(part, width),
        [pltpu.VMEM((hidden, width), bf16)],
    )


def leave(pos, dx1, shuf, parts, o):
    rows, width = dx1.shape
    slots = rows // TOK
    wr = PER_STEP * WIN_ROWS
    cols = [len(groups) * LANES for groups in CALLS]
    return call(
        leave_kernel, "leave", slots // PER_STEP, pos, (dx1, shuf, *parts, o),
        [whole(dx1.shape), whole(shuf.shape)]
        + [columns(a.shape[0], width, 3) for a in parts]
        + [by_rows(wr, width)],
        [struct((slots * WIN_ROWS, c), bf16) for c in cols]
        + [struct((width, width), f32), struct((8, width), f32)],
        [by_rows(wr, c) for c in cols] + [whole((width, width)), whole((8, width))],
        [pltpu.VMEM((width, width), bf16), sheet_of(slots)],
    )


def heads_back(pos, which, packed, prob, do, normed, vec, lanes, parts, earlier=(), others=()):
    rows, span = packed.shape
    width = normed.shape[1]
    steps = rows // (PER_STEP * WIN_ROWS)
    wr = PER_STEP * WIN_ROWS
    units = prob.shape[0] // steps
    groups = CALLS[which]
    dp = struct((rows, span), bf16)
    scratch = [
        pltpu.VMEM((width, span), bf16),
        pltpu.VMEM((width, span), f32),
        pltpu.VMEM((len(groups), LANES, 256), f32),
    ]
    small, flat = (8, 3 * width), (24, LANES)
    if earlier:
        shape = (width // 2, 4 * width + LANES)
        outs, specs = [struct(shape, bf16)] * 2, [whole(shape)] * 2
        scratch += [pltpu.VMEM(flat, f32), pltpu.VMEM(small, f32)]
        earlier = [a[n] for n in range(3) for a in earlier]
    else:
        outs = [struct((width, span), bf16), struct(small, f32), struct(flat, f32)]
        specs = [whole(o.shape) for o in outs]
    extra = (*earlier, *others)
    at = 3 * groups[0] * LANES
    return call(
        functools.partial(heads_kernel, groups=groups, earlier_calls=len(earlier) // 3),
        "heads_%d" % len(groups), steps, pos,
        (packed, prob, do, normed, vec, lanes, *parts, *extra),
        [
            by_rows(wr, span), by_units(units), by_rows(wr, do.shape[1]), by_rows(wr, width),
            whole(vec.shape), whole(lanes.shape),
        ]
        + [columns(a.shape[0], span, at // span) for a in parts]
        + [whole(a.shape) for a in extra],
        [dp, *outs], [by_rows(wr, span), *specs], scratch,
    )


def project_back(pos, dps, parts):
    rows = dps[0].shape[0]
    width = parts[0].shape[1] // 4
    wr = PER_STEP * WIN_ROWS
    return call(
        project_back_kernel, "project_back", rows // wr, pos, (*dps, *parts),
        [by_rows(wr, a.shape[1]) for a in dps]
        + [columns(a.shape[0], 3 * width, 0) for a in parts],
        struct((rows, width), bf16), by_rows(wr, width),
        [pltpu.VMEM((width, 3 * width), bf16)],
    )


def finish(pos, dh, back, tokens, dx1, vec):
    rows, width = tokens.shape
    slots = rows // TOK
    wr = PER_STEP * WIN_ROWS
    fixed = (back, tokens, dx1, vec)
    return call(
        finish_kernel, "finish", slots // PER_STEP, pos, (dh, *fixed),
        [by_rows(wr, width)] + [whole(a.shape) for a in fixed],
        struct(tokens.shape, bf16), whole(tokens.shape), [sheet_of(slots)],
    )


def swap(values, axis, bit):
    count = lax.axis_size(axis)
    return lax.ppermute(values, axis, [(i, i ^ (1 << bit)) for i in range(count)])


SHARD_BIT = 0


def orders():
    top = (lax.axis_size("replica") * lax.axis_size("shard")).bit_length() - 1
    rest = tuple(range(4, top))
    return (SHARD_BIT, 2, 3, *rest), (3, SHARD_BIT, 2, *rest)


def swap_by_core(values, bits):
    count = lax.axis_size("replica") * lax.axis_size("shard")
    perm = [(i, i ^ (1 << bits[(i >> 1) & 1])) for i in range(count)]
    return lax.ppermute(values, ("replica", "shard"), perm)


def my_bits(bits, core, index):
    return (index >> jnp.where(core == 0, bits[0], bits[1])) & 1


class Sum:
    def __init__(self, keep, send, core):
        self.keep, self.core = keep, core
        self.index = lax.axis_index("replica") * 2 + lax.axis_index("shard")
        self.theirs = swap(send, "replica", 0)
        self.halvings = list(zip(*orders()))
        both = [tuple(b for b in o if b != SHARD_BIT) for o in orders()]
        self.gatherings = list(zip(*both))[::-1]
        self.last, self.done = None, False

    def wait(self, *others):
        self.keep = after(self.keep, *others)

    def step(self):
        if self.halvings:
            bits = self.halvings.pop(0)
            keep, theirs = self.keep, self.theirs
            half = keep.shape[0] // 2
            bit = my_bits(bits, self.core, self.index)
            take = lambda b: (
                lax.dynamic_slice_in_dim(keep, b * half, half, 0).astype(f32)
                + lax.dynamic_slice_in_dim(theirs, b * half, half, 0).astype(f32)
            ).astype(bf16)
            send = take(1 - bit)
            self.keep = take(bit)
            self.theirs = swap_by_core(send, bits)
            return send
        if self.last is None:
            total = (self.keep.astype(f32) + self.theirs.astype(f32)).astype(bf16)
        else:
            total = merge(self.keep, self.theirs, my_bits(self.last, self.core, self.index))
        self.keep = total
        if not self.gatherings:
            self.theirs, self.done = swap(total, "replica", 0), True
            return total
        self.last = self.gatherings.pop(0)
        self.theirs = swap_by_core(total, self.last)
        return total

def merge(mine, theirs, bit):
    pair = lambda a, b: jnp.concatenate([a, b], axis=0)
    return jnp.where(bit == 0, pair(mine, theirs), pair(theirs, mine))


def after(values, *others):
    return lax.optimization_barrier((values, *others))[0]


def call_columns(width):
    return [
        slice(j * width + groups[0] * LANES, j * width + (groups[-1] + 1) * LANES)
        for groups in CALLS
        for j in range(3)
    ]


def pack_a_kernel(pos_ref, qkv_ref, proj_ref, own_ref, send_ref):
    width = proj_ref.shape[1]
    at = 0
    for cols in call_columns(width):
        to = slice(at, at + cols.stop - cols.start)
        own_ref[:, to] = qkv_ref[:, cols].astype(bf16)
        at = to.stop
    own_ref[:, 3 * width :] = proj_ref[...].astype(bf16)
    rows = send_ref.shape[0]
    send_ref[...] = own_ref[pl.ds(pl.multiple_of(pos_ref[2] * rows, 16), rows), :]


def pack_a(pos, w_qkv, w_proj):
    rows, width = w_proj.shape
    own, send = (rows, 4 * width), (rows // 2, 4 * width)
    return call(
        pack_a_kernel, "pack_a", 1, pos, (w_qkv, w_proj),
        [whole(w_qkv.shape), whole(w_proj.shape)],
        [struct(own, bf16), struct(send, bf16)], [whole(own), whole(send)], [],
    )


def pack_f_kernel(pos_ref, fc1_ref, fc2_ref, own1_ref, own2_ref, send_ref):
    width = fc2_ref.shape[1]
    part = send_ref.shape[0] // 2
    own1_ref[...] = fc1_ref[...].astype(bf16)
    own2_ref[...] = fc2_ref[...].astype(bf16)
    core = pos_ref[2]
    send_ref[0:part, :] = own1_ref[pl.ds(pl.multiple_of(core * part, 16), part), :]
    for k in range(fc2_ref.shape[0] // (2 * part)):
        at = pl.ds(pl.multiple_of(k * 2 * part + core * part, 16), part)
        send_ref[part:, k * width : (k + 1) * width] = own2_ref[at, :]


def pack_f(pos, w_fc1, w_fc2):
    ops = (w_fc1, w_fc2)
    outs = [struct(a.shape, bf16) for a in (w_fc1, w_fc2, w_fc1)]
    return call(
        pack_f_kernel, "pack_f", 1, pos, ops, [whole(a.shape) for a in ops], outs,
        [whole(a.shape) for a in outs], [],
    )


def unpack_a_kernel(pos_ref, near_ref, far_ref, qkv_ref, proj_ref):
    width = proj_ref.shape[1]
    part = near_ref.shape[0]
    for which, src in ((pos_ref[2], near_ref), (1 - pos_ref[2], far_ref)):
        to = pl.ds(pl.multiple_of(which * part, 16), part)
        at = 0
        for cols in call_columns(width):
            end = at + cols.stop - cols.start
            qkv_ref[to, cols] = src[:, at:end].astype(f32)
            at = end
        proj_ref[to, :] = src[:, 3 * width : 4 * width].astype(f32)


def unpack_a(pos, near, far, w_qkv, w_proj):
    outs = [struct(w_qkv.shape, f32), struct(w_proj.shape, f32)]
    return call(
        unpack_a_kernel, "unpack_a", 1, pos, (near, far), [whole(near.shape)] * 2, outs,
        [whole(a.shape) for a in outs], [],
    )


def unpack_f_kernel(pos_ref, near_ref, far_ref, fc1_ref, fc2_ref):
    width = fc2_ref.shape[1]
    part = near_ref.shape[0] // 2
    for which, src in ((pos_ref[2], near_ref), (1 - pos_ref[2], far_ref)):
        to = pl.ds(pl.multiple_of(which * part, 16), part)
        fc1_ref[to, :] = src[0:part, :].astype(f32)
        for k in range(fc2_ref.shape[0] // (2 * part)):
            to = pl.ds(pl.multiple_of(k * 2 * part + which * part, 16), part)
            fc2_ref[to, :] = src[part:, k * width : (k + 1) * width].astype(f32)


def unpack_f(pos, near, far, w_fc1, w_fc2):
    outs = [struct(w_fc1.shape, f32), struct(w_fc2.shape, f32)]
    return call(
        unpack_f_kernel, "unpack_f", 1, pos, (near, far), [whole(near.shape)] * 2, outs,
        [whole(a.shape) for a in outs], [],
    )


def adam_step(weight, gradient, moment_one, moment_two, decay_here):
    moment_one_new = beta_first * moment_one + (1.0 - beta_first) * gradient
    moment_two_new = beta_second * moment_two + (1.0 - beta_second) * gradient * gradient
    first_hat = moment_one_new / (1.0 - beta_first**STEP)
    second_hat = moment_two_new / (1.0 - beta_second**STEP)
    weight_new = weight - learn_rate * (
        first_hat / (jnp.sqrt(second_hat) + adam_eps) + decay_here * weight
    )
    return (weight_new, moment_one_new, moment_two_new)


def on_device(
    tokens, cotangent, counts, w_qkv, w_proj, w_fc1, w_fc2, vectors,
    first_qkv, first_proj, first_fc1, first_fc2, first_vec,
    second_qkv, second_proj, second_fc1, second_fc2, second_vec,
):
    slots, width = tokens.shape[0], tokens.shape[3]
    by_token = lambda a: a.transpose(1, 2, 0, 3).reshape(TOK * slots, width)
    by_slot = lambda a: a.reshape(SIDE, SIDE, slots, width).transpose(2, 0, 1, 3)
    tokens, cotangent = by_token(tokens), by_token(cotangent)
    shard = lax.axis_index("shard")
    core = lax.axis_index("replica") % 2
    pos = jnp.stack([counts[0], shard, core]).astype(jnp.int32)

    vec_low = vectors.astype(bf16)
    other_vec = swap(vec_low, "shard", 0)
    own_a, send_a = pack_a(pos, w_qkv, w_proj)
    near_a = swap(send_a, "shard", 0)
    own_1, own_2, send_f = pack_f(after(pos, send_a), w_fc1, w_fc2)
    pair = jnp.concatenate
    full_vec = jnp.where(shard == 0, pair([vec_low, other_vec]), pair([other_vec, vec_low]))
    hidden = w_fc1.shape[1]
    vec_f = full_vec.astype(f32)
    vec8 = vec_f[: 8 * width].reshape(8, width)
    b1 = vec_f[8 * width : 8 * width + hidden].reshape(1, hidden)
    table = full_vec[8 * width + hidden :].reshape(HEADS, RELS)
    qkvb = jnp.concatenate([vec8[2], jnp.zeros((width,), f32), vec8[3]])
    qkvb = jnp.concatenate([qkvb[cols] for cols in call_columns(width)]).reshape(1, 3 * width)
    rel = log2_e * jnp.einsum(
        "hr,rkq->khq", table, jnp.asarray(relative_onehot(), bf16), preferred_element_type=f32
    )
    rel = rel.reshape(64, GROUPS, 256).transpose(1, 0, 2)
    shuffle = shuffle_matrix()
    shuf = jnp.asarray(shuffle, bf16)
    back = jnp.asarray(shuffle.T, bf16)
    mask = jnp.asarray(mask_table())
    lanes = jnp.asarray(table_matrix(), bf16)

    win, normed, bias = enter(pos, after(tokens, send_f), shuf, vec8, rel, mask)
    near_f = swap(send_f, "shard", 0)
    near_a = after(near_a, normed)
    far_a = swap(near_a, "replica", 0)
    parts = (own_a, near_a, far_a)
    calls = len(CALLS)
    *saved, o, att = attend(pos, win, back, *parts, vec8, qkvb, bias)
    packed, prob = saved[:calls], saved[calls:]
    far_f = swap(after(near_f, att), "replica", 0)
    act, dx1, keep_f, send_f, sumb, sumh = mlp(
        pos, tokens, att, cotangent, own_1, own_2, near_f, far_f, vec8, b1
    )
    near_w, far_w = near_f, far_f
    sum_f = Sum(keep_f, send_f, core)
    *do, grad_proj, suma = leave(pos, dx1, shuf, parts, o)
    dps, earlier = [], []
    for n in range(calls):
        sent_f = sum_f.step()
        dp, *rest = heads_back(
            pos, n, packed[n], prob[n], after(do[n], sent_f, *dps), normed, vec8, lanes, parts,
            *((earlier, (grad_proj, suma, sumb, sumh)) if n == calls - 1 else ()),
        )
        dps.append(dp)
        earlier.append(rest)
    keep_a, send_a = rest
    sent_f = sum_f.step()
    sum_a = Sum(keep_a, after(send_a, sent_f), core)
    sent_a = sum_a.step()
    dh1 = project_back(pos, (after(dps[0], sent_f, sent_a), *dps[1:]), parts)
    sum_f.wait(dh1)
    sent_f = sum_f.step()
    sum_a.wait(dh1)
    sent_a = sum_a.step()
    grad_input = finish(pos, after(dh1, sent_f, sent_a), back, tokens, dx1, vec8)
    sum_f.wait(grad_input)
    sent_f = sum_f.step()
    sum_a.wait(grad_input)
    sent_a = sum_a.step()
    out = close(pos, after(tokens, sent_f, sent_a), att, act, own_2, near_w, far_w, vec8)
    sum_f.wait(out)
    sum_a.wait(out)
    while not sum_f.done:
        sent_f = sum_f.step()
        sum_a.wait(sent_f)
        sent_a = sum_a.step()
        came_f, came_a = sum_f.theirs, sum_a.theirs
        sum_f.wait(came_a)
        sum_a.wait(came_f)
    near_f, far_f = sum_f.keep, sum_f.theirs
    grad_fc1, grad_fc2 = unpack_f(pos, near_f, far_f, w_fc1, w_fc2)
    step_fc1 = adam_step(w_fc1, grad_fc1, first_fc1, second_fc1, decay_rate)
    sum_a.wait(*step_fc1)
    sent_a = sum_a.step()
    grad_fc2 = after(grad_fc2, sent_a)
    step_fc2 = adam_step(w_fc2, grad_fc2, first_fc2, second_fc2, decay_rate)
    sum_a.wait(*step_fc2)
    while not sum_a.done:
        sent_a = sum_a.step()
    near_a, far_a = sum_a.keep, sum_a.theirs
    grad_vec = near_a[:, 4 * width :].astype(f32).reshape(-1)
    grad_vec = lax.dynamic_slice_in_dim(grad_vec, shard * vectors.shape[0], vectors.shape[0], 0)
    step_vec = adam_step(vectors, grad_vec, first_vec, second_vec, 0.0)
    grad_qkv, grad_proj = unpack_a(pos, near_a, far_a, w_qkv, w_proj)
    step_qkv = adam_step(w_qkv, grad_qkv, first_qkv, second_qkv, decay_rate)
    step_proj = adam_step(w_proj, grad_proj, first_proj, second_proj, decay_rate)
    steps = [
        (grad_qkv, *step_qkv),
        (grad_proj, *step_proj),
        (grad_fc1, *step_fc1),
        (grad_fc2, *step_fc2),
        (grad_vec, *step_vec),
    ]
    return (by_slot(out), by_slot(grad_input), *(s[k] for k in range(4) for s in steps))


def solution(mesh):
    tok = P(("replica", "shard"), None, None, None)
    mat, vec = P("shard", None), P("shard")
    group = (mat, mat, mat, mat, vec)
    return jax.shard_map(
        on_device,
        mesh=mesh,
        in_specs=(tok, tok, P(("replica", "shard"))) + group * 3,
        out_specs=(tok, tok) + group * 4,
        check_vma=False,
    )
```

```python
import functools

import jax
import jax.numpy as jnp
import numpy as np
from jax import lax
from jax.experimental import pallas as pl
from jax.experimental.pallas import tpu as pltpu
from jax.sharding import PartitionSpec as P

HEADS = 16
HEAD_DIM = 32
WIN = 7
SIDE = 14
SHIFT = 3
STEP = 3
RELS = 169
TOK = SIDE * SIDE
TOK_PAD = 208
WIN_ROWS = 4 * 64
LANES = 128
GROUPS = HEADS * HEAD_DIM // LANES
PER_STEP = 2


norm_eps = 1e-05
mask_fill = -100.0
learn_rate = 0.01
beta_first = 0.9
beta_second = 0.999
adam_eps = 1e-08
decay_rate = 0.05
log2_e = 1.4426950408889634
score_scale = HEAD_DIM ** (-0.5)

CALLS = ((0, 1), (2,), (3,))

COSTS_US = dict(
    pack=2, enter=10, attend=18, norm=6, mlp=28, leave=5, heads_2=11, heads_1=6, project_back=5, finish=6, close=6, unpack_a=3,
    unpack_f=4,
)

VMEM_MIB = dict(
    pack=60, enter=60, attend=60, norm=60, mlp=60, leave=24, heads_2=32, heads_1=32, project_back=24,
    finish=32, close=32, unpack_a=16, unpack_f=20,
)

IN_VMEM = {"leave", "heads_2", "heads_1", "project_back", "finish", "close", "attend", "norm", "mlp"}
SCOPED_MIB = dict(
    pack=8, enter=24, attend=24, norm=16, mlp=28, leave=16, heads_2=16, heads_1=16,
    project_back=12, finish=20, close=16, unpack_a=8, unpack_f=8,
)

f32 = jnp.float32
bf16 = jnp.bfloat16


def nn(a, b):
    return lax.dot_general(a, b, (((1,), (0,)), ((), ())), preferred_element_type=f32)


def nt(a, b):
    return lax.dot_general(a, b, (((1,), (1,)), ((), ())), preferred_element_type=f32)


def tn(a, b):
    return lax.dot_general(a, b, (((0,), (0,)), ((), ())), preferred_element_type=f32)


def window_places():
    win, row, col = np.meshgrid(np.arange(4), np.arange(WIN), np.arange(WIN), indexing="ij")
    rolled_r = (win // 2) * WIN + row
    rolled_c = (win % 2) * WIN + col
    src = ((rolled_r + SHIFT) % SIDE) * SIDE + (rolled_c + SHIFT) % SIDE
    dst = win * 64 + row * 8 + col
    return src.reshape(-1), dst.reshape(-1), rolled_r, rolled_c


def shuffle_matrix():
    src, dst, _, _ = window_places()
    out = np.zeros((WIN_ROWS, TOK_PAD), np.float32)
    out[dst, src] = 1.0
    return out


def mask_table():
    _, _, rolled_r, rolled_c = window_places()
    band = lambda r: (r >= SIDE - WIN).astype(np.int32) + (r >= SIDE - SHIFT).astype(np.int32)
    region = (3 * band(rolled_r) + band(rolled_c)).reshape(4, WIN * WIN)
    places = (np.arange(WIN)[:, None] * 8 + np.arange(WIN)[None, :]).reshape(-1)
    out = np.full((4, 64, 64), 0.0, np.float32)
    out[:, :, :] = -1e30
    out[:, :, places] = 0.0
    block = np.where(region[:, :, None] == region[:, None, :], 0.0, mask_fill * log2_e)
    out[np.arange(4)[:, None, None], places[None, :, None], places[None, None, :]] = block
    keys_first = out.transpose(0, 2, 1).reshape(2, LANES, 64)
    return np.tile(keys_first, (1, 1, 4)).astype(np.float32)


def place_matrix():
    row, col = np.meshgrid(np.arange(WIN), np.arange(WIN), indexing="ij")
    out = np.zeros((256, 64), np.float32)
    out[(2 * WIN - 1) * row + col, row * 8 + col] = 1.0
    return out


def table_matrix():
    row, col = np.meshgrid(np.arange(WIN), np.arange(WIN), indexing="ij")
    out = np.zeros((2, 64, 256), np.float32)
    reach = 2 * WIN - 1
    out[:, row * 8 + col, (WIN - 1) * (reach + 1) - reach * row - col] = 1.0
    return out.reshape(LANES, 256)


def stats(values):
    average = jnp.mean(values, axis=-1, keepdims=True)
    centred = values - average
    variance = jnp.mean(centred * centred, axis=-1, keepdims=True)
    inv_std = lax.rsqrt(variance + norm_eps)
    return centred * inv_std, inv_std


def norm_back(grad_out, normed, inv_std, gain_row):
    scaled = grad_out * gain_row
    first_mean = jnp.mean(scaled, axis=-1, keepdims=True)
    second_mean = jnp.mean(scaled * normed, axis=-1, keepdims=True)
    return inv_std * (scaled - first_mean - normed * second_mean)


def get_slot(sheet, slot, slots):
    rows = pl.ds(slot, TOK_PAD, stride=slots)
    return jnp.concatenate([sheet[g, rows, :] for g in range(GROUPS)], axis=1)


def put_slot(sheet, slot, slots, values):
    rows = pl.ds(slot, TOK_PAD, stride=slots)
    for g in range(GROUPS):
        sheet[g, rows, :] = values[:, g * LANES : (g + 1) * LANES]


def get_sheet(sheet, rows):
    return jnp.concatenate([sheet[g, 0:rows, :] for g in range(GROUPS)], axis=1)


def put_sheet(sheet, here, values):
    for g in range(GROUPS):
        sheet[g, here, :] = values[:, g * LANES : (g + 1) * LANES]


def pair_up(rows, diag):
    return jnp.concatenate([rows, rows], axis=1) * diag


def stack_heads(rows, head_masks):
    wide = jnp.concatenate([rows[0:64], rows[64:128]], axis=1)
    return jnp.concatenate([wide * m for m in head_masks], axis=0)


def merge_heads(stacked, lane_head):
    out = stacked[192:256]
    for h in (2, 1, 0):
        out = jnp.where(lane_head == h, stacked[64 * h : 64 * h + 64], out)
    return out


def over_keys(values):
    sums = [
        jnp.broadcast_to(jnp.sum(values[w : w + 64], axis=0, keepdims=True), (64, values.shape[1]))
        for w in (0, 64)
    ]
    return jnp.concatenate(sums, axis=0)


def block_masks():
    lane = lax.broadcasted_iota(jnp.int32, (1, 2 * LANES), 1)
    lane_head = (lane % LANES) // HEAD_DIM
    head_masks = [(lane_head == h).astype(f32).astype(bf16) for h in range(4)]
    row = lax.broadcasted_iota(jnp.int32, (LANES, 2 * LANES), 0)
    col = lax.broadcasted_iota(jnp.int32, (LANES, 2 * LANES), 1)
    diag = ((row // 64) == (col // LANES)).astype(f32).astype(bf16)
    lane_head64 = jnp.broadcast_to(lane_head, (64, 2 * LANES))
    return lane_head64, head_masks, diag


def join_rows(pos_ref, full, own_ref, near_ref, far_ref):
    half = own_ref.shape[0]
    shard, core = pos_ref[1], pos_ref[2]
    other = (1 - shard) * half
    part = half // 2
    full[pl.ds(pl.multiple_of(shard * half, 16), half), :] = own_ref[...]
    full[pl.ds(pl.multiple_of(other + core * part, 16), part), :] = near_ref[...]
    full[pl.ds(pl.multiple_of(other + (1 - core) * part, 16), part), :] = far_ref[...]


def vec_part(vec_ref, n, width):
    return vec_ref[0:1, n * width : (n + 1) * width]


def enter_kernel(
    pos_ref, tok_ref, shuf_ref, qkv_ref, proj_ref, fc1_ref, fc2_ref, part1_ref, part2_ref,
    high_ref, low_ref, own_ref, own1_ref, own2_ref, send_ref, sheet,
):
    step = this_step()
    rows, width = tok_ref.shape
    slots = rows // TOK

    @pl.when(step == 0)
    def _():
        normed, _ = stats(tok_ref[...].astype(f32))
        put_sheet(sheet, slice(0, rows), normed)
        sheet[:, rows:, :] = jnp.zeros((GROUPS, sheet.shape[1] - rows, LANES), f32)

    for i in range(PER_STEP):
        at = slice(i * WIN_ROWS, (i + 1) * WIN_ROWS)
        normed = get_slot(sheet, step * PER_STEP + i, slots)
        high = normed.astype(bf16)
        low = (normed - high.astype(f32)).astype(bf16)
        high_ref[at, :] = nn(shuf_ref[...], high).astype(bf16)
        low_ref[at, :] = nn(shuf_ref[...], low).astype(bf16)
    pack_columns(own_ref, qkv_ref, proj_ref)
    own1_ref[...] = fc1_ref[...].astype(bf16)
    own2_ref[...] = fc2_ref[...].astype(bf16)
    steps = send_ref.shape[1] // width
    part = part1_ref.shape[0]
    send_ref[pl.ds(pl.multiple_of(step * part, 16), part), :] = part1_ref[...].astype(bf16)
    for k in range(steps):
        @pl.when(step == k)
        def _():
            send_ref[steps * part :, k * width : (k + 1) * width] = part2_ref[...].astype(bf16)


def score_bias(vec_ref, mask_ref, place_ref, bias):
    width = GROUPS * LANES
    table_at = 12 * width
    reach = 2 * WIN - 1
    for g in range(GROUPS):
        blocks = []
        for h in range(4):
            at = table_at + (4 * g + h) * RELS
            shift = at % LANES
            entries = vec_ref[0:1, at - shift : at - shift + 3 * LANES]
            if shift:
                entries = pltpu.roll(entries, 3 * LANES - shift, 1)
            entries = jnp.broadcast_to(entries[:, 0:256], (8, 256))
            entries = pltpu.roll(entries, 0, 1, stride=1, stride_axis=0)
            for r in range(WIN):
                turn = 256 - (WIN - 1) * (reach + 1) + reach * r
                blocks.append(pltpu.roll(entries, turn, 1))
            blocks.append(jnp.zeros((8, 256), f32))
        spread = nn(jnp.concatenate(blocks, axis=0).astype(bf16), place_ref[...]) * log2_e
        rel = jnp.concatenate([spread[64 * h : 64 * h + 64] for h in range(4)], axis=1)
        for kind in range(2):
            for w in (0, 64):
                bias[kind * GROUPS + g, w : w + 64, :] = rel + mask_ref[kind, w : w + 64, :]


def attend_kernel(
    pos_ref, high_ref, low_ref, back_ref, own_ref, near_ref, far_ref, vec_ref, mask_ref, place_ref,
    *refs,
):
    packed_refs, prob_refs = refs[: len(CALLS)], refs[len(CALLS) : 2 * len(CALLS)]
    o_ref, att_ref, w_ref, sheet, bias_ref = refs[2 * len(CALLS) :]
    step = this_step()
    rows, width = att_ref.shape
    slots = rows // TOK

    @pl.when(step == 0)
    def _():
        join_rows(pos_ref, w_ref, own_ref, near_ref, far_ref)
        score_bias(vec_ref, mask_ref, place_ref, bias_ref)

    normed = high_ref[...].astype(f32) + low_ref[...].astype(f32)
    low = (normed * (1.0 + vec_part(vec_ref, 0, width)) + vec_part(vec_ref, 1, width)).astype(bf16)
    none = jnp.zeros((1, width), f32)
    biases = (vec_part(vec_ref, 2, width), none, vec_part(vec_ref, 3, width))
    at = 0
    for groups, packed_ref in zip(CALLS, packed_refs):
        cols = slice(at, at + packed_ref.shape[1])
        here = slice(groups[0] * LANES, (groups[-1] + 1) * LANES)
        added = jnp.concatenate([b[:, here] for b in biases], axis=1)
        packed_ref[...] = (nn(low, w_ref[:, cols]) + added).astype(bf16)
        at = cols.stop

    lane_head, head_masks, diag = block_masks()
    units = [(i, n, len(groups)) for i, groups in enumerate(CALLS) for n in range(len(groups))]
    for pair in range(2 * PER_STEP):
        pick = slice(pair * LANES, (pair + 1) * LANES)
        take = lambda u, j: packed_refs[u[0]][
            pick, (j * u[2] + u[1]) * LANES : (j * u[2] + u[1] + 1) * LANES
        ]
        q = [stack_heads(take(u, 0), head_masks) for u in units]
        k = [pair_up(take(u, 1), diag) for u in units]
        s = [nt(a, b) for a, b in zip(k, q)]
        e = [
            jnp.exp2(s[g] * (score_scale * log2_e) + bias_ref[(pair % 2) * GROUPS + g])
            for g in range(GROUPS)
        ]
        p = [(a * (1.0 / over_keys(a))).astype(bf16) for a in e]
        for g, (i, n, count) in enumerate(units):
            prob_refs[i][pair * count + n] = p[g]
        v = [pair_up(take(u, 2), diag) for u in units]
        for g in range(GROUPS):
            o = merge_heads(tn(p[g], v[g]), lane_head).astype(bf16)
            cols = slice(g * LANES, (g + 1) * LANES)
            o_ref[pair * LANES : pair * LANES + 64, cols] = o[:, 0:LANES]
            o_ref[pair * LANES + 64 : (pair + 1) * LANES, cols] = o[:, LANES:]

    branch = (nn(o_ref[...], w_ref[:, 3 * width :]) + vec_part(vec_ref, 4, width)).astype(bf16)
    for i in range(PER_STEP):
        att = nn(back_ref[...], branch[i * WIN_ROWS : (i + 1) * WIN_ROWS])
        put_slot(sheet, step * PER_STEP + i, slots, att)

    @pl.when(step == all_steps() - 1)
    def _():
        att_ref[...] = get_sheet(sheet, rows).astype(bf16)


def join_fc2(pos_ref, full, own_ref, near_ref, far_ref):
    half = own_ref.shape[0]
    shard, core = pos_ref[1], pos_ref[2]
    part = near_ref.shape[0] // 2
    width = full.shape[1]
    for k in range(half // (2 * part)):
        at = k * 4 * part + shard * 2 * part
        full[pl.ds(pl.multiple_of(at, 16), 2 * part), :] = own_ref[
            k * 2 * part : (k + 1) * 2 * part, :
        ]
        for which, src in ((core, near_ref), (1 - core, far_ref)):
            at = k * 4 * part + (1 - shard) * 2 * part + which * part
            full[pl.ds(pl.multiple_of(at, 16), part), :] = src[
                part:, k * width : (k + 1) * width
            ]


def block_place(core, shard, block):
    return jnp.where(core == 0, 2 * shard + block, 2 * block + shard)


def norm_kernel(
    pos_ref, tok_ref, att_ref, cot_ref, vec_ref, low_ref, norm_ref, dm_ref, inv_ref, sum_ref
):
    rows, width = tok_ref.shape
    slots = rows * all_steps() // TOK

    @pl.when(this_step() == 0)
    def _():
        sum_ref[...] = jnp.zeros_like(sum_ref)

    normed, inv_std = stats(tok_ref[...].astype(f32) + att_ref[...].astype(f32))
    gain, shift = vec_part(vec_ref, 5, width), vec_part(vec_ref, 6, width)
    low_ref[...] = (normed * (1.0 + gain) + shift).astype(bf16)
    norm_ref[...] = normed.astype(bf16)
    inv_ref[...] = jnp.broadcast_to(inv_std, inv_ref.shape)
    slot = lax.broadcasted_iota(jnp.int32, (rows, 1), 0) % slots
    dm = cot_ref[...].astype(f32) * (slot < pos_ref[0]).astype(f32)
    dm_ref[...] = dm.astype(bf16)
    sum_ref[0:1, :] += jnp.sum(dm, axis=0, keepdims=True)


def mlp_kernel(
    pos_ref, low_s, dm_s, norm_s, inv_s,
    own1a_ref, near1a_ref, far1a_ref, own1b_ref, near1b_ref, far1b_ref,
    own2_ref, near2_ref, far2_ref, vec_ref, b1a_ref, b1b_ref,
    act_ref, dx1_ref, keep_ref, send_ref, sum_ref, sumb_ref,
    w1_ref, w2_ref, dhid, dh_s,
):
    step = this_step()
    rows, width = low_s.shape
    core = pos_ref[2]
    part = width // 4
    @pl.when(step == 0)
    def _():
        sum_ref[...] = jnp.zeros_like(sum_ref)
        dh_s[...] = jnp.zeros_like(dh_s)

    join_rows(pos_ref, w1_ref.at[:, 0 : 2 * part], own1a_ref, near1a_ref, far1a_ref)
    join_rows(pos_ref, w1_ref.at[:, 2 * part :], own1b_ref, near1b_ref, far1b_ref)
    join_rows(pos_ref, w2_ref, own2_ref, near2_ref, far2_ref)
    b1 = jnp.concatenate([b1a_ref[0:1, :], b1b_ref[0:1, :]], axis=1)
    total = jnp.zeros((1, 4 * part), f32)
    pieces = 2
    for n in range(pieces):
        at = slice(n * rows // pieces, (n + 1) * rows // pieces)
        u = nn(low_s[at, :], w1_ref[...]) + b1
        bell = jnp.exp2(u * u * (-0.5 * log2_e))
        cdf = 0.5 + 0.5 * lax.erf(u * 0.7071067811865476)
        act_ref[at, :] = (u * cdf).astype(bf16)
        dg = nt(dm_s[at, :], w2_ref[...])
        du = (dg * (cdf + u * (bell * 0.3989422804014327))).astype(bf16)
        dhid[at, :] = du
        total += jnp.sum(du.astype(f32), axis=0, keepdims=True)
        dh_s[at, :] += nt(du, w1_ref[...])
    sumb_ref[0:1, :] = total
    grads = tn(low_s[...], dhid[...]), tn(act_ref[...], dm_s[...])
    for sh in range(2):
        for block, grad in enumerate(grads):
            first = grad[sh * 2 * part : sh * 2 * part + part]
            second = grad[sh * 2 * part + part : (sh + 1) * 2 * part]
            for which, dst in ((core, keep_ref), (1 - core, send_ref)):
                to = pl.ds(pl.multiple_of(block_place(which, sh, block) * part, 16), part)
                dst[to, :] = jnp.where(which == 0, first, second).astype(bf16)

    @pl.when(step == all_steps() - 1)
    def _():
        dh2, normed = dh_s[...], norm_s[...].astype(f32)
        inv_std = jnp.concatenate([inv_s[...]] * GROUPS, axis=1)
        grad = norm_back(dh2, normed, inv_std, 1.0 + vec_part(vec_ref, 5, width))
        dx1_ref[...] = (dm_s[...].astype(f32) + grad).astype(bf16)
        sum_ref[0:1, :] = jnp.sum(dh2 * normed, axis=0, keepdims=True)
        sum_ref[1:2, :] = jnp.sum(dh2, axis=0, keepdims=True)


def close_kernel(
    pos_ref, tok_ref, att_ref, act_ref, own_ref, near_ref, far_ref, vec_ref, out_ref, w_ref
):
    step = this_step()
    rows = tok_ref.shape[0]
    slots = rows * all_steps() // TOK

    @pl.when(step == 0)
    def _():
        join_fc2(pos_ref, w_ref, own_ref, near_ref, far_ref)

    slot = lax.broadcasted_iota(jnp.int32, (rows, 1), 0) % slots
    alive = (slot < pos_ref[0]).astype(f32)
    x1 = tok_ref[...].astype(f32) + att_ref[...].astype(f32)
    out = alive * (x1 + nn(act_ref[...], w_ref[...]) + vec_part(vec_ref, 7, out_ref.shape[1]))
    out_ref[...] = out.astype(bf16)


def fold_table(ds_ref, lanes_ref, flat, first_head):
    flat[...] = jnp.zeros_like(flat)
    for g in range(ds_ref.shape[0]):
        whole_g = ds_ref[g].T
        high = whole_g.astype(bf16)
        low = (whole_g - high.astype(f32)).astype(bf16)
        spread = nn(high, lanes_ref[...]) + nn(low, lanes_ref[...])
        for h in range(4):
            total = jnp.zeros((8, 256), f32)
            for r in range(WIN):
                at = 64 * h + 8 * r
                total += pltpu.roll(spread[at : at + 8], (2 * WIN - 1) * r, 1)
            total = pltpu.roll(total, 0, 1, stride=1, stride_axis=0)
            entries = jnp.sum(total, axis=0, keepdims=True)
            entries = jnp.concatenate([entries, jnp.zeros((1, LANES), f32)], axis=1)
            first, shift = divmod((first_head + 4 * g + h) * RELS, LANES)
            if shift:
                entries = pltpu.roll(entries, shift, 1)
            for k in range(3):
                flat[first + k : first + k + 1, :] += entries[:, k * LANES : (k + 1) * LANES]


def leave_kernel(
    pos_ref, dx1_ref, shuf_ref, own_ref, near_ref, far_ref, o_ref,
    *refs,
):
    do_refs = refs[: len(CALLS)]
    gp_ref, sum_ref, w_ref, sheet = refs[len(CALLS) :]
    step = this_step()
    rows, width = dx1_ref.shape
    slots = rows // TOK

    @pl.when(step == 0)
    def _():
        join_rows(pos_ref, w_ref, own_ref, near_ref, far_ref)
        put_sheet(sheet, slice(0, rows), dx1_ref[...].astype(f32))
        sheet[:, rows:, :] = jnp.zeros((GROUPS, sheet.shape[1] - rows, LANES), f32)
        gp_ref[...] = jnp.zeros_like(gp_ref)
        sum_ref[...] = jnp.zeros_like(sum_ref)

    da = []
    for i in range(PER_STEP):
        low = get_slot(sheet, step * PER_STEP + i, slots).astype(bf16)
        da.append(nn(shuf_ref[...], low))
    da = jnp.concatenate(da, axis=0)
    sum_ref[0:1, :] += jnp.sum(da, axis=0, keepdims=True)
    da = da.astype(bf16)
    do = nt(da, w_ref[...]).astype(bf16)
    for groups, do_ref in zip(CALLS, do_refs):
        do_ref[...] = do[:, groups[0] * LANES : (groups[-1] + 1) * LANES]
    gp_ref[...] += tn(o_ref[...], da)


def heads_kernel(*refs, groups, earlier_calls):
    (pos_ref, packed_ref, prob_ref, do_ref, normed_ref, vec_ref, lanes_ref,
     own_ref, near_ref, far_ref) = refs[:10]
    refs = refs[10:]
    last = earlier_calls > 0
    if last:
        g_refs, sum_refs, flat_refs = (
            refs[n * earlier_calls : (n + 1) * earlier_calls] for n in range(3)
        )
        (gp_ref, suma_ref, sumb_ref, sumc_ref, sumh_ref, dp_ref, keep_ref, send_ref,
         w_ref, acc, ds_ref, flat, sum_ref) = refs[3 * earlier_calls :]
    else:
        dp_ref, g_ref, sum_ref, flat, w_ref, acc, ds_ref = refs
    step = this_step()
    width, span = acc.shape
    third = span // 3

    @pl.when(step == 0)
    def _():
        join_rows(pos_ref, w_ref, own_ref, near_ref, far_ref)
        acc[...] = jnp.zeros_like(acc)
        ds_ref[...] = jnp.zeros_like(ds_ref)
        sum_ref[...] = jnp.zeros_like(sum_ref)

    lane_head, head_masks, diag = block_masks()
    for pair in range(2 * PER_STEP):
        pick = slice(pair * LANES, (pair + 1) * LANES)
        low_rows = slice(pair * LANES, pair * LANES + 64)
        high_rows = slice(pair * LANES + 64, (pair + 1) * LANES)
        every = range(len(groups))
        count = len(groups)
        at = [slice(g * LANES, (g + 1) * LANES) for g in range(3 * count)]
        do = [stack_heads(do_ref[pick, at[g]], head_masks) for g in every]
        v = [pair_up(packed_ref[pick, at[2 * count + g]], diag) for g in every]
        p = [prob_ref[pair * count + g] for g in every]
        dp = [nt(v[g], do[g]) for g in every]
        pf = [p[g].astype(f32) for g in every]
        delta = [over_keys(pf[g] * dp[g]) for g in every]
        dv = [nn(p[g], do[g]).astype(bf16) for g in every]
        ds = [pf[g] * (dp[g] - delta[g]) for g in every]
        for g in every:
            ds_ref[g] += ds[g]
        ds = [ds[g].astype(bf16) for g in every]
        k = [pair_up(packed_ref[pick, at[count + g]], diag) for g in every]
        q = [stack_heads(packed_ref[pick, at[g]], head_masks) for g in every]
        dk = [(nn(ds[g], q[g]) * score_scale).astype(bf16) for g in every]
        dq = [(merge_heads(tn(ds[g], k[g]), lane_head) * score_scale).astype(bf16) for g in every]
        for g in every:
            dp_ref[low_rows, at[g]] = dq[g][:, 0:LANES]
            dp_ref[high_rows, at[g]] = dq[g][:, LANES:]
            dp_ref[low_rows, at[count + g]] = dk[g][0:64, 0:LANES]
            dp_ref[high_rows, at[count + g]] = dk[g][64:, LANES:]
            dp_ref[low_rows, at[2 * count + g]] = dv[g][0:64, 0:LANES]
            dp_ref[high_rows, at[2 * count + g]] = dv[g][64:, LANES:]
    acc[...] += tn(normed_ref[...], dp_ref[...])
    sum_ref[0:1, 0:span] += jnp.sum(dp_ref[...].astype(f32), axis=0, keepdims=True)

    @pl.when(step == all_steps() - 1)
    def _():
        weights = w_ref[...]
        sums = sum_ref[0:1, 0:span]
        ones = jnp.ones((8, span), bf16)
        high = sums.astype(bf16)
        low = (sums - high.astype(f32)).astype(bf16)
        both = jnp.concatenate([high, low, jnp.zeros((6, span), bf16)], axis=0)
        shift_grad = jnp.sum(nt(both, weights), axis=0, keepdims=True)
        product = weights.astype(f32) * acc[...]
        high = product.astype(bf16)
        low = (product - high.astype(f32)).astype(bf16)
        gain_grad = (nt(ones, high) + nt(ones, low))[0:1]
        gain = (1.0 + vec_part(vec_ref, 0, width)).reshape(width, 1)
        shift = vec_part(vec_ref, 1, width).reshape(width, 1)
        grads = gain * acc[...] + shift * sums
        fold_table(ds_ref, lanes_ref, flat, 4 * groups[0])
        if not last:
            g_ref[...] = grads.astype(bf16)
            sum_ref[1:2, 0:width] = gain_grad
            sum_ref[2:3, 0:width] = shift_grad
            return
        acc[...] = grads
        core = pos_ref[2]
        part = width // 8
        per = width // LANES
        all_sums = [r[0:1, 0 : 3 * len(c) * LANES] for r, c in zip(sum_refs, CALLS)] + [sums]
        thirds = lambda n: jnp.concatenate(
            [a[:, n * a.shape[1] // 3 : (n + 1) * a.shape[1] // 3] for a in all_sums], axis=1
        )
        rows_of = [
            sum([r[1:2, 0:width] for r in sum_refs], gain_grad),
            sum([r[2:3, 0:width] for r in sum_refs], shift_grad),
            thirds(0),
            thirds(2),
            suma_ref[0:1, :],
        ]
        rows_of += [sumb_ref[0:1, :], sumb_ref[1:2, :], sumc_ref[0:1, :]]
        pieces = [v[:, k * LANES : (k + 1) * LANES] for v in rows_of for k in range(per)]
        mine = 2 * part
        blocks = sumh_ref.shape[1] // (4 * mine)
        for sh in range(2):
            for k in range(blocks):
                at = k * 4 * mine + sh * 2 * mine
                pieces += [sumh_ref[0:1, at : at + mine], sumh_ref[0:1, at + mine : at + 2 * mine]]
        block = jnp.concatenate(pieces + [sum([r[...] for r in flat_refs], flat[...])], axis=0)
        block = jnp.concatenate(
            [block, jnp.zeros((2 * part - block.shape[0], LANES), f32)], axis=0
        ).astype(bf16)
        for which, dst in ((core, keep_ref), (1 - core, send_ref)):
            for sh in range(2):
                for half in range(2):
                    src = sh * 4 * part + which * 2 * part + half * part
                    src = pl.ds(pl.multiple_of(src, 16), part)
                    to = pl.ds(pl.multiple_of(block_place(which, sh, half) * part, 16), part)
                    at = 0
                    for part_ref in (*g_refs, acc, gp_ref):
                        cols = slice(at, at + part_ref.shape[1])
                        dst[to, cols] = part_ref[src, :].astype(bf16)
                        at = cols.stop
                    dst[to, at:] = block[half * part : (half + 1) * part]


def project_back_kernel(pos_ref, *refs):
    dp_refs = refs[: len(CALLS)]
    own_ref, near_ref, far_ref, dh_ref, w_ref = refs[len(CALLS) :]

    @pl.when(this_step() == 0)
    def _():
        join_rows(pos_ref, w_ref, own_ref, near_ref, far_ref)

    dp = jnp.concatenate([r[...] for r in dp_refs], axis=1)
    dh_ref[...] = nt(dp, w_ref[...]).astype(bf16)


def finish_kernel(pos_ref, dh_ref, back_ref, tok_ref, dx1_ref, vec_ref, gi_ref, sheet):
    step = this_step()
    rows, width = tok_ref.shape
    slots = rows // TOK
    for i in range(PER_STEP):
        dh = nn(back_ref[...], dh_ref[i * WIN_ROWS : (i + 1) * WIN_ROWS, :])
        put_slot(sheet, step * PER_STEP + i, slots, dh)

    @pl.when(step == all_steps() - 1)
    def _():
        normed, inv_std = stats(tok_ref[...].astype(f32))
        grad = norm_back(get_sheet(sheet, rows), normed, inv_std, 1.0 + vec_part(vec_ref, 0, width))
        gi_ref[...] = (dx1_ref[...].astype(f32) + grad).astype(bf16)


def whole(shape):
    return pl.BlockSpec(shape, lambda i, *_: (0,) * len(shape))


def by_rows(rows, cols):
    return pl.BlockSpec((rows, cols), lambda i, *_: (i, 0))


def struct(shape, dtype):
    return jax.ShapeDtypeStruct(shape, dtype)


def params(name):
    return pltpu.CompilerParams(
        dimension_semantics=("arbitrary",), vmem_limit_bytes=VMEM_MIB[name] << 20
    )


LOOP = []


def this_step():
    return LOOP[-1][0] if LOOP else pl.program_id(0)


def all_steps():
    return LOOP[-1][1] if LOOP else pl.num_programs(0)


def block_of(ref, spec, step, pos_ref):
    if spec.block_shape is None or tuple(spec.block_shape) == tuple(ref.shape):
        return ref
    cuts = []
    for at, size, full in zip(spec.index_map(step, pos_ref), spec.block_shape, ref.shape):
        if size == full:
            cuts.append(slice(None))
        elif isinstance(at, int):
            cuts.append(slice(at * size, (at + 1) * size))
        else:
            cuts.append(pl.ds(pl.multiple_of(at * size, size), size))
    return ref.at[tuple(cuts)]


def call(kernel, name, steps, pos, ops, in_specs, outs, out_specs, scratch):
    cost = pl.CostEstimate(
        flops=COSTS_US[name] * 1_000_000_000, bytes_accessed=0, transcendentals=0
    )
    if name not in IN_VMEM:
        return pl.pallas_call(
            kernel,
            grid_spec=pltpu.PrefetchScalarGridSpec(
                num_scalar_prefetch=1,
                grid=(steps,),
                in_specs=in_specs,
                out_specs=out_specs,
                scratch_shapes=scratch,
            ),
            out_shape=outs,
            compiler_params=params(name),
            cost_estimate=cost,
            name=name,
        )(pos, *ops)

    several = isinstance(outs, (list, tuple))
    specs = [*in_specs, *(out_specs if several else [out_specs])]

    def loop(pos_ref, *refs):
        def one(step, carry):
            LOOP.append((step, steps))
            blocks = [block_of(r, s, step, pos_ref) for r, s in zip(refs, specs)]
            kernel(pos_ref, *blocks, *refs[len(specs) :])
            LOOP.pop()
            return carry

        if steps == 1:
            one(jnp.int32(0), 0)
        else:
            lax.fori_loop(0, steps, one, 0)

    here = pl.BlockSpec(memory_space=pltpu.VMEM)
    return pl.pallas_call(
        loop,
        in_specs=[pl.BlockSpec(memory_space=pltpu.SMEM)] + [here] * len(ops),
        out_specs=[here] * len(outs) if several else here,
        out_shape=outs,
        scratch_shapes=scratch,
        compiler_params=pltpu.CompilerParams(vmem_limit_bytes=SCOPED_MIB[name] << 20),
        cost_estimate=cost,
        name=name,
    )(pos, *ops)


def by_units(units):
    return pl.BlockSpec((units, LANES, 256), lambda i, *_: (i, 0, 0))


def columns(rows, cols, block):
    return pl.BlockSpec((rows, cols), lambda i, *_: (0, block))


def sheet_of(slots):
    return pltpu.VMEM((GROUPS, slots * TOK_PAD, LANES), f32)


def enter(pos, tokens, shuf, w_qkv, w_proj, w_fc1, w_fc2):
    rows, width = tokens.shape
    slots = rows // TOK
    steps = slots // PER_STEP
    wr = PER_STEP * WIN_ROWS
    hidden = w_fc1.shape[1]
    weights = (w_qkv, w_proj, w_fc1, w_fc2)
    blocks = [(a.shape[0] // steps, a.shape[1]) for a in weights]
    parts = [(w_fc1.shape[0] // 2 // steps, hidden), (w_fc2.shape[0] // 2 // steps, width)]
    win = struct((slots * WIN_ROWS, width), bf16)
    own, send = (w_qkv.shape[0], 4 * width), (width // 2, hidden)
    return call(
        enter_kernel, "enter", steps, pos, (tokens, shuf, *weights, w_fc1, w_fc2),
        [whole(tokens.shape), whole(shuf.shape)]
        + [by_rows(*block) for block in blocks]
        + [
            pl.BlockSpec(parts[0], lambda i, pos: (pos[2] * steps + i, 0)),
            pl.BlockSpec(parts[1], lambda i, pos: (2 * i + pos[2], 0)),
        ],
        [win, win]
        + [struct(a, bf16) for a in (own, w_fc1.shape, w_fc2.shape, send)],
        [by_rows(wr, width)] * 2
        + [by_rows(own[0] // steps, own[1]), by_rows(*blocks[2]), by_rows(*blocks[3]), whole(send)],
        [sheet_of(slots)],
    )


def attend(pos, high, low, *rest):
    rows, width = high.shape
    slots = rows // WIN_ROWS
    steps = slots // PER_STEP
    wr = PER_STEP * WIN_ROWS
    spans = [3 * len(groups) * LANES for groups in CALLS]
    units = [2 * PER_STEP * len(groups) for groups in CALLS]
    return call(
        attend_kernel, "attend", steps, pos, (high, low, *rest),
        [by_rows(wr, width)] * 2 + [whole(a.shape) for a in rest],
        [struct((rows, span), bf16) for span in spans]
        + [struct((steps * n, LANES, 256), bf16) for n in units]
        + [struct((rows, width), bf16), struct((slots * TOK, width), bf16)],
        [by_rows(wr, span) for span in spans]
        + [by_units(n) for n in units]
        + [by_rows(wr, width), whole((slots * TOK, width))],
        [
            pltpu.VMEM((width, 4 * width), bf16),
            sheet_of(slots),
            pltpu.VMEM((2 * GROUPS, LANES, 256), f32),
        ],
    )


def norm(pos, tokens, att, cot, vec):
    rows, width = cot.shape
    steps = 2
    part = rows // steps
    low = struct(cot.shape, bf16)
    return call(
        norm_kernel, "norm", steps, pos, (tokens, att, cot, vec),
        [by_rows(part, width)] * 3 + [whole(vec.shape)],
        [low, low, low, struct((rows, LANES), f32), struct((8, width), f32)],
        [by_rows(part, width)] * 3 + [by_rows(part, LANES), whole((8, width))], [],
    )


def mlp(pos, low, dm, normed, inv, own1, own2, near, far, vec):
    rows, width = low.shape
    hidden = own1.shape[1]
    half = width // 2
    steps = hidden // width
    part = width // 4
    at = lambda rows, cols, row, col: pl.BlockSpec((rows, cols), lambda i, *_: (row, col + i))
    by_columns = lambda rows, cols: pl.BlockSpec((rows, cols), lambda i, *_: (0, i))
    first_b1 = 8 * width // half
    return call(
        mlp_kernel, "mlp", steps, pos,
        (low, dm, normed, inv, own1, near, far, own1, near, far, own2, near, far, vec, vec, vec),
        [whole(low.shape)] * 2
        + [pl.BlockSpec(memory_space=pl.ANY)] * 2
        + [at(half, half, 0, 0), at(part, half, 0, 0), at(part, half, 0, 0)]
        + [at(half, half, 0, steps), at(part, half, 0, steps), at(part, half, 0, steps)]
        + [by_rows(half, width), at(part, width, 1, 0), at(part, width, 1, 0)]
        + [whole(vec.shape), at(1, half, 0, first_b1), at(1, half, 0, first_b1 + steps)],
        [
            struct((rows, hidden), bf16),
            struct(low.shape, bf16),
            struct((width, hidden), bf16),
            struct((width, hidden), bf16),
            struct((8, width), f32),
            struct((8, hidden), f32),
        ],
        [
            by_columns(rows, width),
            whole(low.shape),
            by_columns(width, width),
            by_columns(width, width),
            whole((8, width)),
            by_columns(8, width),
        ],
        [
            pltpu.VMEM((width, width), bf16),
            pltpu.VMEM((width, width), bf16),
            pltpu.VMEM((rows, width), bf16),
            pltpu.VMEM((rows, width), f32),
        ],
    )


def close(pos, tokens, att, act, own, near, far, vec):
    rows, width = tokens.shape
    hidden = act.shape[1]
    steps = 2
    part = rows // steps
    fixed = (own, near, far, vec)
    return call(
        close_kernel, "close", steps, pos, (tokens, att, act, *fixed),
        [by_rows(part, width)] * 2 + [by_rows(part, hidden)] + [whole(a.shape) for a in fixed],
        struct(tokens.shape, bf16), by_rows(part, width),
        [pltpu.VMEM((hidden, width), bf16)],
    )


def leave(pos, dx1, shuf, parts, o):
    rows, width = dx1.shape
    slots = rows // TOK
    wr = PER_STEP * WIN_ROWS
    cols = [len(groups) * LANES for groups in CALLS]
    return call(
        leave_kernel, "leave", slots // PER_STEP, pos, (dx1, shuf, *parts, o),
        [whole(dx1.shape), whole(shuf.shape)]
        + [columns(a.shape[0], width, 3) for a in parts]
        + [by_rows(wr, width)],
        [struct((slots * WIN_ROWS, c), bf16) for c in cols]
        + [struct((width, width), f32), struct((8, width), f32)],
        [by_rows(wr, c) for c in cols] + [whole((width, width)), whole((8, width))],
        [pltpu.VMEM((width, width), bf16), sheet_of(slots)],
    )


def heads_back(pos, which, packed, prob, do, normed, vec, lanes, parts, earlier=(), others=()):
    rows, span = packed.shape
    width = normed.shape[1]
    steps = rows // (PER_STEP * WIN_ROWS)
    wr = PER_STEP * WIN_ROWS
    units = prob.shape[0] // steps
    groups = CALLS[which]
    dp = struct((rows, span), bf16)
    scratch = [
        pltpu.VMEM((width, span), bf16),
        pltpu.VMEM((width, span), f32),
        pltpu.VMEM((len(groups), LANES, 256), f32),
    ]
    small, flat = (8, 3 * width), (24, LANES)
    if earlier:
        shape = (width // 2, 4 * width + LANES)
        outs, specs = [struct(shape, bf16)] * 2, [whole(shape)] * 2
        scratch += [pltpu.VMEM(flat, f32), pltpu.VMEM(small, f32)]
        earlier = [a[n] for n in range(3) for a in earlier]
    else:
        outs = [struct((width, span), bf16), struct(small, f32), struct(flat, f32)]
        specs = [whole(o.shape) for o in outs]
    extra = (*earlier, *others)
    at = 3 * groups[0] * LANES
    return call(
        functools.partial(heads_kernel, groups=groups, earlier_calls=len(earlier) // 3),
        "heads_%d" % len(groups), steps, pos,
        (packed, prob, do, normed, vec, lanes, *parts, *extra),
        [
            by_rows(wr, span), by_units(units), by_rows(wr, do.shape[1]), by_rows(wr, width),
            whole(vec.shape), whole(lanes.shape),
        ]
        + [columns(a.shape[0], span, at // span) for a in parts]
        + [whole(a.shape) for a in extra],
        [dp, *outs], [by_rows(wr, span), *specs], scratch,
    )


def project_back(pos, dps, parts):
    rows = dps[0].shape[0]
    width = parts[0].shape[1] // 4
    wr = PER_STEP * WIN_ROWS
    return call(
        project_back_kernel, "project_back", rows // wr, pos, (*dps, *parts),
        [by_rows(wr, a.shape[1]) for a in dps]
        + [columns(a.shape[0], 3 * width, 0) for a in parts],
        struct((rows, width), bf16), by_rows(wr, width),
        [pltpu.VMEM((width, 3 * width), bf16)],
    )


def finish(pos, dh, back, tokens, dx1, vec):
    rows, width = tokens.shape
    slots = rows // TOK
    wr = PER_STEP * WIN_ROWS
    fixed = (back, tokens, dx1, vec)
    return call(
        finish_kernel, "finish", slots // PER_STEP, pos, (dh, *fixed),
        [by_rows(wr, width)] + [whole(a.shape) for a in fixed],
        struct(tokens.shape, bf16), whole(tokens.shape), [sheet_of(slots)],
    )


def swap(values, axis, bit):
    count = lax.axis_size(axis)
    return lax.ppermute(values, axis, [(i, i ^ (1 << bit)) for i in range(count)])


SHARD_BIT = 0


def orders():
    top = (lax.axis_size("replica") * lax.axis_size("shard")).bit_length() - 1
    rest = tuple(range(4, top))
    return (SHARD_BIT, 2, 3, *rest), (3, SHARD_BIT, 2, *rest)


def swap_by_core(values, bits):
    count = lax.axis_size("replica") * lax.axis_size("shard")
    perm = [(i, i ^ (1 << bits[(i >> 1) & 1])) for i in range(count)]
    return lax.ppermute(values, ("replica", "shard"), perm)


def my_bits(bits, core, index):
    return (index >> jnp.where(core == 0, bits[0], bits[1])) & 1


class Sum:
    def __init__(self, keep, send, core):
        self.keep, self.core = keep, core
        self.index = lax.axis_index("replica") * 2 + lax.axis_index("shard")
        self.theirs = swap(send, "replica", 0)
        self.halvings = list(zip(*orders()))
        both = [tuple(b for b in o if b != SHARD_BIT) for o in orders()]
        self.gatherings = list(zip(*both))[::-1]
        self.last, self.done = None, False

    def wait(self, *others):
        self.keep = after(self.keep, *others)

    def step(self):
        if self.halvings:
            bits = self.halvings.pop(0)
            keep, theirs = self.keep, self.theirs
            half = keep.shape[0] // 2
            bit = my_bits(bits, self.core, self.index)
            take = lambda b: (
                lax.dynamic_slice_in_dim(keep, b * half, half, 0).astype(f32)
                + lax.dynamic_slice_in_dim(theirs, b * half, half, 0).astype(f32)
            ).astype(bf16)
            send = take(1 - bit)
            self.keep = take(bit)
            self.theirs = swap_by_core(send, bits)
            return send
        if self.last is None:
            total = (self.keep.astype(f32) + self.theirs.astype(f32)).astype(bf16)
        else:
            total = merge(self.keep, self.theirs, my_bits(self.last, self.core, self.index))
        self.keep = total
        if not self.gatherings:
            self.theirs, self.done = swap(total, "replica", 0), True
            return total
        self.last = self.gatherings.pop(0)
        self.theirs = swap_by_core(total, self.last)
        return total

def merge(mine, theirs, bit):
    pair = lambda a, b: jnp.concatenate([a, b], axis=0)
    return jnp.where(bit == 0, pair(mine, theirs), pair(theirs, mine))


def after(values, *others):
    return lax.optimization_barrier((values, *others))[0]


def call_columns(width):
    return [
        slice(j * width + groups[0] * LANES, j * width + (groups[-1] + 1) * LANES)
        for groups in CALLS
        for j in range(3)
    ]


def pack_columns(own_ref, qkv_ref, proj_ref):
    width = proj_ref.shape[1]
    at = 0
    for cols in call_columns(width):
        to = slice(at, at + cols.stop - cols.start)
        own_ref[:, to] = qkv_ref[:, cols].astype(bf16)
        at = to.stop
    own_ref[:, at:] = proj_ref[...].astype(bf16)


def pack_kernel(core_ref, qkv_ref, proj_ref, send_ref):
    pack_columns(send_ref, qkv_ref, proj_ref)


def pack(core, w_qkv, w_proj):
    rows, width = w_proj.shape
    mine = lambda a: pl.BlockSpec((rows // 2, a.shape[1]), lambda i, core: (core[0], 0))
    send = (rows // 2, 4 * width)
    return call(
        pack_kernel, "pack", 1, core.reshape(1), (w_qkv, w_proj), [mine(w_qkv), mine(w_proj)],
        struct(send, bf16), whole(send), [],
    )


def unpack_a_kernel(pos_ref, near_ref, far_ref, qkv_ref, proj_ref):
    width = proj_ref.shape[1]
    part = near_ref.shape[0]
    for which, src in ((pos_ref[2], near_ref), (1 - pos_ref[2], far_ref)):
        to = pl.ds(pl.multiple_of(which * part, 16), part)
        at = 0
        for cols in call_columns(width):
            end = at + cols.stop - cols.start
            qkv_ref[to, cols] = src[:, at:end].astype(f32)
            at = end
        proj_ref[to, :] = src[:, 3 * width : 4 * width].astype(f32)


def unpack_a(pos, near, far, w_qkv, w_proj):
    outs = [struct(w_qkv.shape, f32), struct(w_proj.shape, f32)]
    return call(
        unpack_a_kernel, "unpack_a", 1, pos, (near, far), [whole(near.shape)] * 2, outs,
        [whole(a.shape) for a in outs], [],
    )


def unpack_f_kernel(pos_ref, near_ref, far_ref, fc1_ref, fc2_ref):
    width = fc2_ref.shape[1]
    part = near_ref.shape[0] // 2
    for which, src in ((pos_ref[2], near_ref), (1 - pos_ref[2], far_ref)):
        to = pl.ds(pl.multiple_of(which * part, 16), part)
        for k in range(fc1_ref.shape[1] // width):
            for sh in range(2):
                at = k * width + sh * width // 2
                cols = sh * fc1_ref.shape[1] // 2 + k * width // 2
                fc1_ref[to, cols : cols + width // 2] = src[0:part, at : at + width // 2].astype(f32)
        for k in range(fc2_ref.shape[0] // (2 * part)):
            to = pl.ds(pl.multiple_of(k * 2 * part + which * part, 16), part)
            fc2_ref[to, :] = src[part:, k * width : (k + 1) * width].astype(f32)


def unpack_f(pos, near, far, w_fc1, w_fc2):
    outs = [struct(w_fc1.shape, f32), struct(w_fc2.shape, f32)]
    return call(
        unpack_f_kernel, "unpack_f", 1, pos, (near, far), [whole(near.shape)] * 2, outs,
        [whole(a.shape) for a in outs], [],
    )


def adam_step(weight, gradient, moment_one, moment_two, decay_here):
    moment_one_new = beta_first * moment_one + (1.0 - beta_first) * gradient
    moment_two_new = beta_second * moment_two + (1.0 - beta_second) * gradient * gradient
    first_hat = moment_one_new / (1.0 - beta_first**STEP)
    second_hat = moment_two_new / (1.0 - beta_second**STEP)
    weight_new = weight - learn_rate * (
        first_hat / (jnp.sqrt(second_hat) + adam_eps) + decay_here * weight
    )
    return (weight_new, moment_one_new, moment_two_new)


def on_device(
    tokens, cotangent, counts, w_qkv, w_proj, w_fc1, w_fc2, vectors,
    first_qkv, first_proj, first_fc1, first_fc2, first_vec,
    second_qkv, second_proj, second_fc1, second_fc2, second_vec,
):
    slots, width = tokens.shape[0], tokens.shape[3]
    by_token = lambda a: a.transpose(1, 2, 0, 3).reshape(TOK * slots, width)
    by_slot = lambda a: a.reshape(SIDE, SIDE, slots, width).transpose(2, 0, 1, 3)
    tokens, cotangent = by_token(tokens), by_token(cotangent)
    shard = lax.axis_index("shard")
    core = lax.axis_index("replica") & 1

    send_a = pack(core, w_qkv, w_proj)
    near_a = swap(send_a, "shard", 0)
    pos = jnp.stack([after(counts, send_a)[0], shard, core]).astype(jnp.int32)
    vec_low = vectors.astype(bf16)
    other_vec = swap(after(vec_low, send_a), "shard", 0)
    shuffle = shuffle_matrix()
    shuf = jnp.asarray(shuffle, bf16)
    back = jnp.asarray(shuffle.T, bf16)
    mask = jnp.asarray(mask_table())
    lanes = jnp.asarray(table_matrix(), bf16)
    place = jnp.asarray(place_matrix(), bf16)
    normed, low, own_a, own_1, own_2, send_f = enter(
        pos, after(tokens, send_a), shuf, w_qkv, w_proj, w_fc1, w_fc2
    )
    near_f = swap(send_f, "shard", 0)
    near_a = after(near_a, send_f)
    far_a = swap(near_a, "replica", 0)
    parts = (own_a, near_a, far_a)
    pair = jnp.concatenate
    vec = jnp.where(shard == 0, pair([vec_low, other_vec]), pair([other_vec, vec_low]))
    room = -vec.shape[0] % LANES + 3 * LANES
    vec = jnp.pad(vec.astype(f32), (0, room)).reshape(1, -1)

    calls = len(CALLS)
    *saved, o, att = attend(pos, normed, low, back, *parts, vec, mask, place)
    packed, prob = saved[:calls], saved[calls:]
    low, normed_b, dm, inv_b, sumc = norm(pos, tokens, att, cotangent, vec)
    far_f = swap(after(near_f, low), "replica", 0)
    act, dx1, keep_f, send_f, sumb, sumh = mlp(
        pos, low, dm, normed_b, inv_b, own_1, own_2, near_f, far_f, vec
    )
    near_w, far_w = near_f, far_f
    sum_f = Sum(keep_f, send_f, core)
    *do, grad_proj, suma = leave(pos, dx1, shuf, parts, o)
    dps, earlier = [], []
    for n in range(calls):
        sent_f = sum_f.step()
        dp, *rest = heads_back(
            pos, n, packed[n], prob[n], after(do[n], sent_f, *dps), normed, vec, lanes, parts,
            *((earlier, (grad_proj, suma, sumb, sumc, sumh)) if n == calls - 1 else ()),
        )
        dps.append(dp)
        earlier.append(rest)
    keep_a, send_a = rest
    sent_f = sum_f.step()
    sum_a = Sum(keep_a, after(send_a, sent_f), core)
    sent_a = sum_a.step()
    dh1 = project_back(pos, (after(dps[0], sent_f, sent_a), *dps[1:]), parts)

    def both(*others):
        sum_a.wait(*others)
        sent_a = sum_a.step()
        sum_f.wait(*others, sent_a)
        return sent_a, sum_f.step()

    grad_input = finish(pos, after(dh1, *both(dh1)), back, tokens, dx1, vec)
    sent = both(*both(grad_input))
    out = close(pos, after(tokens, *sent), att, act, own_2, near_w, far_w, vec)
    sent = both(out)
    while not sum_f.done:
        sent = both(*sent)
    near_f, far_f = sum_f.keep, after(sum_f.theirs, *sent)
    grad_fc1, grad_fc2 = unpack_f(pos, near_f, far_f, w_fc1, w_fc2)
    sum_a.wait(grad_fc1)
    sent_a = sum_a.step()
    step_fc1 = adam_step(w_fc1, after(grad_fc1, sent_a), first_fc1, second_fc1, decay_rate)
    sum_a.wait(*step_fc1)
    sent_a = sum_a.step()
    step_fc2 = adam_step(w_fc2, after(grad_fc2, sent_a), first_fc2, second_fc2, decay_rate)
    sum_a.wait(*step_fc2)
    while not sum_a.done:
        sum_a.step()
    near_a, far_a = sum_a.keep, sum_a.theirs
    grad_vec = near_a[:, 4 * width :].astype(f32).reshape(-1)
    grad_vec = lax.dynamic_slice_in_dim(grad_vec, shard * vectors.shape[0], vectors.shape[0], 0)
    step_vec = adam_step(vectors, grad_vec, first_vec, second_vec, 0.0)
    grad_qkv, grad_proj = unpack_a(pos, near_a, far_a, w_qkv, w_proj)
    step_qkv = adam_step(w_qkv, grad_qkv, first_qkv, second_qkv, decay_rate)
    step_proj = adam_step(w_proj, grad_proj, first_proj, second_proj, decay_rate)
    steps = [
        (grad_qkv, *step_qkv),
        (grad_proj, *step_proj),
        (grad_fc1, *step_fc1),
        (grad_fc2, *step_fc2),
        (grad_vec, *step_vec),
    ]
    return (by_slot(out), by_slot(grad_input), *(s[k] for k in range(4) for s in steps))


def solution(mesh):
    tok = P(("replica", "shard"), None, None, None)
    mat, vec = P("shard", None), P("shard")
    group = (mat, mat, mat, mat, vec)
    return jax.shard_map(
        on_device,
        mesh=mesh,
        in_specs=(tok, tok, P(("replica", "shard"))) + group * 3,
        out_specs=(tok, tok) + group * 4,
        check_vma=False,
    )
```

```python
import functools

import jax
import jax.numpy as jnp
import numpy as np
from jax import lax
from jax.experimental import pallas as pl
from jax.experimental.pallas import tpu as pltpu
from jax.sharding import PartitionSpec as P

HEADS = 16
HEAD_DIM = 32
WIN = 7
SIDE = 14
SHIFT = 3
STEP = 3
RELS = 169
TOK = SIDE * SIDE
TOK_PAD = 208
WIN_ROWS = 4 * 64
LANES = 128
GROUPS = HEADS * HEAD_DIM // LANES
PER_STEP = 2


norm_eps = 1e-05
mask_fill = -100.0
learn_rate = 0.01
beta_first = 0.9
beta_second = 0.999
adam_eps = 1e-08
decay_rate = 0.05
log2_e = 1.4426950408889634
score_scale = HEAD_DIM ** (-0.5)

CALLS = ((0, 1), (2, 3))

COSTS_US = dict(
    pack=2, fold=1, enter=10, attend=18, norm=6, mlp=28, leave=5, heads_2=11, heads_1=6, project_back=5, finish=6, close=6, unpack_a=3,
    unpack_f=4,
)

VMEM_MIB = dict(
    pack=60, enter=60, attend=60, norm=60, mlp=60, leave=24, heads_2=32, heads_1=32, project_back=24,
    finish=32, close=32, unpack_a=16, unpack_f=20,
)

IN_VMEM = {"fold", "leave", "heads_2", "heads_1", "project_back", "finish", "close", "attend", "norm", "mlp"}
SCOPED_MIB = dict(
    pack=8, fold=8, enter=24, attend=24, norm=16, mlp=28, leave=16, heads_2=16, heads_1=16,
    project_back=12, finish=20, close=16, unpack_a=8, unpack_f=8,
)

f32 = jnp.float32
bf16 = jnp.bfloat16


def nn(a, b):
    return lax.dot_general(a, b, (((1,), (0,)), ((), ())), preferred_element_type=f32)


def nt(a, b):
    return lax.dot_general(a, b, (((1,), (1,)), ((), ())), preferred_element_type=f32)


def tn(a, b):
    return lax.dot_general(a, b, (((0,), (0,)), ((), ())), preferred_element_type=f32)


def window_places():
    win, row, col = np.meshgrid(np.arange(4), np.arange(WIN), np.arange(WIN), indexing="ij")
    rolled_r = (win // 2) * WIN + row
    rolled_c = (win % 2) * WIN + col
    src = ((rolled_r + SHIFT) % SIDE) * SIDE + (rolled_c + SHIFT) % SIDE
    dst = win * 64 + row * 8 + col
    return src.reshape(-1), dst.reshape(-1), rolled_r, rolled_c


def shuffle_matrix():
    src, dst, _, _ = window_places()
    out = np.zeros((WIN_ROWS, TOK_PAD), np.float32)
    out[dst, src] = 1.0
    return out


def mask_table():
    _, _, rolled_r, rolled_c = window_places()
    band = lambda r: (r >= SIDE - WIN).astype(np.int32) + (r >= SIDE - SHIFT).astype(np.int32)
    region = (3 * band(rolled_r) + band(rolled_c)).reshape(4, WIN * WIN)
    places = (np.arange(WIN)[:, None] * 8 + np.arange(WIN)[None, :]).reshape(-1)
    out = np.full((4, 64, 64), 0.0, np.float32)
    out[:, :, :] = -1e30
    out[:, :, places] = 0.0
    block = np.where(region[:, :, None] == region[:, None, :], 0.0, mask_fill * log2_e)
    out[np.arange(4)[:, None, None], places[None, :, None], places[None, None, :]] = block
    keys_first = out.transpose(0, 2, 1).reshape(2, LANES, 64)
    return np.tile(keys_first, (1, 1, 4)).astype(np.float32)


def place_matrix():
    row, col = np.meshgrid(np.arange(WIN), np.arange(WIN), indexing="ij")
    out = np.zeros((256, 64), np.float32)
    out[(2 * WIN - 1) * row + col, row * 8 + col] = 1.0
    return out


def table_matrix():
    row, col = np.meshgrid(np.arange(WIN), np.arange(WIN), indexing="ij")
    out = np.zeros((2, 64, 256), np.float32)
    reach = 2 * WIN - 1
    out[:, row * 8 + col, (WIN - 1) * (reach + 1) - reach * row - col] = 1.0
    return out.reshape(LANES, 256)


def stats(values):
    average = jnp.mean(values, axis=-1, keepdims=True)
    centred = values - average
    variance = jnp.mean(centred * centred, axis=-1, keepdims=True)
    inv_std = lax.rsqrt(variance + norm_eps)
    return centred * inv_std, inv_std


def norm_back(grad_out, normed, inv_std, gain_row):
    scaled = grad_out * gain_row
    first_mean = jnp.mean(scaled, axis=-1, keepdims=True)
    second_mean = jnp.mean(scaled * normed, axis=-1, keepdims=True)
    return inv_std * (scaled - first_mean - normed * second_mean)


def get_slot(sheet, slot, slots):
    rows = pl.ds(slot, TOK_PAD, stride=slots)
    return jnp.concatenate([sheet[g, rows, :] for g in range(GROUPS)], axis=1)


def put_slot(sheet, slot, slots, values):
    rows = pl.ds(slot, TOK_PAD, stride=slots)
    for g in range(GROUPS):
        sheet[g, rows, :] = values[:, g * LANES : (g + 1) * LANES]


def get_sheet(sheet, rows):
    return jnp.concatenate([sheet[g, 0:rows, :] for g in range(GROUPS)], axis=1)


def put_sheet(sheet, here, values):
    for g in range(GROUPS):
        sheet[g, here, :] = values[:, g * LANES : (g + 1) * LANES]


def pair_up(rows, diag):
    return jnp.concatenate([rows, rows], axis=1) * diag


def stack_heads(rows, head_masks):
    wide = jnp.concatenate([rows[0:64], rows[64:128]], axis=1)
    return jnp.concatenate([wide * m for m in head_masks], axis=0)


def merge_heads(stacked, lane_head):
    out = stacked[192:256]
    for h in (2, 1, 0):
        out = jnp.where(lane_head == h, stacked[64 * h : 64 * h + 64], out)
    return out


def over_keys(values):
    sums = [
        jnp.broadcast_to(jnp.sum(values[w : w + 64], axis=0, keepdims=True), (64, values.shape[1]))
        for w in (0, 64)
    ]
    return jnp.concatenate(sums, axis=0)


def block_masks():
    lane = lax.broadcasted_iota(jnp.int32, (1, 2 * LANES), 1)
    lane_head = (lane % LANES) // HEAD_DIM
    head_masks = [(lane_head == h).astype(f32).astype(bf16) for h in range(4)]
    row = lax.broadcasted_iota(jnp.int32, (LANES, 2 * LANES), 0)
    col = lax.broadcasted_iota(jnp.int32, (LANES, 2 * LANES), 1)
    diag = ((row // 64) == (col // LANES)).astype(f32).astype(bf16)
    lane_head64 = jnp.broadcast_to(lane_head, (64, 2 * LANES))
    return lane_head64, head_masks, diag


def join_rows(pos_ref, full, own_ref, near_ref, far_ref):
    half = own_ref.shape[0]
    shard, core = pos_ref[1], pos_ref[2]
    other = (1 - shard) * half
    part = half // 2
    full[pl.ds(pl.multiple_of(shard * half, 16), half), :] = own_ref[...]
    full[pl.ds(pl.multiple_of(other + core * part, 16), part), :] = near_ref[...]
    full[pl.ds(pl.multiple_of(other + (1 - core) * part, 16), part), :] = far_ref[...]


def vec_part(vec_ref, n, width):
    return vec_ref[0:1, n * width : (n + 1) * width]


def enter_kernel(
    pos_ref, tok_ref, shuf_ref, qkv_ref, proj_ref, fc1_ref, fc2_ref, part1_ref, part2_ref,
    high_ref, low_ref, own_ref, own1_ref, own2_ref, send_ref, sheet,
):
    step = this_step()
    rows, width = tok_ref.shape
    slots = rows // TOK

    @pl.when(step == 0)
    def _():
        normed, _ = stats(tok_ref[...].astype(f32))
        put_sheet(sheet, slice(0, rows), normed)
        sheet[:, rows:, :] = jnp.zeros((GROUPS, sheet.shape[1] - rows, LANES), f32)

    for i in range(PER_STEP):
        at = slice(i * WIN_ROWS, (i + 1) * WIN_ROWS)
        normed = get_slot(sheet, step * PER_STEP + i, slots)
        high = normed.astype(bf16)
        low = (normed - high.astype(f32)).astype(bf16)
        high_ref[at, :] = nn(shuf_ref[...], high).astype(bf16)
        low_ref[at, :] = nn(shuf_ref[...], low).astype(bf16)
    pack_columns(own_ref, qkv_ref, proj_ref)
    own1_ref[...] = fc1_ref[...].astype(bf16)
    own2_ref[...] = fc2_ref[...].astype(bf16)
    steps = send_ref.shape[1] // width
    part = part1_ref.shape[0]
    send_ref[pl.ds(pl.multiple_of(step * part, 16), part), :] = part1_ref[...].astype(bf16)
    for k in range(steps):
        @pl.when(step == k)
        def _():
            send_ref[steps * part :, k * width : (k + 1) * width] = part2_ref[...].astype(bf16)


def score_bias(vec_ref, mask_ref, place_ref, bias):
    width = GROUPS * LANES
    table_at = 12 * width
    reach = 2 * WIN - 1
    for g in range(GROUPS):
        blocks = []
        for h in range(4):
            at = table_at + (4 * g + h) * RELS
            shift = at % LANES
            entries = vec_ref[0:1, at - shift : at - shift + 3 * LANES]
            if shift:
                entries = pltpu.roll(entries, 3 * LANES - shift, 1)
            entries = jnp.broadcast_to(entries[:, 0:256], (8, 256))
            entries = pltpu.roll(entries, 0, 1, stride=1, stride_axis=0)
            for r in range(WIN):
                turn = 256 - (WIN - 1) * (reach + 1) + reach * r
                blocks.append(pltpu.roll(entries, turn, 1))
            blocks.append(jnp.zeros((8, 256), f32))
        spread = nn(jnp.concatenate(blocks, axis=0).astype(bf16), place_ref[...]) * log2_e
        rel = jnp.concatenate([spread[64 * h : 64 * h + 64] for h in range(4)], axis=1)
        for kind in range(2):
            for w in (0, 64):
                bias[kind * GROUPS + g, w : w + 64, :] = rel + mask_ref[kind, w : w + 64, :]


def attend_kernel(
    pos_ref, high_ref, low_ref, back_ref, own_ref, near_ref, far_ref, vec_ref, mask_ref, place_ref,
    *refs,
):
    packed_refs, prob_refs = refs[: len(CALLS)], refs[len(CALLS) : 2 * len(CALLS)]
    o_ref, att_ref, w_ref, sheet, bias_ref = refs[2 * len(CALLS) :]
    step = this_step()
    rows, width = att_ref.shape
    slots = rows // TOK

    @pl.when(step == 0)
    def _():
        join_rows(pos_ref, w_ref, own_ref, near_ref, far_ref)
        score_bias(vec_ref, mask_ref, place_ref, bias_ref)

    normed = high_ref[...].astype(f32) + low_ref[...].astype(f32)
    low = (normed * (1.0 + vec_part(vec_ref, 0, width)) + vec_part(vec_ref, 1, width)).astype(bf16)
    none = jnp.zeros((1, width), f32)
    biases = (vec_part(vec_ref, 2, width), none, vec_part(vec_ref, 3, width))
    at = 0
    for groups, packed_ref in zip(CALLS, packed_refs):
        cols = slice(at, at + packed_ref.shape[1])
        here = slice(groups[0] * LANES, (groups[-1] + 1) * LANES)
        added = jnp.concatenate([b[:, here] for b in biases], axis=1)
        packed_ref[...] = (nn(low, w_ref[:, cols]) + added).astype(bf16)
        at = cols.stop

    lane_head, head_masks, diag = block_masks()
    units = [(i, n, len(groups)) for i, groups in enumerate(CALLS) for n in range(len(groups))]
    for pair in range(2 * PER_STEP):
        pick = slice(pair * LANES, (pair + 1) * LANES)
        take = lambda u, j: packed_refs[u[0]][
            pick, (j * u[2] + u[1]) * LANES : (j * u[2] + u[1] + 1) * LANES
        ]
        q = [stack_heads(take(u, 0), head_masks) for u in units]
        k = [pair_up(take(u, 1), diag) for u in units]
        s = [nt(a, b) for a, b in zip(k, q)]
        e = [
            jnp.exp2(s[g] * (score_scale * log2_e) + bias_ref[(pair % 2) * GROUPS + g])
            for g in range(GROUPS)
        ]
        p = [(a * (1.0 / over_keys(a))).astype(bf16) for a in e]
        for g, (i, n, count) in enumerate(units):
            prob_refs[i][pair * count + n] = p[g]
        v = [pair_up(take(u, 2), diag) for u in units]
        for g in range(GROUPS):
            o = merge_heads(tn(p[g], v[g]), lane_head).astype(bf16)
            cols = slice(g * LANES, (g + 1) * LANES)
            o_ref[pair * LANES : pair * LANES + 64, cols] = o[:, 0:LANES]
            o_ref[pair * LANES + 64 : (pair + 1) * LANES, cols] = o[:, LANES:]

    branch = (nn(o_ref[...], w_ref[:, 3 * width :]) + vec_part(vec_ref, 4, width)).astype(bf16)
    for i in range(PER_STEP):
        att = nn(back_ref[...], branch[i * WIN_ROWS : (i + 1) * WIN_ROWS])
        put_slot(sheet, step * PER_STEP + i, slots, att)

    @pl.when(step == all_steps() - 1)
    def _():
        att_ref[...] = get_sheet(sheet, rows).astype(bf16)


def join_fc2(pos_ref, full, own_ref, near_ref, far_ref):
    half = own_ref.shape[0]
    shard, core = pos_ref[1], pos_ref[2]
    part = near_ref.shape[0] // 2
    width = full.shape[1]
    for k in range(half // (2 * part)):
        at = k * 4 * part + shard * 2 * part
        full[pl.ds(pl.multiple_of(at, 16), 2 * part), :] = own_ref[
            k * 2 * part : (k + 1) * 2 * part, :
        ]
        for which, src in ((core, near_ref), (1 - core, far_ref)):
            at = k * 4 * part + (1 - shard) * 2 * part + which * part
            full[pl.ds(pl.multiple_of(at, 16), part), :] = src[
                part:, k * width : (k + 1) * width
            ]


def block_place(core, shard, block):
    return jnp.where(core == 0, 2 * shard + block, 2 * block + shard)


def norm_kernel(
    pos_ref, tok_ref, att_ref, cot_ref, vec_ref, low_ref, norm_ref, dm_ref, inv_ref, sum_ref
):
    rows, width = tok_ref.shape
    slots = rows * all_steps() // TOK

    @pl.when(this_step() == 0)
    def _():
        sum_ref[...] = jnp.zeros_like(sum_ref)

    normed, inv_std = stats(tok_ref[...].astype(f32) + att_ref[...].astype(f32))
    gain, shift = vec_part(vec_ref, 5, width), vec_part(vec_ref, 6, width)
    low_ref[...] = (normed * (1.0 + gain) + shift).astype(bf16)
    norm_ref[...] = normed.astype(bf16)
    inv_ref[...] = jnp.broadcast_to(inv_std, inv_ref.shape)
    slot = lax.broadcasted_iota(jnp.int32, (rows, 1), 0) % slots
    dm = cot_ref[...].astype(f32) * (slot < pos_ref[0]).astype(f32)
    dm_ref[...] = dm.astype(bf16)
    sum_ref[0:1, :] += jnp.sum(dm, axis=0, keepdims=True)


def mlp_kernel(
    pos_ref, low_s, dm_s, norm_s, inv_s,
    own1a_ref, near1a_ref, far1a_ref, own1b_ref, near1b_ref, far1b_ref,
    own2_ref, near2_ref, far2_ref, vec_ref, b1a_ref, b1b_ref,
    act_ref, dx1_ref, keep_ref, send_ref, sum_ref, sumb_ref,
    w1_ref, w2_ref, dhid, dh_s,
):
    step = this_step()
    rows, width = low_s.shape
    core = pos_ref[2]
    part = width // 4
    @pl.when(step == 0)
    def _():
        sum_ref[...] = jnp.zeros_like(sum_ref)
        dh_s[...] = jnp.zeros_like(dh_s)

    join_rows(pos_ref, w1_ref.at[:, 0 : 2 * part], own1a_ref, near1a_ref, far1a_ref)
    join_rows(pos_ref, w1_ref.at[:, 2 * part :], own1b_ref, near1b_ref, far1b_ref)
    join_rows(pos_ref, w2_ref, own2_ref, near2_ref, far2_ref)
    b1 = jnp.concatenate([b1a_ref[0:1, :], b1b_ref[0:1, :]], axis=1)
    total = jnp.zeros((1, 4 * part), f32)
    pieces = 2
    for n in range(pieces):
        at = slice(n * rows // pieces, (n + 1) * rows // pieces)
        u = nn(low_s[at, :], w1_ref[...]) + b1
        bell = jnp.exp2(u * u * (-0.5 * log2_e))
        cdf = 0.5 + 0.5 * lax.erf(u * 0.7071067811865476)
        act_ref[at, :] = (u * cdf).astype(bf16)
        dg = nt(dm_s[at, :], w2_ref[...])
        du = (dg * (cdf + u * (bell * 0.3989422804014327))).astype(bf16)
        dhid[at, :] = du
        total += jnp.sum(du.astype(f32), axis=0, keepdims=True)
        dh_s[at, :] += nt(du, w1_ref[...])
    sumb_ref[0:1, :] = total
    grads = tn(low_s[...], dhid[...]), tn(act_ref[...], dm_s[...])
    for sh in range(2):
        for block, grad in enumerate(grads):
            first = grad[sh * 2 * part : sh * 2 * part + part]
            second = grad[sh * 2 * part + part : (sh + 1) * 2 * part]
            for which, dst in ((core, keep_ref), (1 - core, send_ref)):
                to = pl.ds(pl.multiple_of(block_place(which, sh, block) * part, 16), part)
                dst[to, :] = jnp.where(which == 0, first, second).astype(bf16)

    @pl.when(step == all_steps() - 1)
    def _():
        dh2, normed = dh_s[...], norm_s[...].astype(f32)
        inv_std = jnp.concatenate([inv_s[...]] * GROUPS, axis=1)
        grad = norm_back(dh2, normed, inv_std, 1.0 + vec_part(vec_ref, 5, width))
        dx1_ref[...] = (dm_s[...].astype(f32) + grad).astype(bf16)
        sum_ref[0:1, :] = jnp.sum(dh2 * normed, axis=0, keepdims=True)
        sum_ref[1:2, :] = jnp.sum(dh2, axis=0, keepdims=True)


def close_kernel(
    pos_ref, tok_ref, att_ref, act_ref, own_ref, near_ref, far_ref, vec_ref, out_ref, w_ref
):
    step = this_step()
    rows = tok_ref.shape[0]
    slots = rows * all_steps() // TOK

    @pl.when(step == 0)
    def _():
        join_fc2(pos_ref, w_ref, own_ref, near_ref, far_ref)

    slot = lax.broadcasted_iota(jnp.int32, (rows, 1), 0) % slots
    alive = (slot < pos_ref[0]).astype(f32)
    x1 = tok_ref[...].astype(f32) + att_ref[...].astype(f32)
    out = alive * (x1 + nn(act_ref[...], w_ref[...]) + vec_part(vec_ref, 7, out_ref.shape[1]))
    out_ref[...] = out.astype(bf16)


def fold_table(ds_ref, lanes_ref, flat, first_head):
    flat[...] = jnp.zeros_like(flat)
    for g in range(ds_ref.shape[0]):
        whole_g = ds_ref[g].T
        high = whole_g.astype(bf16)
        low = (whole_g - high.astype(f32)).astype(bf16)
        spread = nn(high, lanes_ref[...]) + nn(low, lanes_ref[...])
        for h in range(4):
            total = jnp.zeros((8, 256), f32)
            for r in range(WIN):
                at = 64 * h + 8 * r
                total += pltpu.roll(spread[at : at + 8], (2 * WIN - 1) * r, 1)
            total = pltpu.roll(total, 0, 1, stride=1, stride_axis=0)
            entries = jnp.sum(total, axis=0, keepdims=True)
            entries = jnp.concatenate([entries, jnp.zeros((1, LANES), f32)], axis=1)
            first, shift = divmod((first_head + 4 * g + h) * RELS, LANES)
            if shift:
                entries = pltpu.roll(entries, shift, 1)
            for k in range(3):
                flat[first + k : first + k + 1, :] += entries[:, k * LANES : (k + 1) * LANES]


def leave_kernel(
    pos_ref, dx1_ref, shuf_ref, own_ref, near_ref, far_ref, o_ref,
    *refs,
):
    do_refs = refs[: len(CALLS)]
    gp_ref, sum_ref, w_ref, sheet = refs[len(CALLS) :]
    step = this_step()
    rows, width = dx1_ref.shape
    slots = rows // TOK

    @pl.when(step == 0)
    def _():
        join_rows(pos_ref, w_ref, own_ref, near_ref, far_ref)
        put_sheet(sheet, slice(0, rows), dx1_ref[...].astype(f32))
        sheet[:, rows:, :] = jnp.zeros((GROUPS, sheet.shape[1] - rows, LANES), f32)
        gp_ref[...] = jnp.zeros_like(gp_ref)
        sum_ref[...] = jnp.zeros_like(sum_ref)

    da = []
    for i in range(PER_STEP):
        low = get_slot(sheet, step * PER_STEP + i, slots).astype(bf16)
        da.append(nn(shuf_ref[...], low))
    da = jnp.concatenate(da, axis=0)
    sum_ref[0:1, :] += jnp.sum(da, axis=0, keepdims=True)
    da = da.astype(bf16)
    do = nt(da, w_ref[...]).astype(bf16)
    for groups, do_ref in zip(CALLS, do_refs):
        do_ref[...] = do[:, groups[0] * LANES : (groups[-1] + 1) * LANES]
    gp_ref[...] += tn(o_ref[...], da)


def heads_kernel(*refs, groups, earlier_calls):
    (pos_ref, packed_ref, prob_ref, do_ref, normed_ref, vec_ref, lanes_ref,
     own_ref, near_ref, far_ref) = refs[:10]
    refs = refs[10:]
    last = earlier_calls > 0
    if last:
        g_refs, sum_refs, flat_refs = (
            refs[n * earlier_calls : (n + 1) * earlier_calls] for n in range(3)
        )
        (gp_ref, suma_ref, sumb_ref, sumc_ref, sumh_ref, dp_ref, keep_ref, send_ref,
         w_ref, acc, ds_ref, flat, sum_ref) = refs[3 * earlier_calls :]
    else:
        dp_ref, g_ref, sum_ref, flat, w_ref, acc, ds_ref = refs
    step = this_step()
    width, span = acc.shape
    third = span // 3

    @pl.when(step == 0)
    def _():
        join_rows(pos_ref, w_ref, own_ref, near_ref, far_ref)
        acc[...] = jnp.zeros_like(acc)
        ds_ref[...] = jnp.zeros_like(ds_ref)
        sum_ref[...] = jnp.zeros_like(sum_ref)

    lane_head, head_masks, diag = block_masks()
    for pair in range(2 * PER_STEP):
        pick = slice(pair * LANES, (pair + 1) * LANES)
        low_rows = slice(pair * LANES, pair * LANES + 64)
        high_rows = slice(pair * LANES + 64, (pair + 1) * LANES)
        every = range(len(groups))
        count = len(groups)
        at = [slice(g * LANES, (g + 1) * LANES) for g in range(3 * count)]
        do = [stack_heads(do_ref[pick, at[g]], head_masks) for g in every]
        v = [pair_up(packed_ref[pick, at[2 * count + g]], diag) for g in every]
        p = [prob_ref[pair * count + g] for g in every]
        dp = [nt(v[g], do[g]) for g in every]
        pf = [p[g].astype(f32) for g in every]
        delta = [over_keys(pf[g] * dp[g]) for g in every]
        dv = [nn(p[g], do[g]).astype(bf16) for g in every]
        ds = [pf[g] * (dp[g] - delta[g]) for g in every]
        for g in every:
            ds_ref[g] += ds[g]
        ds = [ds[g].astype(bf16) for g in every]
        k = [pair_up(packed_ref[pick, at[count + g]], diag) for g in every]
        q = [stack_heads(packed_ref[pick, at[g]], head_masks) for g in every]
        dk = [(nn(ds[g], q[g]) * score_scale).astype(bf16) for g in every]
        dq = [(merge_heads(tn(ds[g], k[g]), lane_head) * score_scale).astype(bf16) for g in every]
        for g in every:
            dp_ref[low_rows, at[g]] = dq[g][:, 0:LANES]
            dp_ref[high_rows, at[g]] = dq[g][:, LANES:]
            dp_ref[low_rows, at[count + g]] = dk[g][0:64, 0:LANES]
            dp_ref[high_rows, at[count + g]] = dk[g][64:, LANES:]
            dp_ref[low_rows, at[2 * count + g]] = dv[g][0:64, 0:LANES]
            dp_ref[high_rows, at[2 * count + g]] = dv[g][64:, LANES:]
    acc[...] += tn(normed_ref[...], dp_ref[...])
    sum_ref[0:1, 0:span] += jnp.sum(dp_ref[...].astype(f32), axis=0, keepdims=True)

    @pl.when(step == all_steps() - 1)
    def _():
        weights = w_ref[...]
        sums = sum_ref[0:1, 0:span]
        ones = jnp.ones((8, span), bf16)
        high = sums.astype(bf16)
        low = (sums - high.astype(f32)).astype(bf16)
        both = jnp.concatenate([high, low, jnp.zeros((6, span), bf16)], axis=0)
        shift_grad = jnp.sum(nt(both, weights), axis=0, keepdims=True)
        product = weights.astype(f32) * acc[...]
        high = product.astype(bf16)
        low = (product - high.astype(f32)).astype(bf16)
        gain_grad = (nt(ones, high) + nt(ones, low))[0:1]
        gain = (1.0 + vec_part(vec_ref, 0, width)).reshape(width, 1)
        shift = vec_part(vec_ref, 1, width).reshape(width, 1)
        grads = gain * acc[...] + shift * sums
        fold_table(ds_ref, lanes_ref, flat, 4 * groups[0])
        if not last:
            g_ref[...] = grads.astype(bf16)
            sum_ref[1:2, 0:width] = gain_grad
            sum_ref[2:3, 0:width] = shift_grad
            return
        acc[...] = grads
        core = pos_ref[2]
        part = width // 8
        per = width // LANES
        all_sums = [r[0:1, 0 : 3 * len(c) * LANES] for r, c in zip(sum_refs, CALLS)] + [sums]
        thirds = lambda n: jnp.concatenate(
            [a[:, n * a.shape[1] // 3 : (n + 1) * a.shape[1] // 3] for a in all_sums], axis=1
        )
        rows_of = [
            sum([r[1:2, 0:width] for r in sum_refs], gain_grad),
            sum([r[2:3, 0:width] for r in sum_refs], shift_grad),
            thirds(0),
            thirds(2),
            suma_ref[0:1, :],
        ]
        rows_of += [sumb_ref[0:1, :], sumb_ref[1:2, :], sumc_ref[0:1, :]]
        pieces = [v[:, k * LANES : (k + 1) * LANES] for v in rows_of for k in range(per)]
        mine = 2 * part
        blocks = sumh_ref.shape[1] // (4 * mine)
        for sh in range(2):
            for k in range(blocks):
                at = k * 4 * mine + sh * 2 * mine
                pieces += [sumh_ref[0:1, at : at + mine], sumh_ref[0:1, at + mine : at + 2 * mine]]
        block = jnp.concatenate(pieces + [sum([r[...] for r in flat_refs], flat[...])], axis=0)
        block = jnp.concatenate(
            [block, jnp.zeros((2 * part - block.shape[0], LANES), f32)], axis=0
        ).astype(bf16)
        for which, dst in ((core, keep_ref), (1 - core, send_ref)):
            for sh in range(2):
                for half in range(2):
                    src = sh * 4 * part + which * 2 * part + half * part
                    src = pl.ds(pl.multiple_of(src, 16), part)
                    to = pl.ds(pl.multiple_of(block_place(which, sh, half) * part, 16), part)
                    at = 0
                    for part_ref in (*g_refs, acc, gp_ref):
                        cols = slice(at, at + part_ref.shape[1])
                        dst[to, cols] = part_ref[src, :].astype(bf16)
                        at = cols.stop
                    dst[to, at:] = block[half * part : (half + 1) * part]


def project_back_kernel(pos_ref, *refs):
    dp_refs = refs[: len(CALLS)]
    own_ref, near_ref, far_ref, dh_ref, w_ref = refs[len(CALLS) :]

    @pl.when(this_step() == 0)
    def _():
        join_rows(pos_ref, w_ref, own_ref, near_ref, far_ref)

    dp = jnp.concatenate([r[...] for r in dp_refs], axis=1)
    dh_ref[...] = nt(dp, w_ref[...]).astype(bf16)


def finish_kernel(pos_ref, dh_ref, back_ref, tok_ref, dx1_ref, vec_ref, gi_ref, sheet):
    step = this_step()
    rows, width = tok_ref.shape
    slots = rows // TOK
    for i in range(PER_STEP):
        dh = nn(back_ref[...], dh_ref[i * WIN_ROWS : (i + 1) * WIN_ROWS, :])
        put_slot(sheet, step * PER_STEP + i, slots, dh)

    @pl.when(step == all_steps() - 1)
    def _():
        normed, inv_std = stats(tok_ref[...].astype(f32))
        grad = norm_back(get_sheet(sheet, rows), normed, inv_std, 1.0 + vec_part(vec_ref, 0, width))
        gi_ref[...] = (dx1_ref[...].astype(f32) + grad).astype(bf16)


def whole(shape):
    return pl.BlockSpec(shape, lambda i, *_: (0,) * len(shape))


def by_rows(rows, cols):
    return pl.BlockSpec((rows, cols), lambda i, *_: (i, 0))


def struct(shape, dtype):
    return jax.ShapeDtypeStruct(shape, dtype)


def params(name):
    return pltpu.CompilerParams(
        dimension_semantics=("arbitrary",), vmem_limit_bytes=VMEM_MIB[name] << 20
    )


LOOP = []


def this_step():
    return LOOP[-1][0] if LOOP else pl.program_id(0)


def all_steps():
    return LOOP[-1][1] if LOOP else pl.num_programs(0)


def block_of(ref, spec, step, pos_ref):
    if spec.block_shape is None or tuple(spec.block_shape) == tuple(ref.shape):
        return ref
    cuts = []
    for at, size, full in zip(spec.index_map(step, pos_ref), spec.block_shape, ref.shape):
        if size == full:
            cuts.append(slice(None))
        elif isinstance(at, int):
            cuts.append(slice(at * size, (at + 1) * size))
        else:
            cuts.append(pl.ds(pl.multiple_of(at * size, size), size))
    return ref.at[tuple(cuts)]


def call(kernel, name, steps, pos, ops, in_specs, outs, out_specs, scratch):
    cost = pl.CostEstimate(
        flops=COSTS_US[name] * 1_000_000_000, bytes_accessed=0, transcendentals=0
    )
    if name not in IN_VMEM:
        return pl.pallas_call(
            kernel,
            grid_spec=pltpu.PrefetchScalarGridSpec(
                num_scalar_prefetch=1,
                grid=(steps,),
                in_specs=in_specs,
                out_specs=out_specs,
                scratch_shapes=scratch,
            ),
            out_shape=outs,
            compiler_params=params(name),
            cost_estimate=cost,
            name=name,
        )(pos, *ops)

    several = isinstance(outs, (list, tuple))
    specs = [*in_specs, *(out_specs if several else [out_specs])]

    def loop(pos_ref, *refs):
        def one(step, carry):
            LOOP.append((step, steps))
            blocks = [block_of(r, s, step, pos_ref) for r, s in zip(refs, specs)]
            kernel(pos_ref, *blocks, *refs[len(specs) :])
            LOOP.pop()
            return carry

        if steps == 1:
            one(jnp.int32(0), 0)
        else:
            lax.fori_loop(0, steps, one, 0)

    here = pl.BlockSpec(memory_space=pltpu.VMEM)
    return pl.pallas_call(
        loop,
        in_specs=[pl.BlockSpec(memory_space=pltpu.SMEM)] + [here] * len(ops),
        out_specs=[here] * len(outs) if several else here,
        out_shape=outs,
        scratch_shapes=scratch,
        compiler_params=pltpu.CompilerParams(vmem_limit_bytes=SCOPED_MIB[name] << 20),
        cost_estimate=cost,
        name=name,
    )(pos, *ops)


def by_units(units):
    return pl.BlockSpec((units, LANES, 256), lambda i, *_: (i, 0, 0))


def columns(rows, cols, block):
    return pl.BlockSpec((rows, cols), lambda i, *_: (0, block))


def sheet_of(slots):
    return pltpu.VMEM((GROUPS, slots * TOK_PAD, LANES), f32)


def enter(pos, tokens, shuf, w_qkv, w_proj, w_fc1, w_fc2):
    rows, width = tokens.shape
    slots = rows // TOK
    steps = slots // PER_STEP
    wr = PER_STEP * WIN_ROWS
    hidden = w_fc1.shape[1]
    weights = (w_qkv, w_proj, w_fc1, w_fc2)
    blocks = [(a.shape[0] // steps, a.shape[1]) for a in weights]
    parts = [(w_fc1.shape[0] // 2 // steps, hidden), (w_fc2.shape[0] // 2 // steps, width)]
    win = struct((slots * WIN_ROWS, width), bf16)
    own, send = (w_qkv.shape[0], 4 * width), (width // 2, hidden)
    return call(
        enter_kernel, "enter", steps, pos, (tokens, shuf, *weights, w_fc1, w_fc2),
        [whole(tokens.shape), whole(shuf.shape)]
        + [by_rows(*block) for block in blocks]
        + [
            pl.BlockSpec(parts[0], lambda i, pos: (pos[2] * steps + i, 0)),
            pl.BlockSpec(parts[1], lambda i, pos: (2 * i + pos[2], 0)),
        ],
        [win, win]
        + [struct(a, bf16) for a in (own, w_fc1.shape, w_fc2.shape, send)],
        [by_rows(wr, width)] * 2
        + [by_rows(own[0] // steps, own[1]), by_rows(*blocks[2]), by_rows(*blocks[3]), whole(send)],
        [sheet_of(slots)],
    )


def attend(pos, high, low, *rest):
    rows, width = high.shape
    slots = rows // WIN_ROWS
    steps = slots // PER_STEP
    wr = PER_STEP * WIN_ROWS
    spans = [3 * len(groups) * LANES for groups in CALLS]
    units = [2 * PER_STEP * len(groups) for groups in CALLS]
    return call(
        attend_kernel, "attend", steps, pos, (high, low, *rest),
        [by_rows(wr, width)] * 2 + [whole(a.shape) for a in rest],
        [struct((rows, span), bf16) for span in spans]
        + [struct((steps * n, LANES, 256), bf16) for n in units]
        + [struct((rows, width), bf16), struct((slots * TOK, width), bf16)],
        [by_rows(wr, span) for span in spans]
        + [by_units(n) for n in units]
        + [by_rows(wr, width), whole((slots * TOK, width))],
        [
            pltpu.VMEM((width, 4 * width), bf16),
            sheet_of(slots),
            pltpu.VMEM((2 * GROUPS, LANES, 256), f32),
        ],
    )


def norm(pos, tokens, att, cot, vec):
    rows, width = cot.shape
    steps = 2
    part = rows // steps
    low = struct(cot.shape, bf16)
    return call(
        norm_kernel, "norm", steps, pos, (tokens, att, cot, vec),
        [by_rows(part, width)] * 3 + [whole(vec.shape)],
        [low, low, low, struct((rows, LANES), f32), struct((8, width), f32)],
        [by_rows(part, width)] * 3 + [by_rows(part, LANES), whole((8, width))], [],
    )


def mlp(pos, low, dm, normed, inv, own1, own2, near, far, vec):
    rows, width = low.shape
    hidden = own1.shape[1]
    half = width // 2
    steps = hidden // width
    part = width // 4
    at = lambda rows, cols, row, col: pl.BlockSpec((rows, cols), lambda i, *_: (row, col + i))
    by_columns = lambda rows, cols: pl.BlockSpec((rows, cols), lambda i, *_: (0, i))
    first_b1 = 8 * width // half
    return call(
        mlp_kernel, "mlp", steps, pos,
        (low, dm, normed, inv, own1, near, far, own1, near, far, own2, near, far, vec, vec, vec),
        [whole(low.shape)] * 2
        + [pl.BlockSpec(memory_space=pl.ANY)] * 2
        + [at(half, half, 0, 0), at(part, half, 0, 0), at(part, half, 0, 0)]
        + [at(half, half, 0, steps), at(part, half, 0, steps), at(part, half, 0, steps)]
        + [by_rows(half, width), at(part, width, 1, 0), at(part, width, 1, 0)]
        + [whole(vec.shape), at(1, half, 0, first_b1), at(1, half, 0, first_b1 + steps)],
        [
            struct((rows, hidden), bf16),
            struct(low.shape, bf16),
            struct((width, hidden), bf16),
            struct((width, hidden), bf16),
            struct((8, width), f32),
            struct((8, hidden), f32),
        ],
        [
            by_columns(rows, width),
            whole(low.shape),
            by_columns(width, width),
            by_columns(width, width),
            whole((8, width)),
            by_columns(8, width),
        ],
        [
            pltpu.VMEM((width, width), bf16),
            pltpu.VMEM((width, width), bf16),
            pltpu.VMEM((rows, width), bf16),
            pltpu.VMEM((rows, width), f32),
        ],
    )


def close(pos, tokens, att, act, own, near, far, vec):
    rows, width = tokens.shape
    hidden = act.shape[1]
    steps = 2
    part = rows // steps
    fixed = (own, near, far, vec)
    return call(
        close_kernel, "close", steps, pos, (tokens, att, act, *fixed),
        [by_rows(part, width)] * 2 + [by_rows(part, hidden)] + [whole(a.shape) for a in fixed],
        struct(tokens.shape, bf16), by_rows(part, width),
        [pltpu.VMEM((hidden, width), bf16)],
    )


def leave(pos, dx1, shuf, parts, o):
    rows, width = dx1.shape
    slots = rows // TOK
    wr = PER_STEP * WIN_ROWS
    cols = [len(groups) * LANES for groups in CALLS]
    return call(
        leave_kernel, "leave", slots // PER_STEP, pos, (dx1, shuf, *parts, o),
        [whole(dx1.shape), whole(shuf.shape)]
        + [columns(a.shape[0], width, 3) for a in parts]
        + [by_rows(wr, width)],
        [struct((slots * WIN_ROWS, c), bf16) for c in cols]
        + [struct((width, width), f32), struct((8, width), f32)],
        [by_rows(wr, c) for c in cols] + [whole((width, width)), whole((8, width))],
        [pltpu.VMEM((width, width), bf16), sheet_of(slots)],
    )


def heads_back(pos, which, packed, prob, do, normed, vec, lanes, parts, earlier=(), others=()):
    rows, span = packed.shape
    width = normed.shape[1]
    steps = rows // (PER_STEP * WIN_ROWS)
    wr = PER_STEP * WIN_ROWS
    units = prob.shape[0] // steps
    groups = CALLS[which]
    dp = struct((rows, span), bf16)
    scratch = [
        pltpu.VMEM((width, span), bf16),
        pltpu.VMEM((width, span), f32),
        pltpu.VMEM((len(groups), LANES, 256), f32),
    ]
    small, flat = (8, 3 * width), (24, LANES)
    if earlier:
        shape = (width // 2, 4 * width + LANES)
        outs, specs = [struct(shape, bf16)] * 2, [whole(shape)] * 2
        scratch += [pltpu.VMEM(flat, f32), pltpu.VMEM(small, f32)]
        earlier = [a[n] for n in range(3) for a in earlier]
    else:
        outs = [struct((width, span), bf16), struct(small, f32), struct(flat, f32)]
        specs = [whole(o.shape) for o in outs]
    extra = (*earlier, *others)
    at = 3 * groups[0] * LANES
    return call(
        functools.partial(heads_kernel, groups=groups, earlier_calls=len(earlier) // 3),
        "heads_%d" % len(groups), steps, pos,
        (packed, prob, do, normed, vec, lanes, *parts, *extra),
        [
            by_rows(wr, span), by_units(units), by_rows(wr, do.shape[1]), by_rows(wr, width),
            whole(vec.shape), whole(lanes.shape),
        ]
        + [columns(a.shape[0], span, at // span) for a in parts]
        + [whole(a.shape) for a in extra],
        [dp, *outs], [by_rows(wr, span), *specs], scratch,
    )


def project_back(pos, dps, parts):
    rows = dps[0].shape[0]
    width = parts[0].shape[1] // 4
    wr = PER_STEP * WIN_ROWS
    return call(
        project_back_kernel, "project_back", rows // wr, pos, (*dps, *parts),
        [by_rows(wr, a.shape[1]) for a in dps]
        + [columns(a.shape[0], 3 * width, 0) for a in parts],
        struct((rows, width), bf16), by_rows(wr, width),
        [pltpu.VMEM((width, 3 * width), bf16)],
    )


def finish(pos, dh, back, tokens, dx1, vec):
    rows, width = tokens.shape
    slots = rows // TOK
    wr = PER_STEP * WIN_ROWS
    fixed = (back, tokens, dx1, vec)
    return call(
        finish_kernel, "finish", slots // PER_STEP, pos, (dh, *fixed),
        [by_rows(wr, width)] + [whole(a.shape) for a in fixed],
        struct(tokens.shape, bf16), whole(tokens.shape), [sheet_of(slots)],
    )


def swap(values, axis, bit):
    count = lax.axis_size(axis)
    return lax.ppermute(values, axis, [(i, i ^ (1 << bit)) for i in range(count)])


SHARD_BIT = 0


def orders():
    top = (lax.axis_size("replica") * lax.axis_size("shard")).bit_length() - 1
    rest = tuple(range(4, top))
    return (SHARD_BIT, 2, 3, *rest), (3, SHARD_BIT, 2, *rest)


def swap_by_core(values, bits):
    count = lax.axis_size("replica") * lax.axis_size("shard")
    perm = [(i, i ^ (1 << bits[(i >> 1) & 1])) for i in range(count)]
    return lax.ppermute(values, ("replica", "shard"), perm)


def my_bits(bits, core, index):
    return (index >> jnp.where(core == 0, bits[0], bits[1])) & 1


class Sum:
    def __init__(self, keep, send, core):
        self.keep, self.core = keep, core
        self.index = lax.axis_index("replica") * 2 + lax.axis_index("shard")
        self.theirs = swap(send, "replica", 0)
        self.halvings = list(zip(*orders()))
        both = [tuple(b for b in o if b != SHARD_BIT) for o in orders()]
        self.gatherings = list(zip(*both))[::-1]
        self.last, self.done = None, False

    def wait(self, *others):
        self.keep = after(self.keep, *others)

    def step(self):
        if self.halvings:
            bits = self.halvings.pop(0)
            keep, theirs = self.keep, self.theirs
            half = keep.shape[0] // 2
            bit = my_bits(bits, self.core, self.index)
            take = lambda b: (
                lax.dynamic_slice_in_dim(keep, b * half, half, 0).astype(f32)
                + lax.dynamic_slice_in_dim(theirs, b * half, half, 0).astype(f32)
            ).astype(bf16)
            if keep.shape[0] >= 256:
                self.keep, send = fold(bit, keep, theirs)
            else:
                send = take(1 - bit)
                self.keep = take(bit)
            self.theirs = swap_by_core(send, bits)
            return send
        if self.last is None:
            total = (self.keep.astype(f32) + self.theirs.astype(f32)).astype(bf16)
        else:
            total = merge(self.keep, self.theirs, my_bits(self.last, self.core, self.index))
        self.keep = total
        if not self.gatherings:
            self.theirs, self.done = swap(total, "replica", 0), True
            return total
        self.last = self.gatherings.pop(0)
        self.theirs = swap_by_core(total, self.last)
        return total

def fold_kernel(bit_ref, mine_ref, theirs_ref, keep_ref, send_ref):
    rows = keep_ref.shape[0]
    for which, dst in ((bit_ref[0], keep_ref), (1 - bit_ref[0], send_ref)):
        at = pl.ds(pl.multiple_of(which * rows, 16), rows)
        dst[...] = (mine_ref[at, :].astype(f32) + theirs_ref[at, :].astype(f32)).astype(bf16)


def fold(bit, mine, theirs):
    half = (mine.shape[0] // 2, mine.shape[1])
    return call(
        fold_kernel, "fold", 1, bit.reshape(1), (mine, theirs), [whole(mine.shape)] * 2,
        [struct(half, bf16)] * 2, [whole(half)] * 2, [],
    )


def merge(mine, theirs, bit):
    pair = lambda a, b: jnp.concatenate([a, b], axis=0)
    return jnp.where(bit == 0, pair(mine, theirs), pair(theirs, mine))


def after(values, *others):
    return lax.optimization_barrier((values, *others))[0]


def call_columns(width):
    return [
        slice(j * width + groups[0] * LANES, j * width + (groups[-1] + 1) * LANES)
        for groups in CALLS
        for j in range(3)
    ]


def pack_columns(own_ref, qkv_ref, proj_ref):
    width = proj_ref.shape[1]
    at = 0
    for cols in call_columns(width):
        to = slice(at, at + cols.stop - cols.start)
        own_ref[:, to] = qkv_ref[:, cols].astype(bf16)
        at = to.stop
    own_ref[:, at:] = proj_ref[...].astype(bf16)


def pack_kernel(core_ref, qkv_ref, proj_ref, send_ref):
    pack_columns(send_ref, qkv_ref, proj_ref)


def pack(core, w_qkv, w_proj):
    rows, width = w_proj.shape
    mine = lambda a: pl.BlockSpec((rows // 2, a.shape[1]), lambda i, core: (core[0], 0))
    send = (rows // 2, 4 * width)
    return call(
        pack_kernel, "pack", 1, core.reshape(1), (w_qkv, w_proj), [mine(w_qkv), mine(w_proj)],
        struct(send, bf16), whole(send), [],
    )


def unpack_a_kernel(pos_ref, near_ref, far_ref, qkv_ref, proj_ref):
    width = proj_ref.shape[1]
    part = near_ref.shape[0]
    for which, src in ((pos_ref[2], near_ref), (1 - pos_ref[2], far_ref)):
        to = pl.ds(pl.multiple_of(which * part, 16), part)
        at = 0
        for cols in call_columns(width):
            end = at + cols.stop - cols.start
            qkv_ref[to, cols] = src[:, at:end].astype(f32)
            at = end
        proj_ref[to, :] = src[:, 3 * width : 4 * width].astype(f32)


def unpack_a(pos, near, far, w_qkv, w_proj):
    outs = [struct(w_qkv.shape, f32), struct(w_proj.shape, f32)]
    return call(
        unpack_a_kernel, "unpack_a", 1, pos, (near, far), [whole(near.shape)] * 2, outs,
        [whole(a.shape) for a in outs], [],
    )


def unpack_f_kernel(pos_ref, near_ref, far_ref, fc1_ref, fc2_ref):
    width = fc2_ref.shape[1]
    part = near_ref.shape[0] // 2
    for which, src in ((pos_ref[2], near_ref), (1 - pos_ref[2], far_ref)):
        to = pl.ds(pl.multiple_of(which * part, 16), part)
        for k in range(fc1_ref.shape[1] // width):
            for sh in range(2):
                at = k * width + sh * width // 2
                cols = sh * fc1_ref.shape[1] // 2 + k * width // 2
                fc1_ref[to, cols : cols + width // 2] = src[0:part, at : at + width // 2].astype(f32)
        for k in range(fc2_ref.shape[0] // (2 * part)):
            to = pl.ds(pl.multiple_of(k * 2 * part + which * part, 16), part)
            fc2_ref[to, :] = src[part:, k * width : (k + 1) * width].astype(f32)


def unpack_f(pos, near, far, w_fc1, w_fc2):
    outs = [struct(w_fc1.shape, f32), struct(w_fc2.shape, f32)]
    return call(
        unpack_f_kernel, "unpack_f", 1, pos, (near, far), [whole(near.shape)] * 2, outs,
        [whole(a.shape) for a in outs], [],
    )


def adam_step(weight, gradient, moment_one, moment_two, decay_here):
    moment_one_new = beta_first * moment_one + (1.0 - beta_first) * gradient
    moment_two_new = beta_second * moment_two + (1.0 - beta_second) * gradient * gradient
    first_hat = moment_one_new / (1.0 - beta_first**STEP)
    second_hat = moment_two_new / (1.0 - beta_second**STEP)
    weight_new = weight - learn_rate * (
        first_hat / (jnp.sqrt(second_hat) + adam_eps) + decay_here * weight
    )
    return (weight_new, moment_one_new, moment_two_new)


def on_device(
    tokens, cotangent, counts, w_qkv, w_proj, w_fc1, w_fc2, vectors,
    first_qkv, first_proj, first_fc1, first_fc2, first_vec,
    second_qkv, second_proj, second_fc1, second_fc2, second_vec,
):
    slots, width = tokens.shape[0], tokens.shape[3]
    by_token = lambda a: a.transpose(1, 2, 0, 3).reshape(TOK * slots, width)
    by_slot = lambda a: a.reshape(SIDE, SIDE, slots, width).transpose(2, 0, 1, 3)
    tokens, cotangent = by_token(tokens), by_token(cotangent)
    shard = lax.axis_index("shard")
    core = lax.axis_index("replica") & 1

    send_a = pack(core, w_qkv, w_proj)
    near_a = swap(send_a, "shard", 0)
    pos = jnp.stack([after(counts, send_a)[0], shard, core]).astype(jnp.int32)
    vec_low = vectors.astype(bf16)
    other_vec = swap(after(vec_low, send_a), "shard", 0)
    shuffle = shuffle_matrix()
    shuf = jnp.asarray(shuffle, bf16)
    back = jnp.asarray(shuffle.T, bf16)
    mask = jnp.asarray(mask_table())
    lanes = jnp.asarray(table_matrix(), bf16)
    place = jnp.asarray(place_matrix(), bf16)
    normed, low, own_a, own_1, own_2, send_f = enter(
        pos, after(tokens, send_a), shuf, w_qkv, w_proj, w_fc1, w_fc2
    )
    near_f = swap(send_f, "shard", 0)
    near_a = after(near_a, send_f)
    far_a = swap(near_a, "replica", 0)
    parts = (own_a, near_a, far_a)
    pair = jnp.concatenate
    vec = jnp.where(shard == 0, pair([vec_low, other_vec]), pair([other_vec, vec_low]))
    room = -vec.shape[0] % LANES + 3 * LANES
    vec = jnp.pad(vec.astype(f32), (0, room)).reshape(1, -1)

    calls = len(CALLS)
    *saved, o, att = attend(pos, normed, low, back, *parts, vec, mask, place)
    packed, prob = saved[:calls], saved[calls:]
    low, normed_b, dm, inv_b, sumc = norm(pos, tokens, att, cotangent, vec)
    far_f = swap(after(near_f, att), "replica", 0)
    act, dx1, keep_f, send_f, sumb, sumh = mlp(
        pos, low, dm, normed_b, inv_b, own_1, own_2, near_f, far_f, vec
    )
    near_w, far_w = near_f, far_f
    sum_f = Sum(keep_f, send_f, core)
    *do, grad_proj, suma = leave(pos, dx1, shuf, parts, o)
    dps, earlier = [], []
    for n in range(calls):
        sent_f = sum_f.step()
        dp, *rest = heads_back(
            pos, n, packed[n], prob[n], after(do[n], sent_f, *dps), normed, vec, lanes, parts,
            *((earlier, (grad_proj, suma, sumb, sumc, sumh)) if n == calls - 1 else ()),
        )
        dps.append(dp)
        earlier.append(rest)
    keep_a, send_a = rest
    sent_f = sum_f.step()
    sum_a = Sum(keep_a, after(send_a, sent_f), core)
    sent_a = sum_a.step()
    dh1 = project_back(pos, (after(dps[0], sent_f, sent_a), *dps[1:]), parts)

    def both(*others):
        sum_a.wait(*others)
        sent_a = sum_a.step()
        sum_f.wait(*others, sent_a)
        return sent_a, sum_f.step()

    grad_input = finish(pos, after(dh1, *both(dh1)), back, tokens, dx1, vec)
    sent = both(grad_input)
    out = close(pos, after(tokens, *sent), att, act, own_2, near_w, far_w, vec)
    sent = both(out)
    while not sum_f.done:
        sent = both(*sent)
    near_f, far_f = sum_f.keep, after(sum_f.theirs, *sent)
    grad_fc1, grad_fc2 = unpack_f(pos, near_f, far_f, w_fc1, w_fc2)
    sum_a.wait(grad_fc1)
    sent_a = sum_a.step()
    step_fc1 = adam_step(w_fc1, after(grad_fc1, sent_a), first_fc1, second_fc1, decay_rate)
    sum_a.wait(*step_fc1)
    sent_a = sum_a.step()
    step_fc2 = adam_step(w_fc2, after(grad_fc2, sent_a), first_fc2, second_fc2, decay_rate)
    sum_a.wait(*step_fc2)
    while not sum_a.done:
        sum_a.step()
    near_a, far_a = sum_a.keep, sum_a.theirs
    grad_vec = near_a[:, 4 * width :].astype(f32).reshape(-1)
    grad_vec = lax.dynamic_slice_in_dim(grad_vec, shard * vectors.shape[0], vectors.shape[0], 0)
    step_vec = adam_step(vectors, grad_vec, first_vec, second_vec, 0.0)
    grad_qkv, grad_proj = unpack_a(pos, near_a, far_a, w_qkv, w_proj)
    step_qkv = adam_step(w_qkv, grad_qkv, first_qkv, second_qkv, decay_rate)
    step_proj = adam_step(w_proj, grad_proj, first_proj, second_proj, decay_rate)
    steps = [
        (grad_qkv, *step_qkv),
        (grad_proj, *step_proj),
        (grad_fc1, *step_fc1),
        (grad_fc2, *step_fc2),
        (grad_vec, *step_vec),
    ]
    return (by_slot(out), by_slot(grad_input), *(s[k] for k in range(4) for s in steps))


def solution(mesh):
    tok = P(("replica", "shard"), None, None, None)
    mat, vec = P("shard", None), P("shard")
    group = (mat, mat, mat, mat, vec)
    return jax.shard_map(
        on_device,
        mesh=mesh,
        in_specs=(tok, tok, P(("replica", "shard"))) + group * 3,
        out_specs=(tok, tok) + group * 4,
        check_vma=False,
    )
```

```python
import functools

import jax
import jax.numpy as jnp
import numpy as np
from jax import lax
from jax.experimental import pallas as pl
from jax.experimental.pallas import tpu as pltpu
from jax.sharding import PartitionSpec as P

HEADS = 16
HEAD_DIM = 32
WIN = 7
SIDE = 14
SHIFT = 3
STEP = 3
RELS = 169
TOK = SIDE * SIDE
TOK_PAD = 208
WIN_ROWS = 4 * 64
LANES = 128
GROUPS = HEADS * HEAD_DIM // LANES
PER_STEP = 2


norm_eps = 1e-05
mask_fill = -100.0
learn_rate = 0.01
beta_first = 0.9
beta_second = 0.999
adam_eps = 1e-08
decay_rate = 0.05
log2_e = 1.4426950408889634
score_scale = HEAD_DIM ** (-0.5)

CALLS = ((0, 1), (2, 3))

COSTS_US = dict(
    pack=2, fold=1, enter=10, attend=18, norm=6, mlp=28, leave=5, heads_2=11, heads_1=6, project_back=5, finish=6, close=6, unpack_a=3,
    unpack_f=4,
)

VMEM_MIB = dict(
    pack=60, enter=60, attend=60, norm=60, mlp=60, leave=24, heads_2=32, heads_1=32, project_back=24,
    finish=32, close=32, unpack_a=16, unpack_f=20,
)

IN_VMEM = {"fold", "leave", "heads_2", "heads_1", "project_back", "finish", "close", "attend", "norm", "mlp"}
SCOPED_MIB = dict(
    pack=8, fold=8, enter=24, attend=24, norm=16, mlp=28, leave=16, heads_2=16, heads_1=16,
    project_back=12, finish=20, close=16, unpack_a=8, unpack_f=8,
)

f32 = jnp.float32
bf16 = jnp.bfloat16


def nn(a, b):
    return lax.dot_general(a, b, (((1,), (0,)), ((), ())), preferred_element_type=f32)


def nt(a, b):
    return lax.dot_general(a, b, (((1,), (1,)), ((), ())), preferred_element_type=f32)


def tn(a, b):
    return lax.dot_general(a, b, (((0,), (0,)), ((), ())), preferred_element_type=f32)


def window_places():
    win, row, col = np.meshgrid(np.arange(4), np.arange(WIN), np.arange(WIN), indexing="ij")
    rolled_r = (win // 2) * WIN + row
    rolled_c = (win % 2) * WIN + col
    src = ((rolled_r + SHIFT) % SIDE) * SIDE + (rolled_c + SHIFT) % SIDE
    dst = win * 64 + row * 8 + col
    return src.reshape(-1), dst.reshape(-1), rolled_r, rolled_c


def shuffle_matrix():
    src, dst, _, _ = window_places()
    out = np.zeros((WIN_ROWS, TOK_PAD), np.float32)
    out[dst, src] = 1.0
    return out


def mask_table():
    _, _, rolled_r, rolled_c = window_places()
    band = lambda r: (r >= SIDE - WIN).astype(np.int32) + (r >= SIDE - SHIFT).astype(np.int32)
    region = (3 * band(rolled_r) + band(rolled_c)).reshape(4, WIN * WIN)
    places = (np.arange(WIN)[:, None] * 8 + np.arange(WIN)[None, :]).reshape(-1)
    out = np.full((4, 64, 64), 0.0, np.float32)
    out[:, :, :] = -1e30
    out[:, :, places] = 0.0
    block = np.where(region[:, :, None] == region[:, None, :], 0.0, mask_fill * log2_e)
    out[np.arange(4)[:, None, None], places[None, :, None], places[None, None, :]] = block
    keys_first = out.transpose(0, 2, 1).reshape(2, LANES, 64)
    return np.tile(keys_first, (1, 1, 4)).astype(np.float32)


def place_matrix():
    row, col = np.meshgrid(np.arange(WIN), np.arange(WIN), indexing="ij")
    out = np.zeros((256, 64), np.float32)
    out[(2 * WIN - 1) * row + col, row * 8 + col] = 1.0
    return out


def table_matrix():
    row, col = np.meshgrid(np.arange(WIN), np.arange(WIN), indexing="ij")
    out = np.zeros((2, 64, 256), np.float32)
    reach = 2 * WIN - 1
    out[:, row * 8 + col, (WIN - 1) * (reach + 1) - reach * row - col] = 1.0
    return out.reshape(LANES, 256)


def stats(values):
    average = jnp.mean(values, axis=-1, keepdims=True)
    centred = values - average
    variance = jnp.mean(centred * centred, axis=-1, keepdims=True)
    inv_std = lax.rsqrt(variance + norm_eps)
    return centred * inv_std, inv_std


def norm_back(grad_out, normed, inv_std, gain_row):
    scaled = grad_out * gain_row
    first_mean = jnp.mean(scaled, axis=-1, keepdims=True)
    second_mean = jnp.mean(scaled * normed, axis=-1, keepdims=True)
    return inv_std * (scaled - first_mean - normed * second_mean)


def get_slot(sheet, slot, slots):
    rows = pl.ds(slot, TOK_PAD, stride=slots)
    return jnp.concatenate([sheet[g, rows, :] for g in range(GROUPS)], axis=1)


def put_slot(sheet, slot, slots, values):
    rows = pl.ds(slot, TOK_PAD, stride=slots)
    for g in range(GROUPS):
        sheet[g, rows, :] = values[:, g * LANES : (g + 1) * LANES]


def get_sheet(sheet, rows):
    return jnp.concatenate([sheet[g, 0:rows, :] for g in range(GROUPS)], axis=1)


def put_sheet(sheet, here, values):
    for g in range(GROUPS):
        sheet[g, here, :] = values[:, g * LANES : (g + 1) * LANES]


def pair_up(rows, diag):
    return jnp.concatenate([rows, rows], axis=1) * diag


def stack_heads(rows, head_masks):
    wide = jnp.concatenate([rows[0:64], rows[64:128]], axis=1)
    return jnp.concatenate([wide * m for m in head_masks], axis=0)


def merge_heads(stacked, lane_head):
    out = stacked[192:256]
    for h in (2, 1, 0):
        out = jnp.where(lane_head == h, stacked[64 * h : 64 * h + 64], out)
    return out


def over_keys(values):
    sums = [
        jnp.broadcast_to(jnp.sum(values[w : w + 64], axis=0, keepdims=True), (64, values.shape[1]))
        for w in (0, 64)
    ]
    return jnp.concatenate(sums, axis=0)


def block_masks():
    lane = lax.broadcasted_iota(jnp.int32, (1, 2 * LANES), 1)
    lane_head = (lane % LANES) // HEAD_DIM
    head_masks = [(lane_head == h).astype(f32).astype(bf16) for h in range(4)]
    row = lax.broadcasted_iota(jnp.int32, (LANES, 2 * LANES), 0)
    col = lax.broadcasted_iota(jnp.int32, (LANES, 2 * LANES), 1)
    diag = ((row // 64) == (col // LANES)).astype(f32).astype(bf16)
    lane_head64 = jnp.broadcast_to(lane_head, (64, 2 * LANES))
    return lane_head64, head_masks, diag


def join_rows(pos_ref, full, own_ref, near_ref, far_ref):
    half = own_ref.shape[0]
    shard, core = pos_ref[1], pos_ref[2]
    other = (1 - shard) * half
    part = half // 2
    full[pl.ds(pl.multiple_of(shard * half, 16), half), :] = own_ref[...]
    full[pl.ds(pl.multiple_of(other + core * part, 16), part), :] = near_ref[...]
    full[pl.ds(pl.multiple_of(other + (1 - core) * part, 16), part), :] = far_ref[...]


def vec_part(vec_ref, n, width):
    return vec_ref[0:1, n * width : (n + 1) * width]


def enter_kernel(
    pos_ref, tok_ref, shuf_ref, qkv_ref, proj_ref, fc1_ref, fc2_ref, part1_ref, part2_ref,
    high_ref, low_ref, own_ref, own1_ref, own2_ref, send_ref, sheet,
):
    step = this_step()
    rows, width = tok_ref.shape
    slots = rows // TOK

    @pl.when(step == 0)
    def _():
        normed, _ = stats(tok_ref[...].astype(f32))
        put_sheet(sheet, slice(0, rows), normed)
        sheet[:, rows:, :] = jnp.zeros((GROUPS, sheet.shape[1] - rows, LANES), f32)

    for i in range(PER_STEP):
        at = slice(i * WIN_ROWS, (i + 1) * WIN_ROWS)
        normed = get_slot(sheet, step * PER_STEP + i, slots)
        high = normed.astype(bf16)
        low = (normed - high.astype(f32)).astype(bf16)
        high_ref[at, :] = nn(shuf_ref[...], high).astype(bf16)
        low_ref[at, :] = nn(shuf_ref[...], low).astype(bf16)
    pack_columns(own_ref, qkv_ref, proj_ref)
    own1_ref[...] = fc1_ref[...].astype(bf16)
    own2_ref[...] = fc2_ref[...].astype(bf16)
    steps = send_ref.shape[1] // width
    part = part1_ref.shape[0]
    send_ref[pl.ds(pl.multiple_of(step * part, 16), part), :] = part1_ref[...].astype(bf16)
    for k in range(steps):
        @pl.when(step == k)
        def _():
            send_ref[steps * part :, k * width : (k + 1) * width] = part2_ref[...].astype(bf16)


def score_bias(vec_ref, mask_ref, place_ref, bias):
    width = GROUPS * LANES
    table_at = 12 * width
    reach = 2 * WIN - 1
    for g in range(GROUPS):
        blocks = []
        for h in range(4):
            at = table_at + (4 * g + h) * RELS
            shift = at % LANES
            entries = vec_ref[0:1, at - shift : at - shift + 3 * LANES]
            if shift:
                entries = pltpu.roll(entries, 3 * LANES - shift, 1)
            entries = jnp.broadcast_to(entries[:, 0:256], (8, 256))
            entries = pltpu.roll(entries, 0, 1, stride=1, stride_axis=0)
            for r in range(WIN):
                turn = 256 - (WIN - 1) * (reach + 1) + reach * r
                blocks.append(pltpu.roll(entries, turn, 1))
            blocks.append(jnp.zeros((8, 256), f32))
        spread = nn(jnp.concatenate(blocks, axis=0).astype(bf16), place_ref[...]) * log2_e
        rel = jnp.concatenate([spread[64 * h : 64 * h + 64] for h in range(4)], axis=1)
        for kind in range(2):
            for w in (0, 64):
                bias[kind * GROUPS + g, w : w + 64, :] = rel + mask_ref[kind, w : w + 64, :]


def attend_kernel(
    pos_ref, high_ref, low_ref, back_ref, own_ref, near_ref, far_ref, vec_ref, mask_ref, place_ref,
    *refs,
):
    packed_refs, prob_refs = refs[: len(CALLS)], refs[len(CALLS) : 2 * len(CALLS)]
    o_ref, att_ref, w_ref, sheet, bias_ref = refs[2 * len(CALLS) :]
    step = this_step()
    rows, width = att_ref.shape
    slots = rows // TOK

    @pl.when(step == 0)
    def _():
        join_rows(pos_ref, w_ref, own_ref, near_ref, far_ref)
        score_bias(vec_ref, mask_ref, place_ref, bias_ref)

    normed = high_ref[...].astype(f32) + low_ref[...].astype(f32)
    low = (normed * (1.0 + vec_part(vec_ref, 0, width)) + vec_part(vec_ref, 1, width)).astype(bf16)
    none = jnp.zeros((1, width), f32)
    biases = (vec_part(vec_ref, 2, width), none, vec_part(vec_ref, 3, width))
    at = 0
    for groups, packed_ref in zip(CALLS, packed_refs):
        cols = slice(at, at + packed_ref.shape[1])
        here = slice(groups[0] * LANES, (groups[-1] + 1) * LANES)
        added = jnp.concatenate([b[:, here] for b in biases], axis=1)
        packed_ref[...] = (nn(low, w_ref[:, cols]) + added).astype(bf16)
        at = cols.stop

    lane_head, head_masks, diag = block_masks()
    units = [(i, n, len(groups)) for i, groups in enumerate(CALLS) for n in range(len(groups))]
    for pair in range(2 * PER_STEP):
        pick = slice(pair * LANES, (pair + 1) * LANES)
        take = lambda u, j: packed_refs[u[0]][
            pick, (j * u[2] + u[1]) * LANES : (j * u[2] + u[1] + 1) * LANES
        ]
        q = [stack_heads(take(u, 0), head_masks) for u in units]
        k = [pair_up(take(u, 1), diag) for u in units]
        s = [nt(a, b) for a, b in zip(k, q)]
        e = [
            jnp.exp2(s[g] * (score_scale * log2_e) + bias_ref[(pair % 2) * GROUPS + g])
            for g in range(GROUPS)
        ]
        p = [(a * (1.0 / over_keys(a))).astype(bf16) for a in e]
        for g, (i, n, count) in enumerate(units):
            prob_refs[i][pair * count + n] = p[g]
        v = [pair_up(take(u, 2), diag) for u in units]
        for g in range(GROUPS):
            o = merge_heads(tn(p[g], v[g]), lane_head).astype(bf16)
            cols = slice(g * LANES, (g + 1) * LANES)
            o_ref[pair * LANES : pair * LANES + 64, cols] = o[:, 0:LANES]
            o_ref[pair * LANES + 64 : (pair + 1) * LANES, cols] = o[:, LANES:]

    branch = (nn(o_ref[...], w_ref[:, 3 * width :]) + vec_part(vec_ref, 4, width)).astype(bf16)
    for i in range(PER_STEP):
        att = nn(back_ref[...], branch[i * WIN_ROWS : (i + 1) * WIN_ROWS])
        put_slot(sheet, step * PER_STEP + i, slots, att)

    @pl.when(step == all_steps() - 1)
    def _():
        att_ref[...] = get_sheet(sheet, rows).astype(bf16)


def join_fc2(pos_ref, full, own_ref, near_ref, far_ref):
    half = own_ref.shape[0]
    shard, core = pos_ref[1], pos_ref[2]
    part = near_ref.shape[0] // 2
    width = full.shape[1]
    for k in range(half // (2 * part)):
        at = k * 4 * part + shard * 2 * part
        full[pl.ds(pl.multiple_of(at, 16), 2 * part), :] = own_ref[
            k * 2 * part : (k + 1) * 2 * part, :
        ]
        for which, src in ((core, near_ref), (1 - core, far_ref)):
            at = k * 4 * part + (1 - shard) * 2 * part + which * part
            full[pl.ds(pl.multiple_of(at, 16), part), :] = src[
                part:, k * width : (k + 1) * width
            ]


def block_place(core, shard, block):
    return jnp.where(core == 0, 2 * shard + block, 2 * block + shard)


def norm_kernel(
    pos_ref, tok_ref, att_ref, cot_ref, vec_ref, low_ref, norm_ref, dm_ref, inv_ref, sum_ref
):
    rows, width = tok_ref.shape
    slots = rows * all_steps() // TOK

    @pl.when(this_step() == 0)
    def _():
        sum_ref[...] = jnp.zeros_like(sum_ref)

    normed, inv_std = stats(tok_ref[...].astype(f32) + att_ref[...].astype(f32))
    gain, shift = vec_part(vec_ref, 5, width), vec_part(vec_ref, 6, width)
    low_ref[...] = (normed * (1.0 + gain) + shift).astype(bf16)
    norm_ref[...] = normed.astype(bf16)
    inv_ref[...] = jnp.broadcast_to(inv_std, inv_ref.shape)
    slot = lax.broadcasted_iota(jnp.int32, (rows, 1), 0) % slots
    dm = cot_ref[...].astype(f32) * (slot < pos_ref[0]).astype(f32)
    dm_ref[...] = dm.astype(bf16)
    sum_ref[0:1, :] += jnp.sum(dm, axis=0, keepdims=True)


def mlp_kernel(
    pos_ref, low_s, dm_s, norm_s, inv_s,
    own1a_ref, near1a_ref, far1a_ref, own1b_ref, near1b_ref, far1b_ref,
    own2_ref, near2_ref, far2_ref, vec_ref, b1a_ref, b1b_ref,
    act_ref, dx1_ref, keep_ref, send_ref, sum_ref, sumb_ref,
    w1_ref, w2_ref, dhid, dh_s,
):
    step = this_step()
    rows, width = low_s.shape
    core = pos_ref[2]
    part = width // 4
    @pl.when(step == 0)
    def _():
        sum_ref[...] = jnp.zeros_like(sum_ref)
        dh_s[...] = jnp.zeros_like(dh_s)

    join_rows(pos_ref, w1_ref.at[:, 0 : 2 * part], own1a_ref, near1a_ref, far1a_ref)
    join_rows(pos_ref, w1_ref.at[:, 2 * part :], own1b_ref, near1b_ref, far1b_ref)
    join_rows(pos_ref, w2_ref, own2_ref, near2_ref, far2_ref)
    b1 = jnp.concatenate([b1a_ref[0:1, :], b1b_ref[0:1, :]], axis=1)
    total = jnp.zeros((1, 4 * part), f32)
    pieces = 2
    for n in range(pieces):
        at = slice(n * rows // pieces, (n + 1) * rows // pieces)
        u = nn(low_s[at, :], w1_ref[...]) + b1
        bell = jnp.exp2(u * u * (-0.5 * log2_e))
        cdf = 0.5 + 0.5 * lax.erf(u * 0.7071067811865476)
        act_ref[at, :] = (u * cdf).astype(bf16)
        dg = nt(dm_s[at, :], w2_ref[...])
        du = (dg * (cdf + u * (bell * 0.3989422804014327))).astype(bf16)
        dhid[at, :] = du
        total += jnp.sum(du.astype(f32), axis=0, keepdims=True)
        dh_s[at, :] += nt(du, w1_ref[...])
    sumb_ref[0:1, :] = total
    grads = tn(low_s[...], dhid[...]), tn(act_ref[...], dm_s[...])
    for sh in range(2):
        for block, grad in enumerate(grads):
            first = grad[sh * 2 * part : sh * 2 * part + part]
            second = grad[sh * 2 * part + part : (sh + 1) * 2 * part]
            for which, dst in ((core, keep_ref), (1 - core, send_ref)):
                to = pl.ds(pl.multiple_of(block_place(which, sh, block) * part, 16), part)
                dst[to, :] = jnp.where(which == 0, first, second).astype(bf16)

    @pl.when(step == all_steps() - 1)
    def _():
        dh2, normed = dh_s[...], norm_s[...].astype(f32)
        inv_std = jnp.concatenate([inv_s[...]] * GROUPS, axis=1)
        grad = norm_back(dh2, normed, inv_std, 1.0 + vec_part(vec_ref, 5, width))
        dx1_ref[...] = (dm_s[...].astype(f32) + grad).astype(bf16)
        sum_ref[0:1, :] = jnp.sum(dh2 * normed, axis=0, keepdims=True)
        sum_ref[1:2, :] = jnp.sum(dh2, axis=0, keepdims=True)


def close_kernel(
    pos_ref, tok_ref, att_ref, act_ref, own_ref, near_ref, far_ref, vec_ref, out_ref, w_ref
):
    step = this_step()
    rows = tok_ref.shape[0]
    slots = rows * all_steps() // TOK

    @pl.when(step == 0)
    def _():
        join_fc2(pos_ref, w_ref, own_ref, near_ref, far_ref)

    slot = lax.broadcasted_iota(jnp.int32, (rows, 1), 0) % slots
    alive = (slot < pos_ref[0]).astype(f32)
    x1 = tok_ref[...].astype(f32) + att_ref[...].astype(f32)
    out = alive * (x1 + nn(act_ref[...], w_ref[...]) + vec_part(vec_ref, 7, out_ref.shape[1]))
    out_ref[...] = out.astype(bf16)


def fold_table(ds_ref, lanes_ref, flat, first_head):
    flat[...] = jnp.zeros_like(flat)
    for g in range(ds_ref.shape[0]):
        whole_g = ds_ref[g].T
        high = whole_g.astype(bf16)
        low = (whole_g - high.astype(f32)).astype(bf16)
        spread = nn(high, lanes_ref[...]) + nn(low, lanes_ref[...])
        for h in range(4):
            total = jnp.zeros((8, 256), f32)
            for r in range(WIN):
                at = 64 * h + 8 * r
                total += pltpu.roll(spread[at : at + 8], (2 * WIN - 1) * r, 1)
            total = pltpu.roll(total, 0, 1, stride=1, stride_axis=0)
            entries = jnp.sum(total, axis=0, keepdims=True)
            entries = jnp.concatenate([entries, jnp.zeros((1, LANES), f32)], axis=1)
            first, shift = divmod((first_head + 4 * g + h) * RELS, LANES)
            if shift:
                entries = pltpu.roll(entries, shift, 1)
            for k in range(3):
                flat[first + k : first + k + 1, :] += entries[:, k * LANES : (k + 1) * LANES]


def leave_kernel(
    pos_ref, dx1_ref, shuf_ref, own_ref, near_ref, far_ref, o_ref,
    *refs,
):
    do_refs = refs[: len(CALLS)]
    gp_ref, sum_ref, w_ref, sheet = refs[len(CALLS) :]
    step = this_step()
    rows, width = dx1_ref.shape
    slots = rows // TOK

    @pl.when(step == 0)
    def _():
        join_rows(pos_ref, w_ref, own_ref, near_ref, far_ref)
        put_sheet(sheet, slice(0, rows), dx1_ref[...].astype(f32))
        sheet[:, rows:, :] = jnp.zeros((GROUPS, sheet.shape[1] - rows, LANES), f32)
        gp_ref[...] = jnp.zeros_like(gp_ref)
        sum_ref[...] = jnp.zeros_like(sum_ref)

    da = []
    for i in range(PER_STEP):
        low = get_slot(sheet, step * PER_STEP + i, slots).astype(bf16)
        da.append(nn(shuf_ref[...], low))
    da = jnp.concatenate(da, axis=0)
    sum_ref[0:1, :] += jnp.sum(da, axis=0, keepdims=True)
    da = da.astype(bf16)
    do = nt(da, w_ref[...]).astype(bf16)
    for groups, do_ref in zip(CALLS, do_refs):
        do_ref[...] = do[:, groups[0] * LANES : (groups[-1] + 1) * LANES]
    gp_ref[...] += tn(o_ref[...], da)


def heads_kernel(*refs, groups, earlier_calls):
    (pos_ref, packed_ref, prob_ref, do_ref, normed_ref, vec_ref, lanes_ref,
     own_ref, near_ref, far_ref) = refs[:10]
    refs = refs[10:]
    last = earlier_calls > 0
    if last:
        g_refs, sum_refs, flat_refs = (
            refs[n * earlier_calls : (n + 1) * earlier_calls] for n in range(3)
        )
        (gp_ref, suma_ref, sumb_ref, sumc_ref, sumh_ref, dp_ref, keep_ref, send_ref,
         w_ref, acc, ds_ref, flat, sum_ref) = refs[3 * earlier_calls :]
    else:
        dp_ref, g_ref, sum_ref, flat, w_ref, acc, ds_ref = refs
    step = this_step()
    width, span = acc.shape
    third = span // 3

    @pl.when(step == 0)
    def _():
        join_rows(pos_ref, w_ref, own_ref, near_ref, far_ref)
        acc[...] = jnp.zeros_like(acc)
        ds_ref[...] = jnp.zeros_like(ds_ref)
        sum_ref[...] = jnp.zeros_like(sum_ref)

    lane_head, head_masks, diag = block_masks()
    for pair in range(2 * PER_STEP):
        pick = slice(pair * LANES, (pair + 1) * LANES)
        low_rows = slice(pair * LANES, pair * LANES + 64)
        high_rows = slice(pair * LANES + 64, (pair + 1) * LANES)
        every = range(len(groups))
        count = len(groups)
        at = [slice(g * LANES, (g + 1) * LANES) for g in range(3 * count)]
        do = [stack_heads(do_ref[pick, at[g]], head_masks) for g in every]
        v = [pair_up(packed_ref[pick, at[2 * count + g]], diag) for g in every]
        p = [prob_ref[pair * count + g] for g in every]
        dp = [nt(v[g], do[g]) for g in every]
        pf = [p[g].astype(f32) for g in every]
        delta = [over_keys(pf[g] * dp[g]) for g in every]
        dv = [nn(p[g], do[g]).astype(bf16) for g in every]
        ds = [pf[g] * (dp[g] - delta[g]) for g in every]
        for g in every:
            ds_ref[g] += ds[g]
        ds = [ds[g].astype(bf16) for g in every]
        k = [pair_up(packed_ref[pick, at[count + g]], diag) for g in every]
        q = [stack_heads(packed_ref[pick, at[g]], head_masks) for g in every]
        dk = [(nn(ds[g], q[g]) * score_scale).astype(bf16) for g in every]
        dq = [(merge_heads(tn(ds[g], k[g]), lane_head) * score_scale).astype(bf16) for g in every]
        for g in every:
            dp_ref[low_rows, at[g]] = dq[g][:, 0:LANES]
            dp_ref[high_rows, at[g]] = dq[g][:, LANES:]
            dp_ref[low_rows, at[count + g]] = dk[g][0:64, 0:LANES]
            dp_ref[high_rows, at[count + g]] = dk[g][64:, LANES:]
            dp_ref[low_rows, at[2 * count + g]] = dv[g][0:64, 0:LANES]
            dp_ref[high_rows, at[2 * count + g]] = dv[g][64:, LANES:]
    acc[...] += tn(normed_ref[...], dp_ref[...])
    sum_ref[0:1, 0:span] += jnp.sum(dp_ref[...].astype(f32), axis=0, keepdims=True)

    @pl.when(step == all_steps() - 1)
    def _():
        weights = w_ref[...]
        sums = sum_ref[0:1, 0:span]
        ones = jnp.ones((8, span), bf16)
        high = sums.astype(bf16)
        low = (sums - high.astype(f32)).astype(bf16)
        both = jnp.concatenate([high, low, jnp.zeros((6, span), bf16)], axis=0)
        shift_grad = jnp.sum(nt(both, weights), axis=0, keepdims=True)
        product = weights.astype(f32) * acc[...]
        high = product.astype(bf16)
        low = (product - high.astype(f32)).astype(bf16)
        gain_grad = (nt(ones, high) + nt(ones, low))[0:1]
        gain = (1.0 + vec_part(vec_ref, 0, width)).reshape(width, 1)
        shift = vec_part(vec_ref, 1, width).reshape(width, 1)
        grads = gain * acc[...] + shift * sums
        fold_table(ds_ref, lanes_ref, flat, 4 * groups[0])
        if not last:
            g_ref[...] = grads.astype(bf16)
            sum_ref[1:2, 0:width] = gain_grad
            sum_ref[2:3, 0:width] = shift_grad
            return
        acc[...] = grads
        core = pos_ref[2]
        part = width // 8
        per = width // LANES
        all_sums = [r[0:1, 0 : 3 * len(c) * LANES] for r, c in zip(sum_refs, CALLS)] + [sums]
        thirds = lambda n: jnp.concatenate(
            [a[:, n * a.shape[1] // 3 : (n + 1) * a.shape[1] // 3] for a in all_sums], axis=1
        )
        rows_of = [
            sum([r[1:2, 0:width] for r in sum_refs], gain_grad),
            sum([r[2:3, 0:width] for r in sum_refs], shift_grad),
            thirds(0),
            thirds(2),
            suma_ref[0:1, :],
        ]
        rows_of += [sumb_ref[0:1, :], sumb_ref[1:2, :], sumc_ref[0:1, :]]
        pieces = [v[:, k * LANES : (k + 1) * LANES] for v in rows_of for k in range(per)]
        mine = 2 * part
        blocks = sumh_ref.shape[1] // (4 * mine)
        for sh in range(2):
            for k in range(blocks):
                at = k * 4 * mine + sh * 2 * mine
                pieces += [sumh_ref[0:1, at : at + mine], sumh_ref[0:1, at + mine : at + 2 * mine]]
        block = jnp.concatenate(pieces + [sum([r[...] for r in flat_refs], flat[...])], axis=0)
        block = jnp.concatenate(
            [block, jnp.zeros((2 * part - block.shape[0], LANES), f32)], axis=0
        ).astype(bf16)
        for which, dst in ((core, keep_ref), (1 - core, send_ref)):
            for sh in range(2):
                for half in range(2):
                    src = sh * 4 * part + which * 2 * part + half * part
                    src = pl.ds(pl.multiple_of(src, 16), part)
                    to = pl.ds(pl.multiple_of(block_place(which, sh, half) * part, 16), part)
                    at = 0
                    for part_ref in (*g_refs, acc, gp_ref):
                        cols = slice(at, at + part_ref.shape[1])
                        dst[to, cols] = part_ref[src, :].astype(bf16)
                        at = cols.stop
                    dst[to, at:] = block[half * part : (half + 1) * part]


def project_back_kernel(pos_ref, *refs):
    dp_refs = refs[: len(CALLS)]
    own_ref, near_ref, far_ref, dh_ref, w_ref = refs[len(CALLS) :]

    @pl.when(this_step() == 0)
    def _():
        join_rows(pos_ref, w_ref, own_ref, near_ref, far_ref)

    dp = jnp.concatenate([r[...] for r in dp_refs], axis=1)
    dh_ref[...] = nt(dp, w_ref[...]).astype(bf16)


def finish_kernel(pos_ref, dh_ref, back_ref, tok_ref, dx1_ref, vec_ref, gi_ref, sheet):
    step = this_step()
    rows, width = tok_ref.shape
    slots = rows // TOK
    for i in range(PER_STEP):
        dh = nn(back_ref[...], dh_ref[i * WIN_ROWS : (i + 1) * WIN_ROWS, :])
        put_slot(sheet, step * PER_STEP + i, slots, dh)

    @pl.when(step == all_steps() - 1)
    def _():
        normed, inv_std = stats(tok_ref[...].astype(f32))
        grad = norm_back(get_sheet(sheet, rows), normed, inv_std, 1.0 + vec_part(vec_ref, 0, width))
        gi_ref[...] = (dx1_ref[...].astype(f32) + grad).astype(bf16)


def whole(shape):
    return pl.BlockSpec(shape, lambda i, *_: (0,) * len(shape))


def by_rows(rows, cols):
    return pl.BlockSpec((rows, cols), lambda i, *_: (i, 0))


def struct(shape, dtype):
    return jax.ShapeDtypeStruct(shape, dtype)


def params(name):
    return pltpu.CompilerParams(
        dimension_semantics=("arbitrary",), vmem_limit_bytes=VMEM_MIB[name] << 20
    )


LOOP = []


def this_step():
    return LOOP[-1][0] if LOOP else pl.program_id(0)


def all_steps():
    return LOOP[-1][1] if LOOP else pl.num_programs(0)


def block_of(ref, spec, step, pos_ref):
    if spec.block_shape is None or tuple(spec.block_shape) == tuple(ref.shape):
        return ref
    cuts = []
    for at, size, full in zip(spec.index_map(step, pos_ref), spec.block_shape, ref.shape):
        if size == full:
            cuts.append(slice(None))
        elif isinstance(at, int):
            cuts.append(slice(at * size, (at + 1) * size))
        else:
            cuts.append(pl.ds(pl.multiple_of(at * size, size), size))
    return ref.at[tuple(cuts)]


def call(kernel, name, steps, pos, ops, in_specs, outs, out_specs, scratch):
    cost = pl.CostEstimate(
        flops=COSTS_US[name] * 1_000_000_000, bytes_accessed=0, transcendentals=0
    )
    if name not in IN_VMEM:
        return pl.pallas_call(
            kernel,
            grid_spec=pltpu.PrefetchScalarGridSpec(
                num_scalar_prefetch=1,
                grid=(steps,),
                in_specs=in_specs,
                out_specs=out_specs,
                scratch_shapes=scratch,
            ),
            out_shape=outs,
            compiler_params=params(name),
            cost_estimate=cost,
            name=name,
        )(pos, *ops)

    several = isinstance(outs, (list, tuple))
    specs = [*in_specs, *(out_specs if several else [out_specs])]

    def loop(pos_ref, *refs):
        def one(step, carry):
            LOOP.append((step, steps))
            blocks = [block_of(r, s, step, pos_ref) for r, s in zip(refs, specs)]
            kernel(pos_ref, *blocks, *refs[len(specs) :])
            LOOP.pop()
            return carry

        if steps == 1:
            one(jnp.int32(0), 0)
        else:
            lax.fori_loop(0, steps, one, 0)

    here = pl.BlockSpec(memory_space=pltpu.VMEM)
    return pl.pallas_call(
        loop,
        in_specs=[pl.BlockSpec(memory_space=pltpu.SMEM)] + [here] * len(ops),
        out_specs=[here] * len(outs) if several else here,
        out_shape=outs,
        scratch_shapes=scratch,
        compiler_params=pltpu.CompilerParams(vmem_limit_bytes=SCOPED_MIB[name] << 20),
        cost_estimate=cost,
        name=name,
    )(pos, *ops)


def by_units(units):
    return pl.BlockSpec((units, LANES, 256), lambda i, *_: (i, 0, 0))


def columns(rows, cols, block):
    return pl.BlockSpec((rows, cols), lambda i, *_: (0, block))


def sheet_of(slots):
    return pltpu.VMEM((GROUPS, slots * TOK_PAD, LANES), f32)


def enter(pos, tokens, shuf, w_qkv, w_proj, w_fc1, w_fc2):
    rows, width = tokens.shape
    slots = rows // TOK
    steps = slots // PER_STEP
    wr = PER_STEP * WIN_ROWS
    hidden = w_fc1.shape[1]
    weights = (w_qkv, w_proj, w_fc1, w_fc2)
    blocks = [(a.shape[0] // steps, a.shape[1]) for a in weights]
    parts = [(w_fc1.shape[0] // 2 // steps, hidden), (w_fc2.shape[0] // 2 // steps, width)]
    win = struct((slots * WIN_ROWS, width), bf16)
    own, send = (w_qkv.shape[0], 4 * width), (width // 2, hidden)
    return call(
        enter_kernel, "enter", steps, pos, (tokens, shuf, *weights, w_fc1, w_fc2),
        [whole(tokens.shape), whole(shuf.shape)]
        + [by_rows(*block) for block in blocks]
        + [
            pl.BlockSpec(parts[0], lambda i, pos: (pos[2] * steps + i, 0)),
            pl.BlockSpec(parts[1], lambda i, pos: (2 * i + pos[2], 0)),
        ],
        [win, win]
        + [struct(a, bf16) for a in (own, w_fc1.shape, w_fc2.shape, send)],
        [by_rows(wr, width)] * 2
        + [by_rows(own[0] // steps, own[1]), by_rows(*blocks[2]), by_rows(*blocks[3]), whole(send)],
        [sheet_of(slots)],
    )


def attend(pos, high, low, *rest):
    rows, width = high.shape
    slots = rows // WIN_ROWS
    steps = slots // PER_STEP
    wr = PER_STEP * WIN_ROWS
    spans = [3 * len(groups) * LANES for groups in CALLS]
    units = [2 * PER_STEP * len(groups) for groups in CALLS]
    return call(
        attend_kernel, "attend", steps, pos, (high, low, *rest),
        [by_rows(wr, width)] * 2 + [whole(a.shape) for a in rest],
        [struct((rows, span), bf16) for span in spans]
        + [struct((steps * n, LANES, 256), bf16) for n in units]
        + [struct((rows, width), bf16), struct((slots * TOK, width), bf16)],
        [by_rows(wr, span) for span in spans]
        + [by_units(n) for n in units]
        + [by_rows(wr, width), whole((slots * TOK, width))],
        [
            pltpu.VMEM((width, 4 * width), bf16),
            sheet_of(slots),
            pltpu.VMEM((2 * GROUPS, LANES, 256), f32),
        ],
    )


def norm(pos, tokens, att, cot, vec):
    rows, width = cot.shape
    steps = 2
    part = rows // steps
    low = struct(cot.shape, bf16)
    return call(
        norm_kernel, "norm", steps, pos, (tokens, att, cot, vec),
        [by_rows(part, width)] * 3 + [whole(vec.shape)],
        [low, low, low, struct((rows, LANES), f32), struct((8, width), f32)],
        [by_rows(part, width)] * 3 + [by_rows(part, LANES), whole((8, width))], [],
    )


def mlp(pos, low, dm, normed, inv, own1, own2, near, far, vec):
    rows, width = low.shape
    hidden = own1.shape[1]
    half = width // 2
    steps = hidden // width
    part = width // 4
    at = lambda rows, cols, row, col: pl.BlockSpec((rows, cols), lambda i, *_: (row, col + i))
    by_columns = lambda rows, cols: pl.BlockSpec((rows, cols), lambda i, *_: (0, i))
    first_b1 = 8 * width // half
    return call(
        mlp_kernel, "mlp", steps, pos,
        (low, dm, normed, inv, own1, near, far, own1, near, far, own2, near, far, vec, vec, vec),
        [whole(low.shape)] * 2
        + [pl.BlockSpec(memory_space=pl.ANY)] * 2
        + [at(half, half, 0, 0), at(part, half, 0, 0), at(part, half, 0, 0)]
        + [at(half, half, 0, steps), at(part, half, 0, steps), at(part, half, 0, steps)]
        + [by_rows(half, width), at(part, width, 1, 0), at(part, width, 1, 0)]
        + [whole(vec.shape), at(1, half, 0, first_b1), at(1, half, 0, first_b1 + steps)],
        [
            struct((rows, hidden), bf16),
            struct(low.shape, bf16),
            struct((width, hidden), bf16),
            struct((width, hidden), bf16),
            struct((8, width), f32),
            struct((8, hidden), f32),
        ],
        [
            by_columns(rows, width),
            whole(low.shape),
            by_columns(width, width),
            by_columns(width, width),
            whole((8, width)),
            by_columns(8, width),
        ],
        [
            pltpu.VMEM((width, width), bf16),
            pltpu.VMEM((width, width), bf16),
            pltpu.VMEM((rows, width), bf16),
            pltpu.VMEM((rows, width), f32),
        ],
    )


def close(pos, tokens, att, act, own, near, far, vec):
    rows, width = tokens.shape
    hidden = act.shape[1]
    steps = 2
    part = rows // steps
    fixed = (own, near, far, vec)
    return call(
        close_kernel, "close", steps, pos, (tokens, att, act, *fixed),
        [by_rows(part, width)] * 2 + [by_rows(part, hidden)] + [whole(a.shape) for a in fixed],
        struct(tokens.shape, bf16), by_rows(part, width),
        [pltpu.VMEM((hidden, width), bf16)],
    )


def leave(pos, dx1, shuf, parts, o):
    rows, width = dx1.shape
    slots = rows // TOK
    wr = PER_STEP * WIN_ROWS
    cols = [len(groups) * LANES for groups in CALLS]
    return call(
        leave_kernel, "leave", slots // PER_STEP, pos, (dx1, shuf, *parts, o),
        [whole(dx1.shape), whole(shuf.shape)]
        + [columns(a.shape[0], width, 3) for a in parts]
        + [by_rows(wr, width)],
        [struct((slots * WIN_ROWS, c), bf16) for c in cols]
        + [struct((width, width), f32), struct((8, width), f32)],
        [by_rows(wr, c) for c in cols] + [whole((width, width)), whole((8, width))],
        [pltpu.VMEM((width, width), bf16), sheet_of(slots)],
    )


def heads_back(pos, which, packed, prob, do, normed, vec, lanes, parts, earlier=(), others=()):
    rows, span = packed.shape
    width = normed.shape[1]
    steps = rows // (PER_STEP * WIN_ROWS)
    wr = PER_STEP * WIN_ROWS
    units = prob.shape[0] // steps
    groups = CALLS[which]
    dp = struct((rows, span), bf16)
    scratch = [
        pltpu.VMEM((width, span), bf16),
        pltpu.VMEM((width, span), f32),
        pltpu.VMEM((len(groups), LANES, 256), f32),
    ]
    small, flat = (8, 3 * width), (24, LANES)
    if earlier:
        shape = (width // 2, 4 * width + LANES)
        outs, specs = [struct(shape, bf16)] * 2, [whole(shape)] * 2
        scratch += [pltpu.VMEM(flat, f32), pltpu.VMEM(small, f32)]
        earlier = [a[n] for n in range(3) for a in earlier]
    else:
        outs = [struct((width, span), bf16), struct(small, f32), struct(flat, f32)]
        specs = [whole(o.shape) for o in outs]
    extra = (*earlier, *others)
    at = 3 * groups[0] * LANES
    return call(
        functools.partial(heads_kernel, groups=groups, earlier_calls=len(earlier) // 3),
        "heads_%d" % len(groups), steps, pos,
        (packed, prob, do, normed, vec, lanes, *parts, *extra),
        [
            by_rows(wr, span), by_units(units), by_rows(wr, do.shape[1]), by_rows(wr, width),
            whole(vec.shape), whole(lanes.shape),
        ]
        + [columns(a.shape[0], span, at // span) for a in parts]
        + [whole(a.shape) for a in extra],
        [dp, *outs], [by_rows(wr, span), *specs], scratch,
    )


def project_back(pos, dps, parts):
    rows = dps[0].shape[0]
    width = parts[0].shape[1] // 4
    wr = PER_STEP * WIN_ROWS
    return call(
        project_back_kernel, "project_back", rows // wr, pos, (*dps, *parts),
        [by_rows(wr, a.shape[1]) for a in dps]
        + [columns(a.shape[0], 3 * width, 0) for a in parts],
        struct((rows, width), bf16), by_rows(wr, width),
        [pltpu.VMEM((width, 3 * width), bf16)],
    )


def finish(pos, dh, back, tokens, dx1, vec):
    rows, width = tokens.shape
    slots = rows // TOK
    wr = PER_STEP * WIN_ROWS
    fixed = (back, tokens, dx1, vec)
    return call(
        finish_kernel, "finish", slots // PER_STEP, pos, (dh, *fixed),
        [by_rows(wr, width)] + [whole(a.shape) for a in fixed],
        struct(tokens.shape, bf16), whole(tokens.shape), [sheet_of(slots)],
    )


def swap(values, axis, bit):
    count = lax.axis_size(axis)
    return lax.ppermute(values, axis, [(i, i ^ (1 << bit)) for i in range(count)])


SHARD_BIT = 0


def orders():
    top = (lax.axis_size("replica") * lax.axis_size("shard")).bit_length() - 1
    rest = tuple(range(4, top))
    return (SHARD_BIT, 2, 3, *rest), (3, SHARD_BIT, 2, *rest)


def swap_by_core(values, bits):
    count = lax.axis_size("replica") * lax.axis_size("shard")
    perm = [(i, i ^ (1 << bits[(i >> 1) & 1])) for i in range(count)]
    return lax.ppermute(values, ("replica", "shard"), perm)


def my_bits(bits, core, index):
    return (index >> jnp.where(core == 0, bits[0], bits[1])) & 1


class Sum:
    def __init__(self, keep, send, core):
        self.keep, self.core = keep, core
        self.index = lax.axis_index("replica") * 2 + lax.axis_index("shard")
        self.theirs = swap(send, "replica", 0)
        self.halvings = list(zip(*orders()))
        both = [tuple(b for b in o if b != SHARD_BIT) for o in orders()]
        self.gatherings = list(zip(*both))[::-1]
        self.last, self.done = None, False

    def wait(self, *others):
        self.keep = after(self.keep, *others)

    def step(self):
        if self.halvings:
            bits = self.halvings.pop(0)
            keep, theirs = self.keep, self.theirs
            half = keep.shape[0] // 2
            bit = my_bits(bits, self.core, self.index)
            take = lambda b: (
                lax.dynamic_slice_in_dim(keep, b * half, half, 0).astype(f32)
                + lax.dynamic_slice_in_dim(theirs, b * half, half, 0).astype(f32)
            ).astype(bf16)
            if keep.shape[0] >= 256:
                self.keep, send = fold(bit, keep, theirs)
            else:
                send = take(1 - bit)
                self.keep = take(bit)
            self.theirs = swap_by_core(send, bits)
            return send
        if self.last is None:
            total = (self.keep.astype(f32) + self.theirs.astype(f32)).astype(bf16)
        else:
            total = merge(self.keep, self.theirs, my_bits(self.last, self.core, self.index))
        self.keep = total
        if not self.gatherings:
            self.theirs, self.done = swap(total, "replica", 0), True
            return total
        self.last = self.gatherings.pop(0)
        self.theirs = swap_by_core(total, self.last)
        return total

def fold_kernel(bit_ref, mine_ref, theirs_ref, keep_ref, send_ref):
    rows = keep_ref.shape[0]
    for which, dst in ((bit_ref[0], keep_ref), (1 - bit_ref[0], send_ref)):
        at = pl.ds(pl.multiple_of(which * rows, 16), rows)
        dst[...] = (mine_ref[at, :].astype(f32) + theirs_ref[at, :].astype(f32)).astype(bf16)


def fold(bit, mine, theirs):
    half = (mine.shape[0] // 2, mine.shape[1])
    return call(
        fold_kernel, "fold", 1, bit.reshape(1), (mine, theirs), [whole(mine.shape)] * 2,
        [struct(half, bf16)] * 2, [whole(half)] * 2, [],
    )


def merge(mine, theirs, bit):
    pair = lambda a, b: jnp.concatenate([a, b], axis=0)
    return jnp.where(bit == 0, pair(mine, theirs), pair(theirs, mine))


def after(values, *others):
    return lax.optimization_barrier((values, *others))[0]


def call_columns(width):
    return [
        slice(j * width + groups[0] * LANES, j * width + (groups[-1] + 1) * LANES)
        for groups in CALLS
        for j in range(3)
    ]


def pack_columns(own_ref, qkv_ref, proj_ref):
    width = proj_ref.shape[1]
    at = 0
    for cols in call_columns(width):
        to = slice(at, at + cols.stop - cols.start)
        own_ref[:, to] = qkv_ref[:, cols].astype(bf16)
        at = to.stop
    own_ref[:, at:] = proj_ref[...].astype(bf16)


def pack_kernel(core_ref, qkv_ref, proj_ref, send_ref):
    pack_columns(send_ref, qkv_ref, proj_ref)


def pack(core, w_qkv, w_proj):
    rows, width = w_proj.shape
    mine = lambda a: pl.BlockSpec((rows // 2, a.shape[1]), lambda i, core: (core[0], 0))
    send = (rows // 2, 4 * width)
    return call(
        pack_kernel, "pack", 1, core.reshape(1), (w_qkv, w_proj), [mine(w_qkv), mine(w_proj)],
        struct(send, bf16), whole(send), [],
    )


def unpack_a_kernel(pos_ref, near_ref, far_ref, qkv_ref, proj_ref):
    width = proj_ref.shape[1]
    part = near_ref.shape[0]
    for which, src in ((pos_ref[2], near_ref), (1 - pos_ref[2], far_ref)):
        to = pl.ds(pl.multiple_of(which * part, 16), part)
        at = 0
        for cols in call_columns(width):
            end = at + cols.stop - cols.start
            qkv_ref[to, cols] = src[:, at:end].astype(f32)
            at = end
        proj_ref[to, :] = src[:, 3 * width : 4 * width].astype(f32)


def unpack_a(pos, near, far, w_qkv, w_proj):
    outs = [struct(w_qkv.shape, f32), struct(w_proj.shape, f32)]
    return call(
        unpack_a_kernel, "unpack_a", 1, pos, (near, far), [whole(near.shape)] * 2, outs,
        [whole(a.shape) for a in outs], [],
    )


def unpack_f_kernel(pos_ref, near_ref, far_ref, fc1_ref, fc2_ref):
    width = fc2_ref.shape[1]
    part = near_ref.shape[0] // 2
    for which, src in ((pos_ref[2], near_ref), (1 - pos_ref[2], far_ref)):
        to = pl.ds(pl.multiple_of(which * part, 16), part)
        for k in range(fc1_ref.shape[1] // width):
            for sh in range(2):
                at = k * width + sh * width // 2
                cols = sh * fc1_ref.shape[1] // 2 + k * width // 2
                fc1_ref[to, cols : cols + width // 2] = src[0:part, at : at + width // 2].astype(f32)
        for k in range(fc2_ref.shape[0] // (2 * part)):
            to = pl.ds(pl.multiple_of(k * 2 * part + which * part, 16), part)
            fc2_ref[to, :] = src[part:, k * width : (k + 1) * width].astype(f32)


def unpack_f(pos, near, far, w_fc1, w_fc2):
    outs = [struct(w_fc1.shape, f32), struct(w_fc2.shape, f32)]
    return call(
        unpack_f_kernel, "unpack_f", 1, pos, (near, far), [whole(near.shape)] * 2, outs,
        [whole(a.shape) for a in outs], [],
    )


def adam_step(weight, gradient, moment_one, moment_two, decay_here):
    moment_one_new = beta_first * moment_one + (1.0 - beta_first) * gradient
    moment_two_new = beta_second * moment_two + (1.0 - beta_second) * gradient * gradient
    first_hat = moment_one_new / (1.0 - beta_first**STEP)
    second_hat = moment_two_new / (1.0 - beta_second**STEP)
    weight_new = weight - learn_rate * (
        first_hat / (jnp.sqrt(second_hat) + adam_eps) + decay_here * weight
    )
    return (weight_new, moment_one_new, moment_two_new)


def on_device(
    tokens, cotangent, counts, w_qkv, w_proj, w_fc1, w_fc2, vectors,
    first_qkv, first_proj, first_fc1, first_fc2, first_vec,
    second_qkv, second_proj, second_fc1, second_fc2, second_vec,
):
    slots, width = tokens.shape[0], tokens.shape[3]
    by_token = lambda a: a.transpose(1, 2, 0, 3).reshape(TOK * slots, width)
    by_slot = lambda a: a.reshape(SIDE, SIDE, slots, width).transpose(2, 0, 1, 3)
    tokens, cotangent = by_token(tokens), by_token(cotangent)
    shard = lax.axis_index("shard")
    core = lax.axis_index("replica") & 1

    send_a = pack(core, w_qkv, w_proj)
    near_a = swap(send_a, "shard", 0)
    pos = jnp.stack([after(counts, send_a)[0], shard, core]).astype(jnp.int32)
    vec_low = vectors.astype(bf16)
    other_vec = swap(after(vec_low, send_a), "shard", 0)
    shuffle = shuffle_matrix()
    shuf = jnp.asarray(shuffle, bf16)
    back = jnp.asarray(shuffle.T, bf16)
    mask = jnp.asarray(mask_table())
    lanes = jnp.asarray(table_matrix(), bf16)
    place = jnp.asarray(place_matrix(), bf16)
    normed, low, own_a, own_1, own_2, send_f = enter(
        pos, after(tokens, send_a), shuf, w_qkv, w_proj, w_fc1, w_fc2
    )
    near_f = swap(send_f, "shard", 0)
    near_a = after(near_a, send_f)
    far_a = swap(near_a, "replica", 0)
    parts = (own_a, near_a, far_a)
    pair = jnp.concatenate
    vec = jnp.where(shard == 0, pair([vec_low, other_vec]), pair([other_vec, vec_low]))
    room = -vec.shape[0] % LANES + 3 * LANES
    vec = jnp.pad(vec.astype(f32), (0, room)).reshape(1, -1)

    calls = len(CALLS)
    *saved, o, att = attend(pos, normed, low, back, *parts, vec, mask, place)
    packed, prob = saved[:calls], saved[calls:]
    low, normed_b, dm, inv_b, sumc = norm(pos, tokens, att, cotangent, vec)
    far_f = swap(after(near_f, att), "replica", 0)
    act, dx1, keep_f, send_f, sumb, sumh = mlp(
        pos, low, dm, normed_b, inv_b, own_1, own_2, near_f, far_f, vec
    )
    near_w, far_w = near_f, far_f
    sum_f = Sum(keep_f, send_f, core)
    *do, grad_proj, suma = leave(pos, dx1, shuf, parts, o)
    dps, earlier = [], []
    for n in range(calls):
        sent_f = sum_f.step()
        dp, *rest = heads_back(
            pos, n, packed[n], prob[n], after(do[n], sent_f, *dps), normed, vec, lanes, parts,
            *((earlier, (grad_proj, suma, sumb, sumc, sumh)) if n == calls - 1 else ()),
        )
        dps.append(dp)
        earlier.append(rest)
    keep_a, send_a = rest
    sent_f = sum_f.step()
    sum_a = Sum(keep_a, after(send_a, sent_f), core)
    sent_a = sum_a.step()
    def both(*others):
        sum_a.wait(*others)
        sent_a = sum_a.step()
        sum_f.wait(*others, sent_a)
        return sent_a, sum_f.step()

    out = close(pos, after(tokens, sent_f, sent_a), att, act, own_2, near_w, far_w, vec)
    dh1 = project_back(pos, (after(dps[0], *both(out)), *dps[1:]), parts)
    grad_input = finish(pos, after(dh1, *both(dh1)), back, tokens, dx1, vec)
    sent = both(grad_input)
    while not sum_f.done:
        sent = both(*sent)
    near_f, far_f = sum_f.keep, after(sum_f.theirs, *sent)
    grad_fc1, grad_fc2 = unpack_f(pos, near_f, far_f, w_fc1, w_fc2)
    sum_a.wait(grad_fc1)
    sent_a = sum_a.step()
    step_fc1 = adam_step(w_fc1, after(grad_fc1, sent_a), first_fc1, second_fc1, decay_rate)
    sum_a.wait(*step_fc1)
    sent_a = sum_a.step()
    step_fc2 = adam_step(w_fc2, after(grad_fc2, sent_a), first_fc2, second_fc2, decay_rate)
    sum_a.wait(*step_fc2)
    while not sum_a.done:
        sum_a.step()
    near_a, far_a = sum_a.keep, sum_a.theirs
    grad_vec = near_a[:, 4 * width :].astype(f32).reshape(-1)
    grad_vec = lax.dynamic_slice_in_dim(grad_vec, shard * vectors.shape[0], vectors.shape[0], 0)
    step_vec = adam_step(vectors, grad_vec, first_vec, second_vec, 0.0)
    grad_qkv, grad_proj = unpack_a(pos, near_a, far_a, w_qkv, w_proj)
    step_qkv = adam_step(w_qkv, grad_qkv, first_qkv, second_qkv, decay_rate)
    step_proj = adam_step(w_proj, grad_proj, first_proj, second_proj, decay_rate)
    steps = [
        (grad_qkv, *step_qkv),
        (grad_proj, *step_proj),
        (grad_fc1, *step_fc1),
        (grad_fc2, *step_fc2),
        (grad_vec, *step_vec),
    ]
    return (by_slot(out), by_slot(grad_input), *(s[k] for k in range(4) for s in steps))


def solution(mesh):
    tok = P(("replica", "shard"), None, None, None)
    mat, vec = P("shard", None), P("shard")
    group = (mat, mat, mat, mat, vec)
    return jax.shard_map(
        on_device,
        mesh=mesh,
        in_specs=(tok, tok, P(("replica", "shard"))) + group * 3,
        out_specs=(tok, tok) + group * 4,
        check_vma=False,
    )
```
